32 devices in a mesh: grp: 2 (over x), orb: 16 (over z, y, core).
Axes of the slice: x: 2, y: 2, z: 4, core: 2. Of those that a mesh axis runs over, the one named last changes fastest.
Arguments:
- three_centre: bfloat16 [16, 64, 16, 4096], P('orb'), may hold values from -0.59765625 to 0.59765625
- green_occ: bfloat16 [32, 4096], P(('grp', 'orb')), parts along dimension 0, may hold values from -0.75 to 0.75
- green_virt: bfloat16 [32, 4096], P(('grp', 'orb')), parts along dimension 0, may hold values from -0.75 to 0.75
- pair_atoms: int32 [16, 2], P('orb'), may hold values from 0 to 15
- basis_count: int32 [16], P('orb'), may hold values from 32 to 64
- chi_target: int32 [16, 256], P('orb'), may hold values from 0 to 63, as said below
Outputs:
- chi_blocks: float32 [128, 4096], P(('grp', 'orb')), parts along dimension 0
The draws below stay inside these ranges and needn't reach their ends.
There are 2 independent parts, one for each index of `grp`. The reference program is written for one: setup_inputs(seed, part) draws one part's arguments, and reference() takes and returns one part's arrays. A program takes and returns all parts, laid end to end along the dimension named above; an argument that names none is the same for every part. Nothing has to cross between parts.
Inputs may be any that keep to these rules, and one draw needn't show every extreme that they name: `chi_target`: block c belongs to device c // 4. Of the 256 entries of one device, at most 32 name blocks of any one device; one device receives exactly 32 from every device.
All inputs are finite; a program needn't handle non-finite values.
Results may differ from the reference program's by a relative error of at most 0.0041.
Values may be sent and summed in bfloat16 or wider, within the bound.
No kernel may reach another device: no remote copies, remote signals or barrier semaphores. Data moves between devices by JAX's collectives and lax.ppermute only.
A program may use at most 128 MiB of HBM per device.

```python
import jax
import jax.numpy as jnp
from jax import lax

BS = 64
NP = 16
PAIR_DEV = 1
CB_DEV = 4
NPAIR = 16
NATOM = 16
NCB = 64
CAP = 32


def draw_chi_target(key, part):
    key = jax.random.fold_in(key, 7)
    device_total = NPAIR // PAIR_DEV
    per_device = PAIR_DEV * NP * NP
    key_hot, key_devices = jax.random.split(key, 2)
    hottest = jax.random.randint(key_hot, (), 0, device_total)

    def one_device(device_key):
        key_order, key_others, key_within = jax.random.split(device_key, 3)
        virtual_slot = jax.random.permutation(key_order, per_device)
        others = jax.random.permutation(key_others, device_total - 1) + 1
        offsets = jnp.concatenate([jnp.zeros((1,), jnp.int32), others.astype(jnp.int32)])
        owner = (hottest + offsets[virtual_slot // CAP]) % device_total
        within = jax.random.randint(key_within, (per_device,), 0, CB_DEV)
        return (owner * CB_DEV + within).astype(jnp.int32)
    device_keys = jax.random.split(key_devices, device_total)
    targets = jax.vmap(one_device)(device_keys)
    return targets.reshape(NPAIR, NP * NP)


def place_ends(drawn, rng, least, high):
    longest = drawn.shape.index(max(drawn.shape))
    spots = []
    for shift in (0, 1):
        where = [jax.random.randint(jax.random.fold_in(rng, axis), (), 0, length) for axis, length in enumerate(drawn.shape)]
        where[longest] = (where[longest] + shift) % drawn.shape[longest]
        spots.append(tuple(where))
    return drawn.at[spots[0]].set(least).at[spots[1]].set(high)


def level_of(stream_key, shape, cuts, least, top_value):
    level = 1.0
    for axis_at, blocks in cuts:
        heights = jax.random.uniform(jax.random.fold_in(jax.random.fold_in(stream_key, 6), axis_at), (blocks,), jnp.float32, least / len(cuts), top_value / len(cuts))
        level = level * jnp.repeat(jnp.exp(heights), shape[axis_at] // blocks).reshape((-1,) + (1,) * (len(shape) - 1 - axis_at))
    return level


def normal_values(own_key, shape, scale, limit, shards=(), held_as=jnp.bfloat16):
    gain = level_of(own_key, shape, shards, -0.22, 0.18) if shards else 1.0
    values = jax.random.normal(own_key, shape, jnp.float32) * scale * gain
    return jnp.minimum(jnp.maximum(values, -limit), limit).astype(held_as)


def setup_inputs(seed: int = 0, part: int = 0) -> dict:
    key_of = jax.random.split(jax.random.key(seed), 7)
    own_keys = jax.random.split(jax.random.fold_in(key_of[6], part), 7)
    three_centre = normal_values(key_of[0], (NPAIR, BS, NP, BS * BS), 0.1, 0.59765625, ((0, 16),))
    green_occ = normal_values(own_keys[1], (NATOM, BS * BS), BS ** -0.5, 0.75, ((0, 16),))
    green_virt = normal_values(own_keys[2], (NATOM, BS * BS), BS ** -0.5, 0.75, ((0, 16),))
    pair_atoms = place_ends(jax.random.randint(key_of[3], (NPAIR, 2), 0, NATOM), jax.random.fold_in(key_of[3], 1), 0, NATOM - 1).astype(jnp.int32)
    basis_count = place_ends(jax.random.randint(key_of[4], (NATOM,), BS // 2, BS + 1), jax.random.fold_in(key_of[4], 1), BS // 2, BS).astype(jnp.int32)
    chi_target = draw_chi_target(jax.random.fold_in(key_of[6], 71), part)
    return dict(three_centre=three_centre, green_occ=green_occ, green_virt=green_virt, pair_atoms=pair_atoms, basis_count=basis_count, chi_target=chi_target)


def reference(three_centre, green_occ, green_virt, pair_atoms, basis_count, chi_target):
    lane_ids = jnp.arange(BS, dtype=jnp.int32)
    present = lane_ids[None, :] < basis_count[:, None]
    valid_entries = (present[:, :, None] & present[:, None, :]).reshape(NATOM, BS * BS)
    zero_value = jnp.zeros((), green_occ.dtype)
    occ_masked = jnp.where(valid_entries, green_occ, zero_value)
    virt_masked = jnp.where(valid_entries, green_virt, zero_value)

    def add_pair(chi_state, inputs):
        integrals, pair_ids, targets = inputs
        occ_block = occ_masked[pair_ids[0]].reshape(BS, BS)
        virt_block = virt_masked[pair_ids[1]].reshape(BS, BS)
        occ_side = jnp.dot(occ_block, integrals.reshape(BS, NP * BS * BS), preferred_element_type=jnp.float32)
        occ_side = lax.optimization_barrier(occ_side.astype(jnp.bfloat16)).astype(jnp.float32)
        virt_side = jnp.dot(integrals.reshape(BS * NP * BS, BS), virt_block, preferred_element_type=jnp.float32)
        virt_side = lax.optimization_barrier(virt_side.astype(jnp.bfloat16)).astype(jnp.float32)
        pair_chi = jnp.einsum("mps,mqs->pq", occ_side.reshape(BS, NP * BS, BS), virt_side.reshape(BS, NP * BS, BS))
        contribution = pair_chi.reshape(NP, BS, NP, BS).transpose(0, 2, 1, 3).reshape(NP * NP, BS * BS)
        return chi_state.at[targets].add(contribution), None

    start_value = jnp.zeros((NCB, BS * BS), jnp.float32)
    chi_blocks, _ = lax.scan(add_pair, start_value, (three_centre, pair_atoms, chi_target))
    return chi_blocks
```

```python
import functools

import jax
import jax.numpy as jnp
from jax import lax
from jax.experimental import pallas as pl
from jax.experimental.pallas import tpu as pltpu
from jax.sharding import PartitionSpec as P

CB_DEV = 4
LAM = 4
PARTS = 4


def relayout_kernel(b_ref, d_ref, e_ref):
    lam, aux, width = b_ref.shape
    bs = d_ref.shape[0] // aux
    rows = aux * aux
    row = lax.broadcasted_iota(jnp.int32, (rows, rows), 0)
    col = lax.broadcasted_iota(jnp.int32, (rows, rows), 1)
    perm = (col == (row % aux) * aux + row // aux).astype(jnp.bfloat16)
    half = aux // 2
    for h in range(2):
        part = b_ref[...].astype(jnp.float32)[:, h * half:(h + 1) * half, :]
        e_ref[h] = part.reshape(lam * half, width).astype(jnp.bfloat16)
    for blk in range(bs // aux):
        pieces = []
        for p in range(aux):
            at = (blk * aux + p) * bs
            pieces.append(jnp.concatenate([b_ref[i, :, at:at + bs] for i in range(lam)], axis=-1))
        stacked = jnp.concatenate(pieces, axis=0)
        moved = jnp.dot(perm, stacked, preferred_element_type=jnp.float32).astype(jnp.bfloat16)
        for a in range(aux):
            d_ref[a * bs + blk * aux:a * bs + (blk + 1) * aux, :] = moved[a * aux:(a + 1) * aux]


def relayout(integrals, part):
    bs, aux, width = integrals.shape
    steps = bs // LAM // PARTS
    lams = bs // PARTS
    return pl.pallas_call(
        relayout_kernel,
        grid=(steps,),
        in_specs=[pl.BlockSpec((LAM, aux, width), lambda i: (part * steps + i, 0, 0))],
        out_specs=[
            pl.BlockSpec((aux * bs, LAM * bs), lambda i: (0, i)),
            pl.BlockSpec((2, LAM * aux // 2, width), lambda i: (0, i, 0)),
        ],
        out_shape=[
            jax.ShapeDtypeStruct((aux * bs, lams * bs), jnp.bfloat16),
            jax.ShapeDtypeStruct((2, lams * aux // 2, width), jnp.bfloat16),
        ],
        compiler_params=pltpu.CompilerParams(vmem_limit_bytes=32 << 20),
        cost_estimate=pl.CostEstimate(
            flops=2 * bs * aux * width * 256 // PARTS,
            bytes_accessed=6 * bs * aux * width // PARTS,
            transcendentals=0,
        ),
    )(integrals)


def chi_kernel(bs, aux, ids_ref, tgt_ref, table_ref, *refs):
    d_parts, e_parts = refs[:PARTS], refs[PARTS:2 * PARTS]
    keep_ref, send_ref = refs[2 * PARTS:2 * PARTS + 2]
    dbuf, ebuf, obuf, outb, acc, d_sem, e_sem = refs[2 * PARTS + 2:]
    half = aux // 2
    width = bs * bs
    d_w = width // PARTS
    e_w = bs * half // PARTS

    def d_copy(i):
        return pltpu.make_async_copy(d_parts[i], dbuf.at[:, pl.ds(i * d_w, d_w)], d_sem.at[i])

    def e_copy(i):
        return pltpu.make_async_copy(e_parts[i], ebuf.at[:, pl.ds(i * e_w, e_w), :], e_sem.at[i])

    for i in range(PARTS):
        d_copy(i).start()
    for i in range(PARTS):
        e_copy(i).start()

    occ = table_ref[ids_ref[0]][:, :bs]
    virt = table_ref[ids_ref[1]][:, bs:]

    wide = LAM * bs
    rep = (
        lax.broadcasted_iota(jnp.int32, (wide, bs), 0) % bs == lax.broadcasted_iota(jnp.int32, (wide, bs), 1)
    ).astype(jnp.bfloat16)
    spread = jnp.dot(rep, virt, preferred_element_type=jnp.float32).astype(jnp.bfloat16)
    spread = jnp.concatenate([spread] * LAM, axis=1)
    same = (
        lax.broadcasted_iota(jnp.int32, (wide, wide), 0) // bs == lax.broadcasted_iota(jnp.int32, (wide, wide), 1) // bs
    )
    virt_w = jnp.where(same, spread, jnp.zeros((), jnp.bfloat16))

    tall = bs * half
    rep_o = (
        lax.broadcasted_iota(jnp.int32, (tall, bs), 0) // half == lax.broadcasted_iota(jnp.int32, (tall, bs), 1)
    ).astype(jnp.bfloat16)
    rep_t = (
        lax.broadcasted_iota(jnp.int32, (bs, tall), 1) // half == lax.broadcasted_iota(jnp.int32, (bs, tall), 0)
    ).astype(jnp.bfloat16)
    spread_o = jnp.dot(rep_o, occ, preferred_element_type=jnp.float32).astype(jnp.bfloat16)
    spread_o = jnp.dot(spread_o, rep_t, preferred_element_type=jnp.float32)
    same_o = (
        lax.broadcasted_iota(jnp.int32, (tall, tall), 0) % half
        == lax.broadcasted_iota(jnp.int32, (tall, tall), 1) % half
    )
    occ_w = jnp.where(same_o, spread_o, 0.0).astype(jnp.bfloat16)

    acc[...] = jnp.zeros_like(acc)

    for i in range(PARTS):
        d_copy(i).wait()
        for j in range(d_w // wide):
            at = i * d_w + j * wide
            got = jnp.dot(dbuf[:, at:at + wide], virt_w, preferred_element_type=jnp.float32)
            dbuf[:, at:at + wide] = got.astype(jnp.bfloat16)
    for i in range(PARTS):
        e_copy(i).wait()

    group = 4 * bs
    lanes = 2 * bs

    @pl.loop(0, width // group)
    def _(j):
        cols = pl.ds(pl.multiple_of(j * group, group), group)
        sides = []
        for h in range(2):
            got = jnp.dot(occ_w, ebuf[h, :, cols], preferred_element_type=jnp.float32)
            sides.append(got.reshape(bs, half, group))
        both = jnp.concatenate(sides, axis=1).astype(jnp.bfloat16)
        for p in range(4):
            rows = pl.ds(pl.multiple_of(j * (4 * aux) + p * aux, aux), aux)
            for q in range(bs // 2):
                obuf[rows, q * lanes:(q + 1) * lanes] = jnp.concatenate(
                    [both[2 * q, :, p * bs:(p + 1) * bs], both[2 * q + 1, :, p * bs:(p + 1) * bs]], axis=-1
                )

    low = lax.broadcasted_iota(jnp.int32, (bs, lanes), 1) < bs
    rows_at = aux * aux
    for n in range(aux // 4):
        for m in range(aux * bs // rows_at):
            got = lax.dot_general(
                obuf[m * rows_at:(m + 1) * rows_at, :],
                dbuf[n * group:(n + 1) * group, :],
                (((1,), (1,)), ((), ())),
                preferred_element_type=jnp.float32,
            )
            for t in range(2):
                outb[t, m * rows_at:(m + 1) * rows_at, :] = got[:, t * lanes:(t + 1) * lanes]

        @pl.loop(0, aux)
        def _(a):
            for t in range(2):
                value = outb[t, pl.ds(a, bs, stride=aux), :]
                first = tgt_ref[a * aux + n * 4 + 2 * t]
                second = tgt_ref[a * aux + n * 4 + 2 * t + 1]
                acc[first] += jnp.where(low, value, 0.0)
                acc[second] += jnp.where(low, 0.0, value)

    pairs = keep_ref.shape[0]

    def joined(i):
        one, two = acc[2 * i], acc[2 * i + 1]
        return jnp.where(low, one, two) + pltpu.roll(jnp.where(low, two, one), bs, 1)

    @pl.loop(0, pairs)
    def _(i):
        keep_ref[i] = joined(i)
        send_ref[i] = joined(pairs + i).astype(jnp.bfloat16)


def chi_blocks_of(ids, targets, table, d_parts, e_parts, bs, aux, blocks):
    half = aux // 2
    width = bs * bs
    pairs = blocks // 4
    any_spec = pl.BlockSpec(memory_space=pl.ANY)
    vmem = pl.BlockSpec(memory_space=pltpu.VMEM)
    smem = pl.BlockSpec(memory_space=pltpu.SMEM)
    return pl.pallas_call(
        functools.partial(chi_kernel, bs, aux),
        in_specs=[smem, smem, vmem] + [any_spec] * (2 * PARTS),
        out_specs=[vmem, vmem],
        out_shape=[
            jax.ShapeDtypeStruct((pairs, bs, 2 * bs), jnp.float32),
            jax.ShapeDtypeStruct((pairs, bs, 2 * bs), jnp.bfloat16),
        ],
        scratch_shapes=[
            pltpu.VMEM((aux * bs, width), jnp.bfloat16),
            pltpu.VMEM((2, bs * half, width), jnp.bfloat16),
            pltpu.VMEM((aux * bs, width), jnp.bfloat16),
            pltpu.VMEM((2, aux * bs, 2 * bs), jnp.float32),
            pltpu.VMEM((blocks, bs, 2 * bs), jnp.float32),
            pltpu.SemaphoreType.DMA((PARTS,)),
            pltpu.SemaphoreType.DMA((PARTS,)),
        ],
        compiler_params=pltpu.CompilerParams(vmem_limit_bytes=60 << 20),
        cost_estimate=pl.CostEstimate(
            flops=2 * (aux * bs) ** 2 * width * 2, bytes_accessed=4 * aux * bs * width, transcendentals=0
        ),
    )(ids, targets, table, *d_parts, *e_parts)


def local(orb, three_centre, green_occ, green_virt, pair_atoms, basis_count, chi_target):
    bs, aux = three_centre.shape[1], three_centre.shape[2]
    bits = orb.bit_length() - 1
    me = lax.axis_index("orb")

    def exchange(value, bit):
        return lax.ppermute(value, "orb", [(i, i ^ (1 << bit)) for i in range(orb)])

    lane = lax.broadcasted_iota(jnp.int32, (bs, 2 * bs), 1) % bs
    row = lax.broadcasted_iota(jnp.int32, (bs, 2 * bs), 0)
    both = jnp.concatenate([green_occ.reshape(bs, bs), green_virt.reshape(bs, bs)], axis=1)
    valid = (lane < basis_count[0]) & (row < basis_count[0])
    table = jnp.where(valid, both, jnp.zeros((), both.dtype))[None]

    for bit in reversed(range(bits)):
        table = jnp.concatenate([table, exchange(table, bit)], axis=0)

    def slot(rel):
        place = jnp.zeros_like(rel)
        for k, bit in enumerate(reversed(range(bits))):
            place = place + (((rel >> bit) & 1) << k)
        return place

    ids = slot(pair_atoms[0] ^ me)
    targets = chi_target[0]
    place = slot((targets // CB_DEV) ^ me) * CB_DEV + targets % CB_DEV

    d_parts, e_parts = zip(*[relayout(three_centre[0], i) for i in range(PARTS)])
    keep, send = chi_blocks_of(ids, place, table, d_parts, e_parts, bs, aux, orb * CB_DEV)
    for bit in range(bits):
        total = keep + exchange(send, bit).astype(jnp.float32)
        rest = total.shape[0] // 2
        if bit + 1 < bits:
            keep, send = total[:rest], total[rest:].astype(jnp.bfloat16)
    total = total.reshape(CB_DEV // 2, bs, 2, bs).transpose(0, 2, 1, 3)
    return total.reshape(CB_DEV, bs * bs)


def solution(mesh):
    in_specs = (
        P("orb", None, None, None),
        P(("grp", "orb"), None),
        P(("grp", "orb"), None),
        P("orb", None),
        P("orb"),
        P("orb", None),
    )
    out_specs = P(("grp", "orb"), None)
    return jax.shard_map(
        functools.partial(local, mesh.shape["orb"]), mesh=mesh, in_specs=in_specs, out_specs=out_specs, check_vma=False
    )
```

```python
import functools

import jax
import jax.numpy as jnp
from jax import lax
from jax.experimental import pallas as pl
from jax.experimental.pallas import tpu as pltpu
from jax.sharding import PartitionSpec as P

CB_DEV = 4
LAM = 4
PARTS = 4
VMEM = 60 << 20


def pack_kernel(count_ref, occ_ref, virt_ref, out_ref, rows_ref):
    lanes = out_ref.shape[2]
    half = out_ref.shape[1] // 2
    for i in range(half):
        rows_ref[i:i + 1, :] = occ_ref[:, i * lanes:(i + 1) * lanes].astype(jnp.float32)
        rows_ref[half + i:half + i + 1, :] = virt_ref[:, i * lanes:(i + 1) * lanes].astype(jnp.float32)
    bs = lanes // 2
    row = lax.broadcasted_iota(jnp.int32, rows_ref.shape, 0)
    lane = lax.broadcasted_iota(jnp.int32, rows_ref.shape, 1)
    count = count_ref[0]
    valid = (2 * (row % half) + lane // bs < count) & (lane % bs < count)
    out_ref[0] = jnp.where(valid, rows_ref[...], 0.0).astype(jnp.bfloat16)


def packed(basis_count, green_occ, green_virt, bs):
    vmem = pl.BlockSpec(memory_space=pltpu.VMEM)
    return pl.pallas_call(
        pack_kernel,
        in_specs=[pl.BlockSpec(memory_space=pltpu.SMEM), vmem, vmem],
        out_specs=vmem,
        out_shape=jax.ShapeDtypeStruct((1, bs, 2 * bs), jnp.bfloat16),
        scratch_shapes=[pltpu.VMEM((bs, 2 * bs), jnp.float32)],
    )(basis_count, green_occ, green_virt)


def relayout_kernel(b_ref, d_ref):
    lam, aux, width = b_ref.shape
    bs = d_ref.shape[0] // aux
    rows = aux * aux
    row = lax.broadcasted_iota(jnp.int32, (rows, rows), 0)
    col = lax.broadcasted_iota(jnp.int32, (rows, rows), 1)
    perm = (col == (row % aux) * aux + row // aux).astype(jnp.bfloat16)
    for blk in range(bs // aux):
        pieces = []
        for p in range(aux):
            at = (blk * aux + p) * bs
            pieces.append(jnp.concatenate([b_ref[i, :, at:at + bs] for i in range(lam)], axis=-1))
        stacked = jnp.concatenate(pieces, axis=0)
        moved = jnp.dot(perm, stacked, preferred_element_type=jnp.float32).astype(jnp.bfloat16)
        for a in range(aux):
            d_ref[a * bs + blk * aux:a * bs + (blk + 1) * aux, :] = moved[a * aux:(a + 1) * aux]


def relayout(integrals, part):
    bs, aux, width = integrals.shape
    steps = bs // LAM // PARTS
    return pl.pallas_call(
        relayout_kernel,
        grid=(steps,),
        in_specs=[pl.BlockSpec((LAM, aux, width), lambda i: (part * steps + i, 0, 0))],
        out_specs=pl.BlockSpec((aux * bs, LAM * bs), lambda i: (0, i)),
        out_shape=jax.ShapeDtypeStruct((aux * bs, bs // PARTS * bs), jnp.bfloat16),
        compiler_params=pltpu.CompilerParams(vmem_limit_bytes=VMEM),
        cost_estimate=pl.CostEstimate(
            flops=2 * bs * aux * width * 256 // PARTS,
            bytes_accessed=4 * bs * aux * width // PARTS,
            transcendentals=0,
        ),
    )(integrals)


def chi_kernel(bs, aux, sends, ids_ref, tgt_ref, table_ref, b_ref, *refs):
    d_parts, refs = refs[:PARTS], refs[PARTS:]
    keep_ref, send_refs, refs = refs[0], refs[1:1 + sends], refs[1 + sends:]
    dbuf, bbuf, obuf, out0, out1, d_sem, b_sem, *accs = refs
    low_acc, high_acc = accs[0], accs[-1]
    half = aux // 2
    width = bs * bs
    wide = LAM * bs
    per = width // PARTS // wide

    def d_copy(part, j):
        src = d_parts[part].at[:, pl.ds(pl.multiple_of(j * wide, wide), wide)]
        at = pl.multiple_of((part * per + j) * wide, wide)
        return pltpu.make_async_copy(src, dbuf.at[:, pl.ds(at, wide)], d_sem.at[part * per + j])

    def b_copy(j):
        cols = pl.ds(pl.multiple_of(j * wide, wide), wide)
        return pltpu.make_async_copy(b_ref.at[:, :, cols], bbuf.at[:, :, cols], b_sem.at[j])

    for part in range(PARTS):
        for j in range(per):
            d_copy(part, j).start()
            b_copy(part * per + j).start()

    occ = table_ref[ids_ref[0], :bs // 2]
    virt = table_ref[ids_ref[1], bs // 2:]

    def spread_rows(block, of_row, count):
        shape = (count, bs // 2)
        pick = of_row(lax.broadcasted_iota(jnp.int32, shape, 0)) // 2 == lax.broadcasted_iota(jnp.int32, shape, 1)
        got = jnp.dot(pick.astype(jnp.bfloat16), block, preferred_element_type=jnp.float32)
        odd = of_row(lax.broadcasted_iota(jnp.int32, (count, bs), 0)) % 2 == 1
        return jnp.where(odd, got[:, bs:], got[:, :bs])

    spread = spread_rows(virt, lambda i: i % bs, wide)
    spread = jnp.concatenate([spread] * LAM, axis=1)
    same = (
        lax.broadcasted_iota(jnp.int32, (wide, wide), 0) // bs == lax.broadcasted_iota(jnp.int32, (wide, wide), 1) // bs
    )
    virt_w = jnp.where(same, spread, 0.0).astype(jnp.bfloat16)

    tall = bs * half
    rep_t = (
        lax.broadcasted_iota(jnp.int32, (bs, tall), 1) // half == lax.broadcasted_iota(jnp.int32, (bs, tall), 0)
    ).astype(jnp.bfloat16)
    spread_o = spread_rows(occ, lambda i: i // half, tall).astype(jnp.bfloat16)
    spread_o = jnp.dot(spread_o, rep_t, preferred_element_type=jnp.float32)
    same_o = (
        lax.broadcasted_iota(jnp.int32, (tall, tall), 0) % half
        == lax.broadcasted_iota(jnp.int32, (tall, tall), 1) % half
    )
    occ_w = jnp.where(same_o, spread_o, 0.0).astype(jnp.bfloat16)

    for ref in accs:
        ref[...] = jnp.zeros_like(ref)

    lanes = 2 * bs
    for part in range(PARTS):

        @pl.loop(0, per)
        def _(i):
            j = part * per + i
            d_copy(part, i).wait()
            b_copy(j).wait()
            cols = pl.ds(pl.multiple_of(j * wide, wide), wide)
            got = jnp.dot(dbuf[:, cols], virt_w, preferred_element_type=jnp.float32)
            dbuf[:, cols] = got.astype(jnp.bfloat16)
            block = bbuf[:, :, cols].astype(jnp.float32)
            sides = []
            for h in range(2):
                side = block[:, h * half:(h + 1) * half, :].reshape(tall, wide).astype(jnp.bfloat16)
                got = jnp.dot(occ_w, side, preferred_element_type=jnp.float32)
                sides.append(got.reshape(bs, half, wide))
            both = jnp.concatenate(sides, axis=1).astype(jnp.bfloat16)
            for p in range(LAM):
                rows = pl.ds(pl.multiple_of(j * (LAM * aux) + p * aux, aux), aux)
                for q in range(bs // 2):
                    obuf[rows, q * lanes:(q + 1) * lanes] = jnp.concatenate(
                        [both[2 * q, :, p * bs:(p + 1) * bs], both[2 * q + 1, :, p * bs:(p + 1) * bs]], axis=-1
                    )

    low = lax.broadcasted_iota(jnp.int32, (bs, lanes), 1) < bs
    shared = len(accs) == 1
    outs = (out0, out1)
    group = 4 * bs

    def scatter(n):
        for a in range(aux):
            for t in range(2):
                value = outs[n % 2][t, pl.ds(a, bs, stride=aux), :]
                first = tgt_ref[a * aux + n * 4 + 2 * t]
                second = tgt_ref[a * aux + n * 4 + 2 * t + 1]
                low_acc[first] += jnp.where(low, value, 0.0) if shared else value
                high_acc[second] += jnp.where(low, 0.0, value) if shared else value

    for n in range(aux // 4):
        if n:
            scatter(n - 1)
        got = lax.dot_general(
            obuf[...],
            dbuf[n * group:(n + 1) * group, :],
            (((1,), (1,)), ((), ())),
            preferred_element_type=jnp.float32,
        )
        for t in range(2):
            outs[n % 2][t] = got[:, t * lanes:(t + 1) * lanes]
    scatter(aux // 4 - 1)

    pairs = keep_ref.shape[0]

    def joined(i):
        if shared:
            one, two = low_acc[2 * i], low_acc[2 * i + 1]
            return jnp.where(low, one, two) + pltpu.roll(jnp.where(low, two, one), bs, 1)
        left = jnp.where(low, low_acc[2 * i], high_acc[2 * i + 1])
        right = jnp.where(low, low_acc[2 * i + 1], high_acc[2 * i])
        return left + pltpu.roll(right, bs, 1)

    @pl.loop(0, pairs)
    def _(i):
        keep_ref[i] = joined(i)
        for k, send_ref in enumerate(send_refs):
            send_ref[i] = joined((k + 1) * pairs + i).astype(jnp.bfloat16)


def chi_blocks_of(ids, targets, table, integrals, d_parts, blocks, sends):
    bs, aux, width = integrals.shape
    pairs = blocks // 2 // (sends + 1)
    any_spec = pl.BlockSpec(memory_space=pl.ANY)
    vmem = pl.BlockSpec(memory_space=pltpu.VMEM)
    smem = pl.BlockSpec(memory_space=pltpu.SMEM)
    acc = pltpu.VMEM((blocks, bs, 2 * bs), jnp.float32)
    chunks = width // (LAM * bs)
    return pl.pallas_call(
        functools.partial(chi_kernel, bs, aux, sends),
        in_specs=[smem, smem, vmem] + [any_spec] * (1 + PARTS),
        out_specs=[vmem] * (1 + sends),
        out_shape=[jax.ShapeDtypeStruct((pairs, bs, 2 * bs), jnp.float32)]
        + [jax.ShapeDtypeStruct((pairs, bs, 2 * bs), jnp.bfloat16)] * sends,
        scratch_shapes=[
            pltpu.VMEM((aux * bs, width), jnp.bfloat16),
            pltpu.VMEM((bs, aux, width), jnp.bfloat16),
            pltpu.VMEM((aux * bs, width), jnp.bfloat16),
            pltpu.VMEM((2, aux * bs, 2 * bs), jnp.float32),
            pltpu.VMEM((2, aux * bs, 2 * bs), jnp.float32),
            pltpu.SemaphoreType.DMA((chunks,)),
            pltpu.SemaphoreType.DMA((chunks,)),
        ]
        + [acc] * (2 if blocks <= 128 else 1),
        compiler_params=pltpu.CompilerParams(vmem_limit_bytes=VMEM),
        cost_estimate=pl.CostEstimate(
            flops=2 * (aux * bs) ** 2 * width * 2, bytes_accessed=4 * aux * bs * width, transcendentals=0
        ),
    )(ids, targets, table, integrals, *d_parts)


def gather_rounds(bits):
    rounds = []
    while bits:
        step = min(2, bits)
        bits -= step
        rounds.append((bits, step))
    return rounds


def sum_rounds(bits):
    rounds, at = [], 0
    while at < bits:
        step = 1 if at < 2 else min(2, bits - at)
        rounds.append((at, step))
        at += step
    return rounds


def local(orb, three_centre, green_occ, green_virt, pair_atoms, basis_count, chi_target):
    bs = three_centre.shape[1]
    bits = orb.bit_length() - 1
    me = lax.axis_index("orb")

    def exchange(value, flip):
        return lax.ppermute(value, "orb", [(i, i ^ flip) for i in range(orb)])

    table = packed(basis_count, green_occ, green_virt, bs)
    ids = jnp.zeros_like(pair_atoms[0])
    rel = pair_atoms[0] ^ me
    count = 1
    for shift, step in gather_rounds(bits):
        table = jnp.concatenate([table] + [exchange(table, v << shift) for v in range(1, 1 << step)], axis=0)
        ids = ids + ((rel >> shift) & ((1 << step) - 1)) * count
        count <<= step

    targets = chi_target[0]
    rel = (targets // CB_DEV) ^ me
    place = jnp.zeros_like(targets)
    for shift, step in sum_rounds(bits):
        place = (place << step) | ((rel >> shift) & ((1 << step) - 1))
    place = place * CB_DEV + targets % CB_DEV

    d_parts = [relayout(three_centre[0], i) for i in range(PARTS)]
    rounds = sum_rounds(bits)
    total, *sends = chi_blocks_of(ids, place, table, three_centre[0], d_parts, orb * CB_DEV, (1 << rounds[0][1]) - 1)
    for k, (shift, step) in enumerate(rounds):
        if k:
            rest = total.shape[0] >> step
            sends = [total[v * rest:(v + 1) * rest].astype(jnp.bfloat16) for v in range(1, 1 << step)]
            total = total[:rest]
        for v, send in enumerate(sends):
            total = total + exchange(send, (v + 1) << shift).astype(jnp.float32)
    total = total.reshape(CB_DEV // 2, bs, 2, bs).transpose(0, 2, 1, 3)
    return total.reshape(CB_DEV, bs * bs)


def solution(mesh):
    in_specs = (
        P("orb", None, None, None),
        P(("grp", "orb"), None),
        P(("grp", "orb"), None),
        P("orb", None),
        P("orb"),
        P("orb", None),
    )
    out_specs = P(("grp", "orb"), None)
    return jax.shard_map(
        functools.partial(local, mesh.shape["orb"]), mesh=mesh, in_specs=in_specs, out_specs=out_specs, check_vma=False
    )
```

```python
import functools

import jax
import jax.numpy as jnp
from jax import lax
from jax.experimental import pallas as pl
from jax.experimental.pallas import tpu as pltpu
from jax.sharding import PartitionSpec as P

CB_DEV = 4
LAM = 4
PARTS = 4
GRANT = 8 << 20


def pack_kernel(count_ref, occ_ref, virt_ref, out_ref, rows_ref):
    lanes = out_ref.shape[2]
    half = out_ref.shape[1] // 2
    for i in range(half):
        rows_ref[i:i + 1, :] = occ_ref[:, i * lanes:(i + 1) * lanes].astype(jnp.float32)
        rows_ref[half + i:half + i + 1, :] = virt_ref[:, i * lanes:(i + 1) * lanes].astype(jnp.float32)
    bs = lanes // 2
    row = lax.broadcasted_iota(jnp.int32, rows_ref.shape, 0)
    lane = lax.broadcasted_iota(jnp.int32, rows_ref.shape, 1)
    count = count_ref[0]
    valid = (2 * (row % half) + lane // bs < count) & (lane % bs < count)
    out_ref[0] = jnp.where(valid, rows_ref[...], 0.0).astype(jnp.bfloat16)


def packed(basis_count, green_occ, green_virt, bs):
    vmem = pl.BlockSpec(memory_space=pltpu.VMEM)
    return pl.pallas_call(
        pack_kernel,
        in_specs=[pl.BlockSpec(memory_space=pltpu.SMEM), vmem, vmem],
        out_specs=vmem,
        out_shape=jax.ShapeDtypeStruct((1, bs, 2 * bs), jnp.bfloat16),
        scratch_shapes=[pltpu.VMEM((bs, 2 * bs), jnp.float32)],
    )(basis_count, green_occ, green_virt)


def relayout_kernel(part, b_ref, d_ref):
    bs, aux, _ = b_ref.shape
    wide = LAM * bs
    rows = aux * aux
    row = lax.broadcasted_iota(jnp.int32, (rows, rows), 0)
    col = lax.broadcasted_iota(jnp.int32, (rows, rows), 1)
    perm = (col == (row % aux) * aux + row // aux).astype(jnp.bfloat16)

    @pl.loop(0, bs // PARTS // LAM)
    def _(i):
        first = part * (bs // PARTS) + i * LAM
        cols = pl.ds(pl.multiple_of(i * wide, wide), wide)
        for blk in range(bs // aux):
            pieces = []
            for p in range(aux):
                at = (blk * aux + p) * bs
                pieces.append(jnp.concatenate([b_ref[first + k, :, at:at + bs] for k in range(LAM)], axis=-1))
            stacked = jnp.concatenate(pieces, axis=0)
            moved = jnp.dot(perm, stacked, preferred_element_type=jnp.float32).astype(jnp.bfloat16)
            for a in range(aux):
                d_ref[a * bs + blk * aux:a * bs + (blk + 1) * aux, cols] = moved[a * aux:(a + 1) * aux]


def in_vmem(count):
    return [pl.BlockSpec(memory_space=pltpu.VMEM)] * count


def in_smem(count):
    return [pl.BlockSpec(memory_space=pltpu.SMEM)] * count


def relayout(integrals, part):
    bs, aux, width = integrals.shape
    return pl.pallas_call(
        functools.partial(relayout_kernel, part),
        in_specs=in_vmem(1),
        out_specs=in_vmem(1)[0],
        out_shape=jax.ShapeDtypeStruct((aux * bs, bs // PARTS * bs), jnp.bfloat16),
        compiler_params=pltpu.CompilerParams(vmem_limit_bytes=GRANT),
        cost_estimate=pl.CostEstimate(
            flops=2 * bs * aux * width * 256 // PARTS,
            bytes_accessed=4 * bs * aux * width // PARTS,
            transcendentals=0,
        ),
    )(integrals)


def spread_rows(block, of_row, count, bs):
    shape = (count, bs // 2)
    pick = of_row(lax.broadcasted_iota(jnp.int32, shape, 0)) // 2 == lax.broadcasted_iota(jnp.int32, shape, 1)
    got = jnp.dot(pick.astype(jnp.bfloat16), block, preferred_element_type=jnp.float32)
    odd = of_row(lax.broadcasted_iota(jnp.int32, (count, bs), 0)) % 2 == 1
    return jnp.where(odd, got[:, bs:], got[:, :bs])


def virt_kernel(bs, ids_ref, table_ref, *refs):
    d_parts, v_ref = refs[:PARTS], refs[PARTS]
    wide = LAM * bs
    spread = spread_rows(table_ref[ids_ref[1], bs // 2:], lambda i: i % bs, wide, bs)
    spread = jnp.concatenate([spread] * LAM, axis=1)
    same = (
        lax.broadcasted_iota(jnp.int32, (wide, wide), 0) // bs == lax.broadcasted_iota(jnp.int32, (wide, wide), 1) // bs
    )
    virt_w = jnp.where(same, spread, 0.0).astype(jnp.bfloat16)
    each = d_parts[0].shape[1]
    for part in range(PARTS):
        for at in range(0, each, wide):
            got = jnp.dot(d_parts[part][:, at:at + wide], virt_w, preferred_element_type=jnp.float32)
            v_ref[:, part * each + at:part * each + at + wide] = got.astype(jnp.bfloat16)


def occ_kernel(ids_ref, table_ref, b_ref, o_ref):
    bs, aux, width = b_ref.shape
    half = aux // 2
    wide = LAM * bs
    lanes = 2 * bs
    tall = bs * half
    rep_t = (
        lax.broadcasted_iota(jnp.int32, (bs, tall), 1) // half == lax.broadcasted_iota(jnp.int32, (bs, tall), 0)
    ).astype(jnp.bfloat16)
    spread = spread_rows(table_ref[ids_ref[0], :bs // 2], lambda i: i // half, tall, bs).astype(jnp.bfloat16)
    spread = jnp.dot(spread, rep_t, preferred_element_type=jnp.float32)
    same = (
        lax.broadcasted_iota(jnp.int32, (tall, tall), 0) % half
        == lax.broadcasted_iota(jnp.int32, (tall, tall), 1) % half
    )
    occ_w = jnp.where(same, spread, 0.0).astype(jnp.bfloat16)

    @pl.loop(0, width // wide, unroll=2)
    def _(j):
        cols = pl.ds(pl.multiple_of(j * wide, wide), wide)
        block = b_ref[:, :, cols].astype(jnp.float32)
        sides = []
        for h in range(2):
            side = block[:, h * half:(h + 1) * half, :].reshape(tall, wide).astype(jnp.bfloat16)
            got = jnp.dot(occ_w, side, preferred_element_type=jnp.float32)
            sides.append(got.reshape(bs, half, wide))
        both = jnp.concatenate(sides, axis=1).astype(jnp.bfloat16)
        for p in range(LAM):
            rows = pl.ds(pl.multiple_of(j * (LAM * aux) + p * aux, aux), aux)
            for q in range(bs // 2):
                o_ref[rows, q * lanes:(q + 1) * lanes] = jnp.concatenate(
                    [both[2 * q, :, p * bs:(p + 1) * bs], both[2 * q + 1, :, p * bs:(p + 1) * bs]], axis=-1
                )


def chi_kernel(bs, sends, tgt_ref, o_ref, v_ref, *refs):
    keep_ref, send_refs, refs = refs[0], refs[1:1 + sends], refs[1 + sends:]
    out0, out1, *accs = refs
    low_acc, high_acc = accs[0], accs[-1]
    aux = o_ref.shape[0] // bs
    lanes = 2 * bs
    for ref in accs:
        ref[...] = jnp.zeros_like(ref)
    low = lax.broadcasted_iota(jnp.int32, (bs, lanes), 1) < bs
    shared = len(accs) == 1
    outs = (out0, out1)
    group = 4 * bs

    def scatter(n):
        for a in range(aux):
            for t in range(2):
                value = outs[n % 2][t, pl.ds(a, bs, stride=aux), :]
                first = tgt_ref[a * aux + n * 4 + 2 * t]
                second = tgt_ref[a * aux + n * 4 + 2 * t + 1]
                low_acc[first] += jnp.where(low, value, 0.0) if shared else value
                high_acc[second] += jnp.where(low, 0.0, value) if shared else value

    for n in range(aux // 4):
        if n:
            scatter(n - 1)
        got = lax.dot_general(
            o_ref[...],
            v_ref[n * group:(n + 1) * group, :],
            (((1,), (1,)), ((), ())),
            preferred_element_type=jnp.float32,
        )
        for t in range(2):
            outs[n % 2][t] = got[:, t * lanes:(t + 1) * lanes]
    scatter(aux // 4 - 1)

    pairs = keep_ref.shape[0]

    def joined(i):
        if shared:
            one, two = low_acc[2 * i], low_acc[2 * i + 1]
            return jnp.where(low, one, two) + pltpu.roll(jnp.where(low, two, one), bs, 1)
        left = jnp.where(low, low_acc[2 * i], high_acc[2 * i + 1])
        right = jnp.where(low, low_acc[2 * i + 1], high_acc[2 * i])
        return left + pltpu.roll(right, bs, 1)

    @pl.loop(0, pairs)
    def _(i):
        keep_ref[i] = joined(i)
        for k, send_ref in enumerate(send_refs):
            send_ref[i] = joined((k + 1) * pairs + i).astype(jnp.bfloat16)


def chi_blocks_of(ids, targets, table, integrals, d_parts, blocks, sends):
    bs, aux, width = integrals.shape
    pairs = blocks // 2 // (sends + 1)
    side = jax.ShapeDtypeStruct((aux * bs, width), jnp.bfloat16)
    params = pltpu.CompilerParams(vmem_limit_bytes=GRANT)
    cost = pl.CostEstimate(flops=2 * (aux * bs) ** 2 * width, bytes_accessed=4 * aux * bs * width, transcendentals=0)
    virt_side = pl.pallas_call(
        functools.partial(virt_kernel, bs),
        in_specs=in_smem(1) + in_vmem(1 + PARTS),
        out_specs=in_vmem(1)[0],
        out_shape=side,
        compiler_params=params,
        cost_estimate=cost,
    )(ids, table, *d_parts)
    occ_side = pl.pallas_call(
        occ_kernel,
        in_specs=in_smem(1) + in_vmem(2),
        out_specs=in_vmem(1)[0],
        out_shape=side,
        compiler_params=params,
        cost_estimate=cost,
    )(ids, table, integrals)
    accs = 2 if blocks <= 128 else 1
    acc = pltpu.VMEM((blocks, bs, 2 * bs), jnp.float32)
    out = pltpu.VMEM((2, aux * bs, 2 * bs), jnp.float32)
    return pl.pallas_call(
        functools.partial(chi_kernel, bs, sends),
        in_specs=in_smem(1) + in_vmem(2),
        out_specs=in_vmem(1 + sends),
        out_shape=[jax.ShapeDtypeStruct((pairs, bs, 2 * bs), jnp.float32)]
        + [jax.ShapeDtypeStruct((pairs, bs, 2 * bs), jnp.bfloat16)] * sends,
        scratch_shapes=[out, out] + [acc] * accs,
        compiler_params=pltpu.CompilerParams(vmem_limit_bytes=GRANT + 4 * (accs * blocks + 2 * aux * 2) * bs * 2 * bs),
        cost_estimate=cost,
    )(targets, occ_side, virt_side)


def gather_rounds(bits):
    rounds = []
    while bits:
        step = min(2, bits)
        bits -= step
        rounds.append((bits, step))
    return rounds


def sum_rounds(bits):
    rounds, at = [], 0
    while at < bits:
        step = 1 if at < 2 else min(2, bits - at)
        rounds.append((at, step))
        at += step
    return rounds


def local(orb, three_centre, green_occ, green_virt, pair_atoms, basis_count, chi_target):
    bs = three_centre.shape[1]
    bits = orb.bit_length() - 1
    me = lax.axis_index("orb")

    def exchange(value, flip):
        return lax.ppermute(value, "orb", [(i, i ^ flip) for i in range(orb)])

    table = packed(basis_count, green_occ, green_virt, bs)
    ids = jnp.zeros_like(pair_atoms[0])
    rel = pair_atoms[0] ^ me
    count = 1
    for shift, step in gather_rounds(bits):
        table = jnp.concatenate([table] + [exchange(table, v << shift) for v in range(1, 1 << step)], axis=0)
        ids = ids + ((rel >> shift) & ((1 << step) - 1)) * count
        count <<= step

    targets = chi_target[0]
    rel = (targets // CB_DEV) ^ me
    place = jnp.zeros_like(targets)
    for shift, step in sum_rounds(bits):
        place = (place << step) | ((rel >> shift) & ((1 << step) - 1))
    place = place * CB_DEV + targets % CB_DEV

    d_parts = [relayout(three_centre[0], i) for i in range(PARTS)]
    rounds = sum_rounds(bits)
    total, *sends = chi_blocks_of(ids, place, table, three_centre[0], d_parts, orb * CB_DEV, (1 << rounds[0][1]) - 1)
    for k, (shift, step) in enumerate(rounds):
        if k:
            rest = total.shape[0] >> step
            sends = [total[v * rest:(v + 1) * rest].astype(jnp.bfloat16) for v in range(1, 1 << step)]
            total = total[:rest]
        for v, send in enumerate(sends):
            total = total + exchange(send, (v + 1) << shift).astype(jnp.float32)
    total = total.reshape(CB_DEV // 2, bs, 2, bs).transpose(0, 2, 1, 3)
    return total.reshape(CB_DEV, bs * bs)


def solution(mesh):
    in_specs = (
        P("orb", None, None, None),
        P(("grp", "orb"), None),
        P(("grp", "orb"), None),
        P("orb", None),
        P("orb"),
        P("orb", None),
    )
    out_specs = P(("grp", "orb"), None)
    return jax.shard_map(
        functools.partial(local, mesh.shape["orb"]), mesh=mesh, in_specs=in_specs, out_specs=out_specs, check_vma=False
    )
```

```python
import functools

import jax
import jax.numpy as jnp
from jax import lax
from jax.experimental import pallas as pl
from jax.experimental.pallas import tpu as pltpu
from jax.sharding import PartitionSpec as P

CB_DEV = 4
LAM = 4
PARTS = 4
GRANT = 8 << 20


def pack_kernel(owner_rounds, table_rounds, me_ref, count_ref, pair_ref, tgt_ref, occ_ref, virt_ref, *refs):
    out_ref, ids_ref, place_ref, rows_ref = refs
    lanes = out_ref.shape[2]
    half = out_ref.shape[1] // 2
    for i in range(half):
        rows_ref[i:i + 1, :] = occ_ref[:, i * lanes:(i + 1) * lanes].astype(jnp.float32)
        rows_ref[half + i:half + i + 1, :] = virt_ref[:, i * lanes:(i + 1) * lanes].astype(jnp.float32)
    bs = lanes // 2
    row = lax.broadcasted_iota(jnp.int32, rows_ref.shape, 0)
    lane = lax.broadcasted_iota(jnp.int32, rows_ref.shape, 1)
    count = count_ref[0]
    valid = (2 * (row % half) + lane // bs < count) & (lane % bs < count)
    out_ref[0] = jnp.where(valid, rows_ref[...], 0.0).astype(jnp.bfloat16)

    me = me_ref[0]
    rel = pair_ref[...] ^ me
    ids, weight = jnp.zeros_like(rel), 1
    for shift, step in table_rounds:
        ids = ids + ((rel >> shift) & ((1 << step) - 1)) * weight
        weight <<= step
    ids_ref[...] = ids

    targets = tgt_ref[...]
    rel = (targets // CB_DEV) ^ me
    place = jnp.zeros_like(targets)
    for shift, step in owner_rounds:
        place = (place << step) | ((rel >> shift) & ((1 << step) - 1))
    place_ref[...] = place * CB_DEV + targets % CB_DEV


def packed(me, basis_count, pair_atoms, chi_target, green_occ, green_virt, bs, bits):
    return pl.pallas_call(
        functools.partial(pack_kernel, sum_rounds(bits), gather_rounds(bits)),
        in_specs=in_smem(2) + in_vmem(4),
        out_specs=in_vmem(3),
        out_shape=[
            jax.ShapeDtypeStruct((1, bs, 2 * bs), jnp.bfloat16),
            jax.ShapeDtypeStruct(pair_atoms.shape, jnp.int32),
            jax.ShapeDtypeStruct(chi_target.shape, jnp.int32),
        ],
        scratch_shapes=[pltpu.VMEM((bs, 2 * bs), jnp.float32)],
        compiler_params=pltpu.CompilerParams(vmem_limit_bytes=2 << 20),
    )(me, basis_count, pair_atoms, chi_target, green_occ, green_virt)


def relayout_kernel(part, b_ref, _, d_ref):
    bs, aux, _ = b_ref.shape
    wide = LAM * bs
    rows = aux * aux
    row = lax.broadcasted_iota(jnp.int32, (rows, rows), 0)
    col = lax.broadcasted_iota(jnp.int32, (rows, rows), 1)
    perm = (col == (row % aux) * aux + row // aux).astype(jnp.bfloat16)

    @pl.loop(0, bs // PARTS // LAM)
    def _(i):
        first = part * (bs // PARTS) + i * LAM
        cols = pl.ds(pl.multiple_of(i * wide, wide), wide)
        for blk in range(bs // aux):
            pieces = []
            for p in range(aux):
                at = (blk * aux + p) * bs
                pieces.append(jnp.concatenate([b_ref[first + k, :, at:at + bs] for k in range(LAM)], axis=-1))
            stacked = jnp.concatenate(pieces, axis=0)
            moved = jnp.dot(perm, stacked, preferred_element_type=jnp.float32).astype(jnp.bfloat16)
            for a in range(aux):
                d_ref[a * bs + blk * aux:a * bs + (blk + 1) * aux, cols] = moved[a * aux:(a + 1) * aux]


def in_vmem(count):
    return [pl.BlockSpec(memory_space=pltpu.VMEM)] * count


def in_smem(count):
    return [pl.BlockSpec(memory_space=pltpu.SMEM)] * count


def relayout(integrals, part, after):
    bs, aux, width = integrals.shape
    return pl.pallas_call(
        functools.partial(relayout_kernel, part),
        in_specs=in_vmem(1) + [pl.BlockSpec(memory_space=pl.ANY)],
        out_specs=in_vmem(1)[0],
        out_shape=jax.ShapeDtypeStruct((aux * bs, bs // PARTS * bs), jnp.bfloat16),
        compiler_params=pltpu.CompilerParams(vmem_limit_bytes=GRANT),
        cost_estimate=pl.CostEstimate(
            flops=2 * bs * aux * width * 256 // PARTS,
            bytes_accessed=4 * bs * aux * width // PARTS,
            transcendentals=0,
        ),
    )(integrals, after)


def spread_rows(block, of_row, count, bs):
    shape = (count, bs // 2)
    pick = of_row(lax.broadcasted_iota(jnp.int32, shape, 0)) // 2 == lax.broadcasted_iota(jnp.int32, shape, 1)
    got = jnp.dot(pick.astype(jnp.bfloat16), block, preferred_element_type=jnp.float32)
    odd = of_row(lax.broadcasted_iota(jnp.int32, (count, bs), 0)) % 2 == 1
    return jnp.where(odd, got[:, bs:], got[:, :bs])


def green_block(tables, slot):
    count = tables[0].shape[0]
    block = tables[0][slot % count].astype(jnp.float32)
    for k in range(1, len(tables)):
        block = jnp.where(slot // count == k, tables[k][slot % count].astype(jnp.float32), block)
    return block.astype(jnp.bfloat16)


def virt_kernel(bs, pieces, ids_ref, *refs):
    tables, d_parts, v_ref = refs[:pieces], refs[pieces:pieces + PARTS], refs[-1]
    wide = LAM * bs
    spread = spread_rows(green_block(tables, ids_ref[1])[bs // 2:], lambda i: i % bs, wide, bs)
    spread = jnp.concatenate([spread] * LAM, axis=1)
    same = (
        lax.broadcasted_iota(jnp.int32, (wide, wide), 0) // bs == lax.broadcasted_iota(jnp.int32, (wide, wide), 1) // bs
    )
    virt_w = jnp.where(same, spread, 0.0).astype(jnp.bfloat16)
    each = d_parts[0].shape[1]
    for part in range(PARTS):
        for at in range(0, each, wide):
            got = jnp.dot(d_parts[part][:, at:at + wide], virt_w, preferred_element_type=jnp.float32)
            v_ref[:, part * each + at:part * each + at + wide] = got.astype(jnp.bfloat16)


def occ_kernel(pieces, ids_ref, *refs):
    tables, (b_ref, o_ref) = refs[:pieces], refs[pieces:]
    bs, aux, width = b_ref.shape
    half = aux // 2
    wide = 8 * bs
    lanes = 2 * bs
    tall = bs * half
    rep_t = (
        lax.broadcasted_iota(jnp.int32, (bs, tall), 1) // half == lax.broadcasted_iota(jnp.int32, (bs, tall), 0)
    ).astype(jnp.bfloat16)
    spread = spread_rows(green_block(tables, ids_ref[0])[:bs // 2], lambda i: i // half, tall, bs).astype(jnp.bfloat16)
    spread = jnp.dot(spread, rep_t, preferred_element_type=jnp.float32)
    same = (
        lax.broadcasted_iota(jnp.int32, (tall, tall), 0) % half
        == lax.broadcasted_iota(jnp.int32, (tall, tall), 1) % half
    )
    occ_w = jnp.where(same, spread, 0.0).astype(jnp.bfloat16)

    @pl.loop(0, width // wide)
    def _(j):
        cols = pl.ds(pl.multiple_of(j * wide, wide), wide)
        block = b_ref[:, :, cols].astype(jnp.float32)
        sides = []
        for h in range(2):
            side = block[:, h * half:(h + 1) * half, :].reshape(tall, wide).astype(jnp.bfloat16)
            got = jnp.dot(occ_w, side, preferred_element_type=jnp.float32)
            sides.append(got.reshape(bs, half, wide))
        both = jnp.concatenate(sides, axis=1).astype(jnp.bfloat16)
        for p in range(wide // bs):
            rows = pl.ds(pl.multiple_of(j * (wide // bs * aux) + p * aux, aux), aux)
            for q in range(bs // 2):
                o_ref[rows, q * lanes:(q + 1) * lanes] = jnp.concatenate(
                    [both[2 * q, :, p * bs:(p + 1) * bs], both[2 * q + 1, :, p * bs:(p + 1) * bs]], axis=-1
                )


def chi_kernel(bs, sends, tgt_ref, o_ref, v_ref, *refs):
    keep_ref, send_refs, refs = refs[0], refs[1:1 + sends], refs[1 + sends:]
    out0, out1, *accs = refs
    low_acc, high_acc = accs[0], accs[-1]
    aux = o_ref.shape[0] // bs
    lanes = 2 * bs
    for ref in accs:
        ref[...] = jnp.zeros_like(ref)
    low = lax.broadcasted_iota(jnp.int32, (bs, lanes), 1) < bs
    shared = len(accs) == 1
    outs = (out0, out1)
    group = 4 * bs

    def scatter(n):
        for a in range(aux):
            for t in range(2):
                value = outs[n % 2][t, pl.ds(a, bs, stride=aux), :]
                first = tgt_ref[a * aux + n * 4 + 2 * t]
                second = tgt_ref[a * aux + n * 4 + 2 * t + 1]
                low_acc[first] += jnp.where(low, value, 0.0) if shared else value
                high_acc[second] += jnp.where(low, 0.0, value) if shared else value

    for n in range(aux // 4):
        if n:
            scatter(n - 1)
        got = lax.dot_general(
            o_ref[...],
            v_ref[n * group:(n + 1) * group, :],
            (((1,), (1,)), ((), ())),
            preferred_element_type=jnp.float32,
        )
        for t in range(2):
            outs[n % 2][t] = got[:, t * lanes:(t + 1) * lanes]
    scatter(aux // 4 - 1)

    pairs = keep_ref.shape[0]

    def joined(i):
        if shared:
            one, two = low_acc[2 * i], low_acc[2 * i + 1]
            return jnp.where(low, one, two) + pltpu.roll(jnp.where(low, two, one), bs, 1)
        left = jnp.where(low, low_acc[2 * i], high_acc[2 * i + 1])
        right = jnp.where(low, low_acc[2 * i + 1], high_acc[2 * i])
        return left + pltpu.roll(right, bs, 1)

    @pl.loop(0, pairs)
    def _(i):
        keep_ref[i] = joined(i)
        for k, send_ref in enumerate(send_refs):
            send_ref[i] = joined((k + 1) * pairs + i).astype(jnp.bfloat16)


def chi_blocks_of(ids, targets, tables, integrals, d_parts, blocks, sends):
    bs, aux, width = integrals.shape
    pairs = blocks // 2 // (sends + 1)
    side = jax.ShapeDtypeStruct((aux * bs, width), jnp.bfloat16)
    params = pltpu.CompilerParams(vmem_limit_bytes=GRANT)
    cost = pl.CostEstimate(flops=2 * (aux * bs) ** 2 * width, bytes_accessed=4 * aux * bs * width, transcendentals=0)
    virt_side = pl.pallas_call(
        functools.partial(virt_kernel, bs, len(tables)),
        in_specs=in_smem(1) + in_vmem(len(tables) + PARTS),
        out_specs=in_vmem(1)[0],
        out_shape=side,
        compiler_params=params,
        cost_estimate=cost,
    )(ids, *tables, *d_parts)
    occ_side = pl.pallas_call(
        functools.partial(occ_kernel, len(tables)),
        in_specs=in_smem(1) + in_vmem(len(tables) + 1),
        out_specs=in_vmem(1)[0],
        out_shape=side,
        compiler_params=params,
        cost_estimate=cost,
    )(ids, *tables, integrals)
    accs = 2 if blocks <= 128 else 1
    acc = pltpu.VMEM((blocks, bs, 2 * bs), jnp.float32)
    out = pltpu.VMEM((2, aux * bs, 2 * bs), jnp.float32)
    return pl.pallas_call(
        functools.partial(chi_kernel, bs, sends),
        in_specs=in_smem(1) + in_vmem(2),
        out_specs=in_vmem(1 + sends),
        out_shape=[jax.ShapeDtypeStruct((pairs, bs, 2 * bs), jnp.float32)]
        + [jax.ShapeDtypeStruct((pairs, bs, 2 * bs), jnp.bfloat16)] * sends,
        scratch_shapes=[out, out] + [acc] * accs,
        compiler_params=pltpu.CompilerParams(vmem_limit_bytes=GRANT + 4 * (accs * blocks + 2 * aux * 2) * bs * 2 * bs),
        cost_estimate=cost,
    )(targets, occ_side, virt_side)


def gather_rounds(bits):
    return [(shift, step) for shift, step in reversed(sum_rounds(bits))]


def sum_rounds(bits):
    rounds, at = [], 0
    while at < bits:
        step = 1 if at < 2 else min(2, bits - at)
        rounds.append((at, step))
        at += step
    return rounds


def local(orb, three_centre, green_occ, green_virt, pair_atoms, basis_count, chi_target):
    bs = three_centre.shape[1]
    bits = orb.bit_length() - 1
    me = lax.axis_index("orb")

    def exchange(value, flip):
        return lax.ppermute(value, "orb", [(i, i ^ flip) for i in range(orb)])

    integrals = three_centre[0]
    table, ids, place = packed(
        me[None].astype(jnp.int32), basis_count, pair_atoms, chi_target, green_occ, green_virt, bs, bits
    )
    rounds = gather_rounds(bits)
    tables, after = [table], [table]
    for shift, step in rounds:
        table = tables[0] if len(tables) == 1 else jnp.concatenate(tables, axis=0)
        tables = [table] + [exchange(table, v << shift) for v in range(1, 1 << step)]
        after.append(tables[-1])
    d_parts = [relayout(integrals, i, after[max(0, i - PARTS + len(rounds))]) for i in range(PARTS)]
    rounds = sum_rounds(bits)
    total, *sends = chi_blocks_of(
        ids[0], place[0], tables, integrals, d_parts, orb * CB_DEV, (1 << rounds[0][1]) - 1
    )
    for k, (shift, step) in enumerate(rounds):
        if k:
            rest = total.shape[0] >> step
            sends = [total[v * rest:(v + 1) * rest].astype(jnp.bfloat16) for v in range(1, 1 << step)]
            total = total[:rest]
        for v, send in enumerate(sends):
            total = total + exchange(send, (v + 1) << shift).astype(jnp.float32)
    total = total.reshape(CB_DEV // 2, bs, 2, bs).transpose(0, 2, 1, 3)
    return total.reshape(CB_DEV, bs * bs)


def solution(mesh):
    in_specs = (
        P("orb", None, None, None),
        P(("grp", "orb"), None),
        P(("grp", "orb"), None),
        P("orb", None),
        P("orb"),
        P("orb", None),
    )
    out_specs = P(("grp", "orb"), None)
    return jax.shard_map(
        functools.partial(local, mesh.shape["orb"]), mesh=mesh, in_specs=in_specs, out_specs=out_specs, check_vma=False
    )
```

```python
import functools

import jax
import jax.numpy as jnp
from jax import lax
from jax.experimental import pallas as pl
from jax.experimental.pallas import tpu as pltpu
from jax.sharding import PartitionSpec as P

CB_DEV = 4
LAM = 4
PARTS = 4
GRANT = 8 << 20


def pack_kernel(owner_rounds, table_rounds, me_ref, count_ref, *refs):
    sources, (out_ref, ids_ref, place_ref), (rows_ref, *held, sems) = refs[:4], refs[4:7], refs[7:]
    copies = [pltpu.make_async_copy(src, dst, sems.at[k]) for k, (src, dst) in enumerate(zip(sources, held))]
    for copy in copies:
        copy.start()
    for copy in copies:
        copy.wait()
    pair_ref, tgt_ref, occ_ref, virt_ref = held
    lanes = out_ref.shape[2]
    half = out_ref.shape[1] // 2
    for i in range(half):
        rows_ref[i:i + 1, :] = occ_ref[:, i * lanes:(i + 1) * lanes].astype(jnp.float32)
        rows_ref[half + i:half + i + 1, :] = virt_ref[:, i * lanes:(i + 1) * lanes].astype(jnp.float32)
    bs = lanes // 2
    row = lax.broadcasted_iota(jnp.int32, rows_ref.shape, 0)
    lane = lax.broadcasted_iota(jnp.int32, rows_ref.shape, 1)
    count = count_ref[0]
    valid = (2 * (row % half) + lane // bs < count) & (lane % bs < count)
    out_ref[0] = jnp.where(valid, rows_ref[...], 0.0).astype(jnp.bfloat16)

    me = me_ref[0]
    rel = pair_ref[...] ^ me
    ids, weight = jnp.zeros_like(rel), 1
    for shift, step in table_rounds:
        ids = ids + ((rel >> shift) & ((1 << step) - 1)) * weight
        weight <<= step
    ids_ref[...] = ids

    targets = tgt_ref[...]
    rel = (targets // CB_DEV) ^ me
    place = jnp.zeros_like(targets)
    for shift, step in owner_rounds:
        place = (place << step) | ((rel >> shift) & ((1 << step) - 1))
    place_ref[...] = place * CB_DEV + targets % CB_DEV


def packed(me, basis_count, pair_atoms, chi_target, green_occ, green_virt, bs, bits):
    return pl.pallas_call(
        functools.partial(pack_kernel, sum_rounds(bits), gather_rounds(bits)),
        in_specs=in_smem(2) + [pl.BlockSpec(memory_space=pl.ANY)] * 4,
        out_specs=in_vmem(3),
        out_shape=[
            jax.ShapeDtypeStruct((1, bs, 2 * bs), jnp.bfloat16),
            jax.ShapeDtypeStruct(pair_atoms.shape, jnp.int32),
            jax.ShapeDtypeStruct(chi_target.shape, jnp.int32),
        ],
        scratch_shapes=[pltpu.VMEM((bs, 2 * bs), jnp.float32)]
        + [pltpu.VMEM(x.shape, x.dtype) for x in (pair_atoms, chi_target, green_occ, green_virt)]
        + [pltpu.SemaphoreType.DMA((4,))],
        compiler_params=pltpu.CompilerParams(vmem_limit_bytes=60 << 20),
    )(me, basis_count, pair_atoms, chi_target, green_occ, green_virt)


def relayout_kernel(part, b_hbm, *refs):
    d_ref, b_ref, sems = refs[-3:]
    lams, aux, width = b_ref.shape
    bs = d_ref.shape[0] // aux
    wide = LAM * bs

    def copy(i):
        held = pl.ds(i * LAM, LAM)
        return pltpu.make_async_copy(b_hbm.at[pl.ds(part * lams + i * LAM, LAM)], b_ref.at[held], sems.at[i])

    for i in range(lams // LAM):
        copy(i).start()
    rows = aux * aux
    row = lax.broadcasted_iota(jnp.int32, (rows, rows), 0)
    col = lax.broadcasted_iota(jnp.int32, (rows, rows), 1)
    perm = (col == (row % aux) * aux + row // aux).astype(jnp.bfloat16)

    @pl.loop(0, lams // LAM)
    def _(i):
        copy(i).wait()
        cols = pl.ds(pl.multiple_of(i * wide, wide), wide)
        for blk in range(bs // aux):
            pieces = []
            for p in range(aux):
                at = (blk * aux + p) * bs
                pieces.append(jnp.concatenate([b_ref[i * LAM + k, :, at:at + bs] for k in range(LAM)], axis=-1))
            stacked = jnp.concatenate(pieces, axis=0)
            moved = jnp.dot(perm, stacked, preferred_element_type=jnp.float32).astype(jnp.bfloat16)
            for a in range(aux):
                d_ref[a * bs + blk * aux:a * bs + (blk + 1) * aux, cols] = moved[a * aux:(a + 1) * aux]


def in_vmem(count):
    return [pl.BlockSpec(memory_space=pltpu.VMEM)] * count


def in_smem(count):
    return [pl.BlockSpec(memory_space=pltpu.SMEM)] * count


def relayout(integrals, part, after):
    bs, aux, width = integrals.shape
    lams = bs // PARTS
    hidden = pl.BlockSpec(memory_space=pl.ANY)
    return pl.pallas_call(
        functools.partial(relayout_kernel, part),
        in_specs=[hidden] * (1 + len(after)),
        out_specs=in_vmem(1)[0],
        out_shape=jax.ShapeDtypeStruct((aux * bs, lams * bs), jnp.bfloat16),
        scratch_shapes=[
            pltpu.VMEM((lams, aux, width), integrals.dtype),
            pltpu.SemaphoreType.DMA((lams // LAM,)),
        ],
        compiler_params=pltpu.CompilerParams(vmem_limit_bytes=48 << 20),
        cost_estimate=pl.CostEstimate(
            flops=2 * bs * aux * width * 256 // PARTS,
            bytes_accessed=4 * bs * aux * width // PARTS,
            transcendentals=0,
        ),
    )(integrals, *after)


def spread_rows(block, of_row, count, bs):
    shape = (count, bs // 2)
    pick = of_row(lax.broadcasted_iota(jnp.int32, shape, 0)) // 2 == lax.broadcasted_iota(jnp.int32, shape, 1)
    got = jnp.dot(pick.astype(jnp.bfloat16), block, preferred_element_type=jnp.float32)
    odd = of_row(lax.broadcasted_iota(jnp.int32, (count, bs), 0)) % 2 == 1
    return jnp.where(odd, got[:, bs:], got[:, :bs])


def green_block(tables, slot):
    count = tables[0].shape[0]
    block = tables[0][slot % count].astype(jnp.float32)
    for k in range(1, len(tables)):
        block = jnp.where(slot // count == k, tables[k][slot % count].astype(jnp.float32), block)
    return block.astype(jnp.bfloat16)


def virt_kernel(bs, pieces, ids_ref, *refs):
    tables, d_parts, v_ref = refs[:pieces], refs[pieces:pieces + PARTS], refs[-1]
    wide = LAM * bs
    spread = spread_rows(green_block(tables, ids_ref[1])[bs // 2:], lambda i: i % bs, wide, bs)
    spread = jnp.concatenate([spread] * LAM, axis=1)
    same = (
        lax.broadcasted_iota(jnp.int32, (wide, wide), 0) // bs == lax.broadcasted_iota(jnp.int32, (wide, wide), 1) // bs
    )
    virt_w = jnp.where(same, spread, 0.0).astype(jnp.bfloat16)
    each = d_parts[0].shape[1]
    for part in range(PARTS):
        for at in range(0, each, wide):
            got = jnp.dot(d_parts[part][:, at:at + wide], virt_w, preferred_element_type=jnp.float32)
            v_ref[:, part * each + at:part * each + at + wide] = got.astype(jnp.bfloat16)


def occ_kernel(pieces, ids_ref, *refs):
    tables, (b_hbm, o_ref, b_ref, sems) = refs[:pieces], refs[pieces:]
    bs, aux, width = b_ref.shape
    half = aux // 2
    wide = LAM * bs
    lanes = 2 * bs

    def copy(j):
        cols = pl.ds(pl.multiple_of(j * wide, wide), wide)
        return pltpu.make_async_copy(b_hbm.at[:, :, cols], b_ref.at[:, :, cols], sems.at[j])

    for j in range(width // wide):
        copy(j).start()
    tall = bs * half
    rep_t = (
        lax.broadcasted_iota(jnp.int32, (bs, tall), 1) // half == lax.broadcasted_iota(jnp.int32, (bs, tall), 0)
    ).astype(jnp.bfloat16)
    spread = spread_rows(green_block(tables, ids_ref[0])[:bs // 2], lambda i: i // half, tall, bs).astype(jnp.bfloat16)
    spread = jnp.dot(spread, rep_t, preferred_element_type=jnp.float32)
    same = (
        lax.broadcasted_iota(jnp.int32, (tall, tall), 0) % half
        == lax.broadcasted_iota(jnp.int32, (tall, tall), 1) % half
    )
    occ_w = jnp.where(same, spread, 0.0).astype(jnp.bfloat16)

    low = lax.broadcasted_iota(jnp.int32, (bs // 2, half, lanes), 2) < bs

    @pl.loop(0, width // wide, unroll=2)
    def _(j):
        copy(j).wait()
        cols = pl.ds(pl.multiple_of(j * wide, wide), wide)
        block = b_ref[:, :, cols].astype(jnp.float32)
        for h in range(2):
            side = block[:, h * half:(h + 1) * half, :].reshape(tall, wide).astype(jnp.bfloat16)
            got = jnp.dot(occ_w, side, preferred_element_type=jnp.float32).reshape(bs // 2, 2, half, wide)
            for t in range(wide // lanes):
                even = got[:, 0, :, t * lanes:(t + 1) * lanes]
                odd = got[:, 1, :, t * lanes:(t + 1) * lanes]
                turned = pltpu.roll(jnp.where(low, odd, even), bs, 2)
                tile = jnp.concatenate([jnp.where(low, even, turned), jnp.where(low, turned, odd)], axis=1)
                tile = tile.astype(jnp.bfloat16)
                at = h * tall + (j * (wide // bs) + 2 * t) * half
                for q in range(bs // 2):
                    o_ref[pl.ds(pl.multiple_of(at, aux), aux), q * lanes:(q + 1) * lanes] = tile[q]


def chi_kernel(bs, sends, tgt_ref, o_ref, v_ref, *refs):
    keep_ref, send_refs, refs = refs[0], refs[1:1 + sends], refs[1 + sends:]
    out0, out1, *accs = refs
    low_acc, high_acc = accs[0], accs[-1]
    aux = o_ref.shape[0] // bs
    half = aux // 2
    lanes = 2 * bs
    for ref in accs:
        ref[...] = jnp.zeros_like(ref)
    low = lax.broadcasted_iota(jnp.int32, (bs, lanes), 1) < bs
    shared = len(accs) == 1
    outs = (out0, out1)
    group = 4 * bs

    def scatter(n):
        for a in range(aux):
            for t in range(2):
                value = outs[n % 2][t, pl.ds(a // half * (half * bs) + a % half, bs, stride=half), :]
                first = tgt_ref[a * aux + n * 4 + 2 * t]
                second = tgt_ref[a * aux + n * 4 + 2 * t + 1]
                low_acc[first] += jnp.where(low, value, 0.0) if shared else value
                high_acc[second] += jnp.where(low, 0.0, value) if shared else value

    for n in range(aux // 4):
        if n:
            scatter(n - 1)
        got = lax.dot_general(
            o_ref[...],
            v_ref[n * group:(n + 1) * group, :],
            (((1,), (1,)), ((), ())),
            preferred_element_type=jnp.float32,
        )
        for t in range(2):
            outs[n % 2][t] = got[:, t * lanes:(t + 1) * lanes]
    scatter(aux // 4 - 1)

    pairs = keep_ref.shape[0]

    def joined(i):
        if shared:
            one, two = low_acc[2 * i], low_acc[2 * i + 1]
            return jnp.where(low, one, two) + pltpu.roll(jnp.where(low, two, one), bs, 1)
        left = jnp.where(low, low_acc[2 * i], high_acc[2 * i + 1])
        right = jnp.where(low, low_acc[2 * i + 1], high_acc[2 * i])
        return left + pltpu.roll(right, bs, 1)

    @pl.loop(0, pairs)
    def _(i):
        keep_ref[i] = joined(i)
        for k, send_ref in enumerate(send_refs):
            send_ref[i] = joined((k + 1) * pairs + i).astype(jnp.bfloat16)


def chi_blocks_of(ids, targets, tables, integrals, d_parts, blocks, sends):
    bs, aux, width = integrals.shape
    pairs = blocks // 2 // (sends + 1)
    side = jax.ShapeDtypeStruct((aux * bs, width), jnp.bfloat16)
    params = pltpu.CompilerParams(vmem_limit_bytes=GRANT)
    cost = pl.CostEstimate(flops=2 * (aux * bs) ** 2 * width, bytes_accessed=4 * aux * bs * width, transcendentals=0)
    virt_side = pl.pallas_call(
        functools.partial(virt_kernel, bs, len(tables)),
        in_specs=in_smem(1) + in_vmem(len(tables) + PARTS),
        out_specs=in_vmem(1)[0],
        out_shape=side,
        compiler_params=params,
        cost_estimate=cost,
    )(ids, *tables, *d_parts)
    occ_side = pl.pallas_call(
        functools.partial(occ_kernel, len(tables)),
        in_specs=in_smem(1) + in_vmem(len(tables)) + [pl.BlockSpec(memory_space=pl.ANY)],
        out_specs=in_vmem(1)[0],
        out_shape=side,
        scratch_shapes=[
            pltpu.VMEM(integrals.shape, integrals.dtype),
            pltpu.SemaphoreType.DMA((width // (LAM * bs),)),
        ],
        compiler_params=pltpu.CompilerParams(vmem_limit_bytes=40 << 20),
        cost_estimate=cost,
    )(ids, *tables, integrals)
    accs = 2 if blocks <= 128 else 1
    acc = pltpu.VMEM((blocks, bs, 2 * bs), jnp.float32)
    out = pltpu.VMEM((2, aux * bs, 2 * bs), jnp.float32)
    return pl.pallas_call(
        functools.partial(chi_kernel, bs, sends),
        in_specs=in_smem(1) + in_vmem(2),
        out_specs=in_vmem(1 + sends),
        out_shape=[jax.ShapeDtypeStruct((pairs, bs, 2 * bs), jnp.float32)]
        + [jax.ShapeDtypeStruct((pairs, bs, 2 * bs), jnp.bfloat16)] * sends,
        scratch_shapes=[out, out] + [acc] * accs,
        compiler_params=pltpu.CompilerParams(vmem_limit_bytes=GRANT + 4 * (accs * blocks + 2 * aux * 2) * bs * 2 * bs),
        cost_estimate=cost,
    )(targets, occ_side, virt_side)


def gather_rounds(bits):
    return [(shift, step) for shift, step in reversed(sum_rounds(bits))]


def sum_rounds(bits):
    rounds, at = [], 0
    while at < bits:
        step = 1 if at < 2 else min(2, bits - at)
        rounds.append((at, step))
        at += step
    return rounds


def local(orb, three_centre, green_occ, green_virt, pair_atoms, basis_count, chi_target):
    bs = three_centre.shape[1]
    bits = orb.bit_length() - 1
    me = lax.axis_index("orb")

    def exchange(value, flip):
        return lax.ppermute(value, "orb", [(i, i ^ flip) for i in range(orb)])

    integrals = three_centre[0]
    table, ids, place = packed(
        me[None].astype(jnp.int32), basis_count, pair_atoms, chi_target, green_occ, green_virt, bs, bits
    )
    rounds = gather_rounds(bits)
    tables, d_parts = [table], []
    for k, (shift, step) in enumerate(rounds):
        after = tables[-1:] if k else []
        table = tables[0] if len(tables) == 1 else jnp.concatenate(tables, axis=0)
        if k and len(d_parts) == k:
            table, d_parts[-1] = lax.optimization_barrier((table, d_parts[-1]))
        tables = [table] + [exchange(table, v << shift) for v in range(1, 1 << step)]
        parts = [i for i in range(PARTS) if min(i, len(rounds) - 1) == k]
        d_parts += [relayout(integrals, i, after) for i in parts]
    rounds = sum_rounds(bits)
    total, *sends = chi_blocks_of(
        ids[0], place[0], tables, integrals, d_parts, orb * CB_DEV, (1 << rounds[0][1]) - 1
    )
    for k, (shift, step) in enumerate(rounds):
        if k:
            rest = total.shape[0] >> step
            sends = [total[v * rest:(v + 1) * rest].astype(jnp.bfloat16) for v in range(1, 1 << step)]
            total = total[:rest]
        for v, send in enumerate(sends):
            total = total + exchange(send, (v + 1) << shift).astype(jnp.float32)
    total = total.reshape(CB_DEV // 2, bs, 2, bs).transpose(0, 2, 1, 3)
    return total.reshape(CB_DEV, bs * bs)


def solution(mesh):
    in_specs = (
        P("orb", None, None, None),
        P(("grp", "orb"), None),
        P(("grp", "orb"), None),
        P("orb", None),
        P("orb"),
        P("orb", None),
    )
    out_specs = P(("grp", "orb"), None)
    return jax.shard_map(
        functools.partial(local, mesh.shape["orb"]), mesh=mesh, in_specs=in_specs, out_specs=out_specs, check_vma=False
    )
```

```python
import functools

import jax
import jax.numpy as jnp
from jax import lax
from jax.experimental import pallas as pl
from jax.experimental.pallas import tpu as pltpu
from jax.sharding import PartitionSpec as P

CB_DEV = 4
LAM = 4
PARTS = 4
GRANT = 8 << 20


def pack_kernel(owner_rounds, table_rounds, me_ref, count_ref, *refs):
    sources, (out_ref, ids_ref, place_ref), (rows_ref, *held, sems) = refs[:4], refs[4:7], refs[7:]
    copies = [pltpu.make_async_copy(src, dst, sems.at[k]) for k, (src, dst) in enumerate(zip(sources, held))]
    for copy in copies:
        copy.start()
    for copy in copies:
        copy.wait()
    pair_ref, tgt_ref, occ_ref, virt_ref = held
    lanes = out_ref.shape[2]
    half = out_ref.shape[1] // 2
    for i in range(half):
        rows_ref[i:i + 1, :] = occ_ref[:, i * lanes:(i + 1) * lanes].astype(jnp.float32)
        rows_ref[half + i:half + i + 1, :] = virt_ref[:, i * lanes:(i + 1) * lanes].astype(jnp.float32)
    bs = lanes // 2
    row = lax.broadcasted_iota(jnp.int32, rows_ref.shape, 0)
    lane = lax.broadcasted_iota(jnp.int32, rows_ref.shape, 1)
    count = count_ref[0]
    valid = (2 * (row % half) + lane // bs < count) & (lane % bs < count)
    out_ref[0] = jnp.where(valid, rows_ref[...], 0.0).astype(jnp.bfloat16)

    me = me_ref[0]
    rel = pair_ref[...] ^ me
    ids, weight = jnp.zeros_like(rel), 1
    for shift, step in table_rounds:
        ids = ids + ((rel >> shift) & ((1 << step) - 1)) * weight
        weight <<= step
    ids_ref[...] = ids

    targets = tgt_ref[...]
    rel = (targets // CB_DEV) ^ me
    place = jnp.zeros_like(targets)
    for shift, step in owner_rounds:
        place = (place << step) | ((rel >> shift) & ((1 << step) - 1))
    place_ref[...] = place * CB_DEV + targets % CB_DEV


def packed(me, basis_count, pair_atoms, chi_target, green_occ, green_virt, bs, bits):
    return pl.pallas_call(
        functools.partial(pack_kernel, sum_rounds(bits), gather_rounds(bits)),
        in_specs=in_smem(2) + [pl.BlockSpec(memory_space=pl.ANY)] * 4,
        out_specs=in_vmem(3),
        out_shape=[
            jax.ShapeDtypeStruct((1, bs, 2 * bs), jnp.bfloat16),
            jax.ShapeDtypeStruct(pair_atoms.shape, jnp.int32),
            jax.ShapeDtypeStruct(chi_target.shape, jnp.int32),
        ],
        scratch_shapes=[pltpu.VMEM((bs, 2 * bs), jnp.float32)]
        + [pltpu.VMEM(x.shape, x.dtype) for x in (pair_atoms, chi_target, green_occ, green_virt)]
        + [pltpu.SemaphoreType.DMA((4,))],
        compiler_params=pltpu.CompilerParams(vmem_limit_bytes=60 << 20),
    )(me, basis_count, pair_atoms, chi_target, green_occ, green_virt)


def halves_joined(one, two, low, lanes):
    turned = pltpu.roll(jnp.where(low, two, one), lanes // 2, one.ndim - 1)
    return jnp.where(low, one, turned), jnp.where(low, turned, two)


def relayout_kernel(part, b_hbm, *refs):
    d_ref, b_ref, sems = refs[-3:]
    tiles, lams, aux, lanes = b_ref.shape
    per = aux // 2

    def copy(c):
        held = pl.ds(pl.multiple_of(c * lanes, lanes), lanes)
        return pltpu.make_async_copy(b_hbm.at[pl.ds(part * lams, lams), :, held], b_ref.at[c], sems.at[c])

    for c in range(tiles):
        copy(c).start()
    rows = aux * aux
    row = lax.broadcasted_iota(jnp.int32, (rows, rows), 0)
    col = lax.broadcasted_iota(jnp.int32, (rows, rows), 1)
    perm = (col == (row % aux) * aux + row // aux).astype(jnp.bfloat16)
    low = lax.broadcasted_iota(jnp.int32, (per, aux, lanes), 2) < lanes // 2

    @pl.loop(0, tiles // per)
    def _(blk):
        for c in range(per):
            copy(blk * per + c).wait()
        held = b_ref[pl.ds(blk * per, per)].astype(jnp.float32)
        for i in range(0, lams, LAM):
            columns = []
            for k in range(0, LAM, 2):
                even, odd = halves_joined(held[:, i + k], held[:, i + k + 1], low, lanes)
                columns.append(jnp.stack([even, odd], axis=1).reshape(rows, lanes).astype(jnp.bfloat16))
            moved = jnp.dot(perm, jnp.concatenate(columns, axis=1), preferred_element_type=jnp.float32)
            moved = moved.astype(jnp.bfloat16)
            for a in range(aux):
                for t in range(LAM // 2):
                    d_ref[a * (tiles // per) + blk, i // 2 + t] = moved[
                        a * aux:(a + 1) * aux, t * lanes:(t + 1) * lanes
                    ]


def in_vmem(count):
    return [pl.BlockSpec(memory_space=pltpu.VMEM)] * count


def in_smem(count):
    return [pl.BlockSpec(memory_space=pltpu.SMEM)] * count


def relayout(integrals, part, after):
    bs, aux, width = integrals.shape
    lams = bs // PARTS
    hidden = pl.BlockSpec(memory_space=pl.ANY)
    return pl.pallas_call(
        functools.partial(relayout_kernel, part),
        in_specs=[hidden] * (1 + len(after)),
        out_specs=in_vmem(1)[0],
        out_shape=jax.ShapeDtypeStruct((bs, lams // 2, aux, 2 * bs), jnp.bfloat16),
        scratch_shapes=[
            pltpu.VMEM((bs // 2, lams, aux, 2 * bs), integrals.dtype),
            pltpu.SemaphoreType.DMA((bs // 2,)),
        ],
        compiler_params=pltpu.CompilerParams(vmem_limit_bytes=48 << 20),
        cost_estimate=pl.CostEstimate(
            flops=2 * bs * aux * width * 256 // PARTS,
            bytes_accessed=4 * bs * aux * width // PARTS,
            transcendentals=0,
        ),
    )(integrals, *after)


def spread_rows(block, of_row, count, bs):
    shape = (count, bs // 2)
    pick = of_row(lax.broadcasted_iota(jnp.int32, shape, 0)) // 2 == lax.broadcasted_iota(jnp.int32, shape, 1)
    got = jnp.dot(pick.astype(jnp.bfloat16), block, preferred_element_type=jnp.float32)
    odd = of_row(lax.broadcasted_iota(jnp.int32, (count, bs), 0)) % 2 == 1
    return jnp.where(odd, got[:, bs:], got[:, :bs])


def green_block(tables, slot):
    count = tables[0].shape[0]
    block = tables[0][slot % count].astype(jnp.float32)
    for k in range(1, len(tables)):
        block = jnp.where(slot // count == k, tables[k][slot % count].astype(jnp.float32), block)
    return block.astype(jnp.bfloat16)


def virt_kernel(bs, pieces, ids_ref, *refs):
    tables, d_parts, v_ref = refs[:pieces], refs[pieces:pieces + PARTS], refs[-1]
    wide = LAM * bs
    spread = spread_rows(green_block(tables, ids_ref[1])[bs // 2:], lambda i: i % bs, wide, bs)
    spread = jnp.concatenate([spread] * LAM, axis=1)
    same = (
        lax.broadcasted_iota(jnp.int32, (wide, wide), 0) // bs == lax.broadcasted_iota(jnp.int32, (wide, wide), 1) // bs
    )
    virt_w = jnp.where(same, spread, 0.0).astype(jnp.bfloat16)
    blocks, each, rows, lanes = d_parts[0].shape
    for part in range(PARTS):
        for at in range(0, each, 2):
            block = flat(d_parts[part], slice(None), [at, at + 1])
            got = jnp.dot(block, virt_w, preferred_element_type=jnp.float32).astype(jnp.bfloat16)
            for t in range(2):
                v_ref[:, part * each + at + t] = got[:, t * lanes:(t + 1) * lanes].reshape(blocks, rows, lanes)


def flat(ref, blocks, tiles):
    got = [ref[blocks, t] for t in tiles]
    return jnp.concatenate([x.reshape(x.shape[0] * x.shape[1], x.shape[2]) for x in got], axis=1)


def occ_kernel(pieces, ids_ref, *refs):
    tables, (b_hbm, o_ref, b_ref, sems, *results) = refs[:pieces], refs[pieces:]
    tiles, bs, aux, lanes = b_ref.shape
    half = aux // 2

    def copy(c):
        cols = pl.ds(pl.multiple_of(c * lanes, lanes), lanes)
        return pltpu.make_async_copy(b_hbm.at[:, :, cols], b_ref.at[c], sems.at[c])

    for c in range(tiles):
        copy(c).start()
    tall = bs * half
    rep_t = (
        lax.broadcasted_iota(jnp.int32, (bs, tall), 1) // half == lax.broadcasted_iota(jnp.int32, (bs, tall), 0)
    ).astype(jnp.bfloat16)
    spread = spread_rows(green_block(tables, ids_ref[0])[:bs // 2], lambda i: i // half, tall, bs).astype(jnp.bfloat16)
    spread = jnp.dot(spread, rep_t, preferred_element_type=jnp.float32)
    same = (
        lax.broadcasted_iota(jnp.int32, (tall, tall), 0) % half
        == lax.broadcasted_iota(jnp.int32, (tall, tall), 1) % half
    )
    occ_w = jnp.where(same, spread, 0.0).astype(jnp.bfloat16)
    low = lax.broadcasted_iota(jnp.int32, (bs // 2, half, lanes), 2) < lanes // 2

    def product(j, h):
        sides = []
        for t in range(2):
            block = b_ref[2 * j + t].astype(jnp.float32)[:, h * half:(h + 1) * half]
            sides.append(block.reshape(tall, lanes).astype(jnp.bfloat16))
        results[h][...] = jnp.dot(occ_w, jnp.concatenate(sides, axis=1), preferred_element_type=jnp.float32)

    def placed(j, h):
        for t in range(2):
            got = results[h][:, t * lanes:(t + 1) * lanes].reshape(bs // 2, 2, half, lanes)
            pair = halves_joined(got[:, 0], got[:, 1], low, lanes)
            o_ref[h * tiles + 2 * j + t] = jnp.concatenate(pair, axis=1).astype(jnp.bfloat16)

    def arrived(j):
        for t in range(2):
            copy(2 * j + t).wait()

    arrived(0)
    product(0, 0)
    product(0, 1)
    placed(0, 0)

    @pl.loop(1, tiles // 2)
    def _(j):
        arrived(j)
        placed(j - 1, 1)
        product(j, 0)
        placed(j, 0)
        product(j, 1)

    placed(tiles // 2 - 1, 1)


def chi_kernel(bs, sends, tgt_ref, o_ref, v_ref, *refs):
    keep_ref, send_refs, refs = refs[0], refs[1:1 + sends], refs[1 + sends:]
    out0, out1, *accs = refs
    low_acc, high_acc = accs[0], accs[-1]
    tiles, aux, lanes = o_ref.shape[1:]
    half = aux // 2
    for ref in accs:
        ref[...] = jnp.zeros_like(ref)
    low = lax.broadcasted_iota(jnp.int32, (bs, lanes), 1) < bs
    shared = len(accs) == 1
    outs = (out0, out1)
    group = 4 * bs

    def scatter(n):
        for a in range(aux):
            for t in range(2):
                value = outs[n % 2][t, pl.ds(a // half * (half * bs) + a % half, bs, stride=half), :]
                first = tgt_ref[a * aux + n * 4 + 2 * t]
                second = tgt_ref[a * aux + n * 4 + 2 * t + 1]
                low_acc[first] += jnp.where(low, value, 0.0) if shared else value
                high_acc[second] += jnp.where(low, 0.0, value) if shared else value

    for n in range(aux // 4):
        if n:
            scatter(n - 1)
        got = lax.dot_general(
            flat(o_ref, slice(None), range(tiles)),
            flat(v_ref, slice(n * group // aux, (n + 1) * group // aux), range(tiles)),
            (((1,), (1,)), ((), ())),
            preferred_element_type=jnp.float32,
        )
        for t in range(2):
            outs[n % 2][t] = got[:, t * lanes:(t + 1) * lanes]
    scatter(aux // 4 - 1)

    pairs = keep_ref.shape[0]

    def joined(i):
        if shared:
            one, two = low_acc[2 * i], low_acc[2 * i + 1]
            return jnp.where(low, one, two) + pltpu.roll(jnp.where(low, two, one), bs, 1)
        left = jnp.where(low, low_acc[2 * i], high_acc[2 * i + 1])
        right = jnp.where(low, low_acc[2 * i + 1], high_acc[2 * i])
        return left + pltpu.roll(right, bs, 1)

    @pl.loop(0, pairs)
    def _(i):
        keep_ref[i] = joined(i)
        for k, send_ref in enumerate(send_refs):
            send_ref[i] = joined((k + 1) * pairs + i).astype(jnp.bfloat16)


def chi_blocks_of(ids, targets, tables, integrals, d_parts, blocks, sends):
    bs, aux, width = integrals.shape
    pairs = blocks // 2 // (sends + 1)
    side = jax.ShapeDtypeStruct((bs, bs // 2, aux, 2 * bs), jnp.bfloat16)
    params = pltpu.CompilerParams(vmem_limit_bytes=GRANT)
    cost = pl.CostEstimate(flops=2 * (aux * bs) ** 2 * width, bytes_accessed=4 * aux * bs * width, transcendentals=0)
    virt_side = pl.pallas_call(
        functools.partial(virt_kernel, bs, len(tables)),
        in_specs=in_smem(1) + in_vmem(len(tables) + PARTS),
        out_specs=in_vmem(1)[0],
        out_shape=side,
        compiler_params=params,
        cost_estimate=cost,
    )(ids, *tables, *d_parts)
    occ_side = pl.pallas_call(
        functools.partial(occ_kernel, len(tables)),
        in_specs=in_smem(1) + in_vmem(len(tables)) + [pl.BlockSpec(memory_space=pl.ANY)],
        out_specs=in_vmem(1)[0],
        out_shape=side,
        scratch_shapes=[
            pltpu.VMEM((bs // 2, bs, aux, 2 * bs), integrals.dtype),
            pltpu.SemaphoreType.DMA((bs // 2,)),
        ]
        + [pltpu.VMEM((bs * aux // 2, 4 * bs), jnp.float32)] * 2,
        compiler_params=pltpu.CompilerParams(vmem_limit_bytes=40 << 20),
        cost_estimate=cost,
    )(ids, *tables, integrals)
    accs = 2 if blocks <= 128 else 1
    acc = pltpu.VMEM((blocks, bs, 2 * bs), jnp.float32)
    out = pltpu.VMEM((2, aux * bs, 2 * bs), jnp.float32)
    return pl.pallas_call(
        functools.partial(chi_kernel, bs, sends),
        in_specs=in_smem(1) + in_vmem(2),
        out_specs=in_vmem(1 + sends),
        out_shape=[jax.ShapeDtypeStruct((pairs, bs, 2 * bs), jnp.float32)]
        + [jax.ShapeDtypeStruct((pairs, bs, 2 * bs), jnp.bfloat16)] * sends,
        scratch_shapes=[out, out] + [acc] * accs,
        compiler_params=pltpu.CompilerParams(vmem_limit_bytes=GRANT + 4 * (accs * blocks + 2 * aux * 2) * bs * 2 * bs),
        cost_estimate=cost,
    )(targets, occ_side, virt_side)


def gather_rounds(bits):
    return [(shift, step) for shift, step in reversed(sum_rounds(bits))]


def sum_rounds(bits):
    rounds, at = [], 0
    while at < bits:
        step = 1 if at < 2 else min(2, bits - at)
        rounds.append((at, step))
        at += step
    return rounds


def local(orb, three_centre, green_occ, green_virt, pair_atoms, basis_count, chi_target):
    bs = three_centre.shape[1]
    bits = orb.bit_length() - 1
    me = lax.axis_index("orb")

    def exchange(value, flip):
        return lax.ppermute(value, "orb", [(i, i ^ flip) for i in range(orb)])

    integrals = three_centre[0]
    table, ids, place = packed(
        me[None].astype(jnp.int32), basis_count, pair_atoms, chi_target, green_occ, green_virt, bs, bits
    )
    rounds = gather_rounds(bits)
    tables, d_parts = [table], []
    for k, (shift, step) in enumerate(rounds):
        after = tables[-1:] if k else []
        table = tables[0] if len(tables) == 1 else jnp.concatenate(tables, axis=0)
        if k and len(d_parts) == k:
            table, d_parts[-1] = lax.optimization_barrier((table, d_parts[-1]))
        tables = [table] + [exchange(table, v << shift) for v in range(1, 1 << step)]
        parts = [i for i in range(PARTS) if min(i, len(rounds) - 1) == k]
        d_parts += [relayout(integrals, i, after) for i in parts]
    rounds = sum_rounds(bits)
    total, *sends = chi_blocks_of(
        ids[0], place[0], tables, integrals, d_parts, orb * CB_DEV, (1 << rounds[0][1]) - 1
    )
    for k, (shift, step) in enumerate(rounds):
        if k:
            rest = total.shape[0] >> step
            sends = [total[v * rest:(v + 1) * rest].astype(jnp.bfloat16) for v in range(1, 1 << step)]
            total = total[:rest]
        for v, send in enumerate(sends):
            total = total + exchange(send, (v + 1) << shift).astype(jnp.float32)
    total = total.reshape(CB_DEV // 2, bs, 2, bs).transpose(0, 2, 1, 3)
    return total.reshape(CB_DEV, bs * bs)


def solution(mesh):
    in_specs = (
        P("orb", None, None, None),
        P(("grp", "orb"), None),
        P(("grp", "orb"), None),
        P("orb", None),
        P("orb"),
        P("orb", None),
    )
    out_specs = P(("grp", "orb"), None)
    return jax.shard_map(
        functools.partial(local, mesh.shape["orb"]), mesh=mesh, in_specs=in_specs, out_specs=out_specs, check_vma=False
    )
```

```python
import functools

import jax
import jax.numpy as jnp
from jax import lax
from jax.experimental import pallas as pl
from jax.experimental.pallas import tpu as pltpu
from jax.sharding import PartitionSpec as P

CB_DEV = 4
LAM = 4
PARTS = 4
GRANT = 8 << 20


def pack_kernel(place_rounds, table_rounds, me_ref, count_ref, *refs):
    sources, (out_ref, ids_ref, place_ref), (rows_ref, *held, sems) = refs[:4], refs[4:7], refs[7:]
    copies = [pltpu.make_async_copy(src, dst, sems.at[k]) for k, (src, dst) in enumerate(zip(sources, held))]
    for copy in copies:
        copy.start()
    for copy in copies:
        copy.wait()
    pair_ref, tgt_ref, occ_ref, virt_ref = held
    lanes = out_ref.shape[2]
    half = out_ref.shape[1] // 2
    for i in range(half):
        rows_ref[i:i + 1, :] = occ_ref[:, i * lanes:(i + 1) * lanes].astype(jnp.float32)
        rows_ref[half + i:half + i + 1, :] = virt_ref[:, i * lanes:(i + 1) * lanes].astype(jnp.float32)
    bs = lanes // 2
    row = lax.broadcasted_iota(jnp.int32, rows_ref.shape, 0)
    lane = lax.broadcasted_iota(jnp.int32, rows_ref.shape, 1)
    count = count_ref[0]
    valid = (2 * (row % half) + lane // bs < count) & (lane % bs < count)
    out_ref[0] = jnp.where(valid, rows_ref[...], 0.0).astype(jnp.bfloat16)

    me = me_ref[0]
    rel = pair_ref[...] ^ me
    ids, weight = jnp.zeros_like(rel), 1
    for shift, step in table_rounds:
        ids = ids + ((rel >> shift) & ((1 << step) - 1)) * weight
        weight <<= step
    ids_ref[...] = ids

    targets = tgt_ref[...]
    rel = (targets // CB_DEV) ^ me
    place = jnp.zeros_like(targets)
    for shift, step in place_rounds:
        place = (place << step) | ((rel >> shift) & ((1 << step) - 1))
    place_ref[...] = place * CB_DEV + targets % CB_DEV


def packed(me, basis_count, pair_atoms, chi_target, green_occ, green_virt, bs, bits):
    return pl.pallas_call(
        functools.partial(pack_kernel, owner_rounds(bits), gather_rounds(bits)),
        in_specs=in_smem(2) + [pl.BlockSpec(memory_space=pl.ANY)] * 4,
        out_specs=in_vmem(3),
        out_shape=[
            jax.ShapeDtypeStruct((1, bs, 2 * bs), jnp.bfloat16),
            jax.ShapeDtypeStruct(pair_atoms.shape, jnp.int32),
            jax.ShapeDtypeStruct(chi_target.shape, jnp.int32),
        ],
        scratch_shapes=[pltpu.VMEM((bs, 2 * bs), jnp.float32)]
        + [pltpu.VMEM(x.shape, x.dtype) for x in (pair_atoms, chi_target, green_occ, green_virt)]
        + [pltpu.SemaphoreType.DMA((4,))],
        compiler_params=pltpu.CompilerParams(vmem_limit_bytes=60 << 20),
    )(me, basis_count, pair_atoms, chi_target, green_occ, green_virt)


def halves_joined(one, two, low, lanes):
    turned = pltpu.roll(jnp.where(low, two, one), lanes // 2, one.ndim - 1)
    return jnp.where(low, one, turned), jnp.where(low, turned, two)


def relayout_kernel(part, b_hbm, *refs):
    d_ref, b_ref, sems, *turns = refs[-5:]
    lams, aux, width = b_ref.shape
    lanes = d_ref.shape[3]
    tiles, half, bs = width // lanes, aux // 2, lanes // 2

    def copy(i):
        held = pl.ds(2 * i, 2)
        return pltpu.make_async_copy(b_hbm.at[pl.ds(part * lams + 2 * i, 2)], b_ref.at[held], sems.at[i])

    for i in range(lams // 2):
        copy(i).start()
    low = lax.broadcasted_iota(jnp.int32, (aux, lanes), 1) < bs

    def turned(i, turn):
        for c in range(tiles):
            one, two = [b_ref[2 * i + k, :, c * lanes:(c + 1) * lanes].astype(jnp.float32) for k in range(2)]
            for k, joined in enumerate(halves_joined(one, two, low, lanes)):
                for h in range(2):
                    at = (h * bs + 2 * c + k) * half
                    turn[at:at + half, :] = joined[h * half:(h + 1) * half]
        for a in range(aux):
            rows = turn[pl.ds(a // half * (bs * half) + a % half, bs, stride=half), :].astype(jnp.bfloat16)
            d_ref[a * (bs // aux):(a + 1) * (bs // aux), i] = rows.reshape(bs // aux, aux, lanes)

    @pl.loop(0, lams // 4)
    def _(i):
        for k, turn in enumerate(turns):
            copy(2 * i + k).wait()
        for k, turn in enumerate(turns):
            turned(2 * i + k, turn)


def in_vmem(count):
    return [pl.BlockSpec(memory_space=pltpu.VMEM)] * count


def in_smem(count):
    return [pl.BlockSpec(memory_space=pltpu.SMEM)] * count


def relayout(integrals, part, after):
    bs, aux, width = integrals.shape
    lams = bs // PARTS
    hidden = pl.BlockSpec(memory_space=pl.ANY)
    return pl.pallas_call(
        functools.partial(relayout_kernel, part),
        in_specs=[hidden] * (1 + len(after)),
        out_specs=in_vmem(1)[0],
        out_shape=jax.ShapeDtypeStruct((bs, lams // 2, aux, 2 * bs), jnp.bfloat16),
        scratch_shapes=[
            pltpu.VMEM((lams, aux, width), integrals.dtype),
            pltpu.SemaphoreType.DMA((lams // 2,)),
        ]
        + [pltpu.VMEM((aux * bs, 2 * bs), jnp.float32)] * 2,
        compiler_params=pltpu.CompilerParams(vmem_limit_bytes=48 << 20),
        cost_estimate=pl.CostEstimate(
            flops=2 * bs * aux * width * 256 // PARTS,
            bytes_accessed=4 * bs * aux * width // PARTS,
            transcendentals=0,
        ),
    )(integrals, *after)


def spread_rows(block, of_row, count, bs):
    shape = (count, bs // 2)
    pick = of_row(lax.broadcasted_iota(jnp.int32, shape, 0)) // 2 == lax.broadcasted_iota(jnp.int32, shape, 1)
    got = jnp.dot(pick.astype(jnp.bfloat16), block, preferred_element_type=jnp.float32)
    odd = of_row(lax.broadcasted_iota(jnp.int32, (count, bs), 0)) % 2 == 1
    return jnp.where(odd, got[:, bs:], got[:, :bs])


def green_block(tables, slot):
    count = tables[0].shape[0]
    block = tables[0][slot % count].astype(jnp.float32)
    for k in range(1, len(tables)):
        block = jnp.where(slot // count == k, tables[k][slot % count].astype(jnp.float32), block)
    return block.astype(jnp.bfloat16)


def virt_kernel(bs, pieces, ids_ref, *refs):
    tables, d_parts, v_ref = refs[:pieces], refs[pieces:pieces + PARTS], refs[-1]
    wide = LAM * bs
    spread = spread_rows(green_block(tables, ids_ref[1])[bs // 2:], lambda i: i % bs, wide, bs)
    spread = jnp.concatenate([spread] * LAM, axis=1)
    same = (
        lax.broadcasted_iota(jnp.int32, (wide, wide), 0) // bs == lax.broadcasted_iota(jnp.int32, (wide, wide), 1) // bs
    )
    virt_w = jnp.where(same, spread, 0.0).astype(jnp.bfloat16)
    blocks, each, rows, lanes = d_parts[0].shape
    for part in range(PARTS):
        for at in range(0, each, 2):
            block = flat(d_parts[part], slice(None), [at, at + 1])
            got = jnp.dot(block, virt_w, preferred_element_type=jnp.float32).astype(jnp.bfloat16)
            for t in range(2):
                v_ref[:, part * each + at + t] = got[:, t * lanes:(t + 1) * lanes].reshape(blocks, rows, lanes)


def flat(ref, blocks, tiles):
    got = [ref[blocks, t] for t in tiles]
    return jnp.concatenate([x.reshape(x.shape[0] * x.shape[1], x.shape[2]) for x in got], axis=1)


def occ_kernel(pieces, ids_ref, *refs):
    tables, (b_hbm, o_ref, b_ref, sems, *results) = refs[:pieces], refs[pieces:]
    bs, aux, width = b_ref.shape
    half, lanes = aux // 2, 2 * bs
    tiles = width // lanes

    def columns(j):
        return pl.ds(pl.multiple_of(j * (2 * lanes), 2 * lanes), 2 * lanes)

    def copy(j):
        return pltpu.make_async_copy(b_hbm.at[:, :, columns(j)], b_ref.at[:, :, columns(j)], sems.at[j])

    for j in range(tiles // 2):
        copy(j).start()
    tall = bs * half
    rep_t = (
        lax.broadcasted_iota(jnp.int32, (bs, tall), 1) // half == lax.broadcasted_iota(jnp.int32, (bs, tall), 0)
    ).astype(jnp.bfloat16)
    spread = spread_rows(green_block(tables, ids_ref[0])[:bs // 2], lambda i: i // half, tall, bs).astype(jnp.bfloat16)
    spread = jnp.dot(spread, rep_t, preferred_element_type=jnp.float32)
    same = (
        lax.broadcasted_iota(jnp.int32, (tall, tall), 0) % half
        == lax.broadcasted_iota(jnp.int32, (tall, tall), 1) % half
    )
    occ_w = jnp.where(same, spread, 0.0).astype(jnp.bfloat16)
    low = lax.broadcasted_iota(jnp.int32, (bs // 2, half, lanes), 2) < lanes // 2

    def product(j, h):
        block = b_ref[:, :, columns(j)].astype(jnp.float32)[:, h * half:(h + 1) * half]
        side = block.reshape(tall, 2 * lanes).astype(jnp.bfloat16)
        results[h][...] = jnp.dot(occ_w, side, preferred_element_type=jnp.float32)

    def placed(j, h):
        for t in range(2):
            got = results[h][:, t * lanes:(t + 1) * lanes].reshape(bs // 2, 2, half, lanes)
            pair = halves_joined(got[:, 0], got[:, 1], low, lanes)
            o_ref[h * tiles + 2 * j + t] = jnp.concatenate(pair, axis=1).astype(jnp.bfloat16)

    copy(0).wait()
    product(0, 0)
    product(0, 1)
    placed(0, 0)

    @pl.loop(1, tiles // 2)
    def _(j):
        copy(j).wait()
        placed(j - 1, 1)
        product(j, 0)
        placed(j, 0)
        product(j, 1)

    placed(tiles // 2 - 1, 1)


def chi_kernel(bs, sends, tgt_ref, o_ref, v_ref, *refs):
    keep_ref, send_refs, refs = refs[0], refs[1:1 + sends], refs[1 + sends:]
    out0, out1, *accs = refs
    low_acc, high_acc = accs[0], accs[-1]
    tiles, aux, lanes = o_ref.shape[1:]
    half = aux // 2
    for ref in accs:
        ref[...] = jnp.zeros_like(ref)
    low = lax.broadcasted_iota(jnp.int32, (bs, lanes), 1) < bs
    shared = len(accs) == 1
    outs = (out0, out1)
    group = 4 * bs

    def scatter(n):
        for a in range(aux):
            for t in range(2):
                value = outs[n % 2][t, pl.ds(a // half * (half * bs) + a % half, bs, stride=half), :]
                first = tgt_ref[a * aux + n * 4 + 2 * t]
                second = tgt_ref[a * aux + n * 4 + 2 * t + 1]
                low_acc[first] += jnp.where(low, value, 0.0) if shared else value
                high_acc[second] += jnp.where(low, 0.0, value) if shared else value

    for n in range(aux // 4):
        if n:
            scatter(n - 1)
        got = lax.dot_general(
            flat(o_ref, slice(None), range(tiles)),
            flat(v_ref, slice(n * group // aux, (n + 1) * group // aux), range(tiles)),
            (((1,), (1,)), ((), ())),
            preferred_element_type=jnp.float32,
        )
        for t in range(2):
            outs[n % 2][t] = got[:, t * lanes:(t + 1) * lanes]
    scatter(aux // 4 - 1)

    pairs = keep_ref.shape[0]

    def joined(i):
        if shared:
            one, two = low_acc[2 * i], low_acc[2 * i + 1]
            return jnp.where(low, one, two) + pltpu.roll(jnp.where(low, two, one), bs, 1)
        left = jnp.where(low, low_acc[2 * i], high_acc[2 * i + 1])
        right = jnp.where(low, low_acc[2 * i + 1], high_acc[2 * i])
        return left + pltpu.roll(right, bs, 1)

    @pl.loop(0, pairs)
    def _(i):
        keep_ref[i] = joined(i)
        for k, send_ref in enumerate(send_refs):
            send_ref[i] = joined((k + 1) * pairs + i).astype(jnp.bfloat16)


def chi_blocks_of(ids, targets, tables, integrals, d_parts, blocks, sends):
    bs, aux, width = integrals.shape
    pairs = blocks // 2 // (sends + 1)
    side = jax.ShapeDtypeStruct((bs, bs // 2, aux, 2 * bs), jnp.bfloat16)
    params = pltpu.CompilerParams(vmem_limit_bytes=GRANT)
    cost = pl.CostEstimate(flops=2 * (aux * bs) ** 2 * width, bytes_accessed=4 * aux * bs * width, transcendentals=0)
    virt_side = pl.pallas_call(
        functools.partial(virt_kernel, bs, len(tables)),
        in_specs=in_smem(1) + in_vmem(len(tables) + PARTS),
        out_specs=in_vmem(1)[0],
        out_shape=side,
        compiler_params=params,
        cost_estimate=cost,
    )(ids, *tables, *d_parts)
    occ_side = pl.pallas_call(
        functools.partial(occ_kernel, len(tables)),
        in_specs=in_smem(1) + in_vmem(len(tables)) + [pl.BlockSpec(memory_space=pl.ANY)],
        out_specs=in_vmem(1)[0],
        out_shape=side,
        scratch_shapes=[
            pltpu.VMEM(integrals.shape, integrals.dtype),
            pltpu.SemaphoreType.DMA((bs // 4,)),
        ]
        + [pltpu.VMEM((bs * aux // 2, 4 * bs), jnp.float32)] * 2,
        compiler_params=pltpu.CompilerParams(vmem_limit_bytes=40 << 20),
        cost_estimate=cost,
    )(ids, *tables, integrals)
    accs = 2 if blocks <= 128 else 1
    acc = pltpu.VMEM((blocks, bs, 2 * bs), jnp.float32)
    out = pltpu.VMEM((2, aux * bs, 2 * bs), jnp.float32)
    return pl.pallas_call(
        functools.partial(chi_kernel, bs, sends),
        in_specs=in_smem(1) + in_vmem(2),
        out_specs=in_vmem(1 + sends),
        out_shape=[jax.ShapeDtypeStruct((pairs, bs, 2 * bs), jnp.float32)]
        + [jax.ShapeDtypeStruct((pairs, bs, 2 * bs), jnp.bfloat16)] * sends,
        scratch_shapes=[out, out] + [acc] * accs,
        compiler_params=pltpu.CompilerParams(vmem_limit_bytes=GRANT + 4 * (accs * blocks + 2 * aux * 2) * bs * 2 * bs),
        cost_estimate=cost,
    )(targets, occ_side, virt_side)


def gather_rounds(bits):
    rounds, at = [], 0
    while at < bits:
        step = 1 if at < 2 else min(2, bits - at)
        rounds.append((at, step))
        at += step
    return rounds[::-1]


def owner_rounds(bits):
    return [(bit, 1) for bit in range(bits)]


def local(orb, three_centre, green_occ, green_virt, pair_atoms, basis_count, chi_target):
    bs = three_centre.shape[1]
    bits = orb.bit_length() - 1
    me = lax.axis_index("orb")

    def exchange(value, flip):
        return lax.ppermute(value, "orb", [(i, i ^ flip) for i in range(orb)])

    integrals = three_centre[0]
    table, ids, place = packed(
        me[None].astype(jnp.int32), basis_count, pair_atoms, chi_target, green_occ, green_virt, bs, bits
    )
    rounds = gather_rounds(bits)
    tables, d_parts = [table], []
    for k, (shift, step) in enumerate(rounds):
        after = tables[-1:] if k else []
        table = tables[0] if len(tables) == 1 else jnp.concatenate(tables, axis=0)
        if k and len(d_parts) == k:
            table, d_parts[-1] = lax.optimization_barrier((table, d_parts[-1]))
        tables = [table] + [exchange(table, v << shift) for v in range(1, 1 << step)]
        parts = [i for i in range(PARTS) if min(i, len(rounds) - 1) == k]
        d_parts += [relayout(integrals, i, after) for i in parts]
    total, send = chi_blocks_of(ids[0], place[0], tables, integrals, d_parts, orb * CB_DEV, 1)
    total = total + exchange(send, 1).astype(jnp.float32)
    total = total.reshape([2] * (bits - 1) + [-1, bs, 2 * bs])
    halves = [total[..., :bs // 2, :], total[..., bs // 2:, :]]
    todo = [list(range(1, bits)), list(range(2, bits)) + [1]]
    left = [list(range(1, bits)) for _ in halves]
    for k in range(bits - 1):
        sends, keeps = [], []
        for part, order, axes in zip(halves, todo, left):
            axis = axes.index(order[k])
            axes.remove(order[k])
            keeps.append(lax.index_in_dim(part, 0, axis, keepdims=False))
            sends.append(lax.index_in_dim(part, 1, axis, keepdims=False).astype(jnp.bfloat16))
        came = [exchange(send, 1 << order[k]) for send, order in zip(sends, todo)]
        halves = [keep + got.astype(jnp.float32) for keep, got in zip(keeps, came)]
    total = jnp.concatenate(halves, axis=-2)
    total = total.reshape(CB_DEV // 2, bs, 2, bs).transpose(0, 2, 1, 3)
    return total.reshape(CB_DEV, bs * bs)


def solution(mesh):
    in_specs = (
        P("orb", None, None, None),
        P(("grp", "orb"), None),
        P(("grp", "orb"), None),
        P("orb", None),
        P("orb"),
        P("orb", None),
    )
    out_specs = P(("grp", "orb"), None)
    return jax.shard_map(
        functools.partial(local, mesh.shape["orb"]), mesh=mesh, in_specs=in_specs, out_specs=out_specs, check_vma=False
    )
```

```python
import functools

import jax
import jax.numpy as jnp
from jax import lax
from jax.experimental import pallas as pl
from jax.experimental.pallas import tpu as pltpu
from jax.sharding import PartitionSpec as P

CB_DEV = 4
LAM = 4
PARTS = 4
GRANT = 8 << 20


def pack_kernel(pairs, table_rounds, me_ref, count_ref, *refs):
    sources, (out_ref, ids_ref, place_ref), (rows_ref, *held, sems) = refs[:4], refs[4:7], refs[7:]
    copies = [pltpu.make_async_copy(src, dst, sems.at[k]) for k, (src, dst) in enumerate(zip(sources, held))]
    for copy in copies:
        copy.start()
    for copy in copies:
        copy.wait()
    pair_ref, tgt_ref, occ_ref, virt_ref = held
    lanes = out_ref.shape[2]
    half = out_ref.shape[1] // 2
    for i in range(half):
        rows_ref[i:i + 1, :] = occ_ref[:, i * lanes:(i + 1) * lanes].astype(jnp.float32)
        rows_ref[half + i:half + i + 1, :] = virt_ref[:, i * lanes:(i + 1) * lanes].astype(jnp.float32)
    bs = lanes // 2
    row = lax.broadcasted_iota(jnp.int32, rows_ref.shape, 0)
    lane = lax.broadcasted_iota(jnp.int32, rows_ref.shape, 1)
    count = count_ref[0]
    valid = (2 * (row % half) + lane // bs < count) & (lane % bs < count)
    out_ref[0] = jnp.where(valid, rows_ref[...], 0.0).astype(jnp.bfloat16)

    me = me_ref[0]
    rel = pair_ref[...] ^ me
    ids, weight = jnp.zeros_like(rel), 1
    for shift, step in table_rounds:
        ids = ids + ((rel >> shift) & ((1 << step) - 1)) * weight
        weight <<= step
    ids_ref[...] = ids

    targets = tgt_ref[...]
    owner = targets // CB_DEV
    place = ((owner ^ me) & 1) * pairs + (owner >> 1)
    place_ref[...] = place * CB_DEV + targets % CB_DEV


def packed(me, basis_count, pair_atoms, chi_target, green_occ, green_virt, bs, bits):
    return pl.pallas_call(
        functools.partial(pack_kernel, 1 << (bits - 1), gather_rounds(bits)),
        in_specs=in_smem(2) + [pl.BlockSpec(memory_space=pl.ANY)] * 4,
        out_specs=in_vmem(3),
        out_shape=[
            jax.ShapeDtypeStruct((1, bs, 2 * bs), jnp.bfloat16),
            jax.ShapeDtypeStruct(pair_atoms.shape, jnp.int32),
            jax.ShapeDtypeStruct(chi_target.shape, jnp.int32),
        ],
        scratch_shapes=[pltpu.VMEM((bs, 2 * bs), jnp.float32)]
        + [pltpu.VMEM(x.shape, x.dtype) for x in (pair_atoms, chi_target, green_occ, green_virt)]
        + [pltpu.SemaphoreType.DMA((4,))],
        compiler_params=pltpu.CompilerParams(vmem_limit_bytes=60 << 20),
    )(me, basis_count, pair_atoms, chi_target, green_occ, green_virt)


def halves_joined(one, two, low, lanes):
    turned = pltpu.roll(jnp.where(low, two, one), lanes // 2, one.ndim - 1)
    return jnp.where(low, one, turned), jnp.where(low, turned, two)


def relayout_kernel(part, b_hbm, *refs):
    d_ref, b_ref, sems, *turns = refs[-5:]
    lams, aux, width = b_ref.shape
    lanes = d_ref.shape[3]
    tiles, half, bs = width // lanes, aux // 2, lanes // 2

    def copy(i):
        held = pl.ds(2 * i, 2)
        return pltpu.make_async_copy(b_hbm.at[pl.ds(part * lams + 2 * i, 2)], b_ref.at[held], sems.at[i])

    for i in range(lams // 2):
        copy(i).start()
    low = lax.broadcasted_iota(jnp.int32, (aux, lanes), 1) < bs

    def turned(i, turn):
        for c in range(tiles):
            one, two = [b_ref[2 * i + k, :, c * lanes:(c + 1) * lanes].astype(jnp.float32) for k in range(2)]
            for k, joined in enumerate(halves_joined(one, two, low, lanes)):
                for h in range(2):
                    at = (h * bs + 2 * c + k) * half
                    turn[at:at + half, :] = joined[h * half:(h + 1) * half]
        for a in range(aux):
            rows = turn[pl.ds(a // half * (bs * half) + a % half, bs, stride=half), :].astype(jnp.bfloat16)
            d_ref[a * (bs // aux):(a + 1) * (bs // aux), i] = rows.reshape(bs // aux, aux, lanes)

    @pl.loop(0, lams // 4)
    def _(i):
        for k, turn in enumerate(turns):
            copy(2 * i + k).wait()
        for k, turn in enumerate(turns):
            turned(2 * i + k, turn)


def in_vmem(count):
    return [pl.BlockSpec(memory_space=pltpu.VMEM)] * count


def in_smem(count):
    return [pl.BlockSpec(memory_space=pltpu.SMEM)] * count


def relayout(integrals, part, after):
    bs, aux, width = integrals.shape
    lams = bs // PARTS
    hidden = pl.BlockSpec(memory_space=pl.ANY)
    return pl.pallas_call(
        functools.partial(relayout_kernel, part),
        in_specs=[hidden] * (1 + len(after)),
        out_specs=in_vmem(1)[0],
        out_shape=jax.ShapeDtypeStruct((bs, lams // 2, aux, 2 * bs), jnp.bfloat16),
        scratch_shapes=[
            pltpu.VMEM((lams, aux, width), integrals.dtype),
            pltpu.SemaphoreType.DMA((lams // 2,)),
        ]
        + [pltpu.VMEM((aux * bs, 2 * bs), jnp.float32)] * 2,
        compiler_params=pltpu.CompilerParams(vmem_limit_bytes=48 << 20),
        cost_estimate=pl.CostEstimate(
            flops=2 * bs * aux * width * 256 // PARTS,
            bytes_accessed=4 * bs * aux * width // PARTS,
            transcendentals=0,
        ),
    )(integrals, *after)


def spread_rows(block, of_row, count, bs):
    shape = (count, bs // 2)
    pick = of_row(lax.broadcasted_iota(jnp.int32, shape, 0)) // 2 == lax.broadcasted_iota(jnp.int32, shape, 1)
    got = jnp.dot(pick.astype(jnp.bfloat16), block, preferred_element_type=jnp.float32)
    odd = of_row(lax.broadcasted_iota(jnp.int32, (count, bs), 0)) % 2 == 1
    return jnp.where(odd, got[:, bs:], got[:, :bs])


def green_block(tables, slot):
    count = tables[0].shape[0]
    block = tables[0][slot % count].astype(jnp.float32)
    for k in range(1, len(tables)):
        block = jnp.where(slot // count == k, tables[k][slot % count].astype(jnp.float32), block)
    return block.astype(jnp.bfloat16)


def virt_kernel(bs, pieces, ids_ref, *refs):
    tables, d_parts, v_ref = refs[:pieces], refs[pieces:pieces + PARTS], refs[-1]
    wide = LAM * bs
    spread = spread_rows(green_block(tables, ids_ref[1])[bs // 2:], lambda i: i % bs, wide, bs)
    spread = jnp.concatenate([spread] * LAM, axis=1)
    same = (
        lax.broadcasted_iota(jnp.int32, (wide, wide), 0) // bs == lax.broadcasted_iota(jnp.int32, (wide, wide), 1) // bs
    )
    virt_w = jnp.where(same, spread, 0.0).astype(jnp.bfloat16)
    blocks, each, rows, lanes = d_parts[0].shape
    for part in range(PARTS):
        for at in range(0, each, 2):
            block = flat(d_parts[part], slice(None), [at, at + 1])
            got = jnp.dot(block, virt_w, preferred_element_type=jnp.float32).astype(jnp.bfloat16)
            for t in range(2):
                v_ref[:, part * each + at + t] = got[:, t * lanes:(t + 1) * lanes].reshape(blocks, rows, lanes)


def flat(ref, blocks, tiles):
    got = [ref[blocks, t] for t in tiles]
    return jnp.concatenate([x.reshape(x.shape[0] * x.shape[1], x.shape[2]) for x in got], axis=1)


def occ_kernel(pieces, ids_ref, *refs):
    tables, (b_hbm, o_ref, b_ref, sems, *results) = refs[:pieces], refs[pieces:]
    bs, aux, width = b_ref.shape
    half, lanes = aux // 2, 2 * bs
    tiles = width // lanes

    def columns(j):
        return pl.ds(pl.multiple_of(j * (2 * lanes), 2 * lanes), 2 * lanes)

    def copy(j):
        return pltpu.make_async_copy(b_hbm.at[:, :, columns(j)], b_ref.at[:, :, columns(j)], sems.at[j])

    for j in range(tiles // 2):
        copy(j).start()
    tall = bs * half
    rep_t = (
        lax.broadcasted_iota(jnp.int32, (bs, tall), 1) // half == lax.broadcasted_iota(jnp.int32, (bs, tall), 0)
    ).astype(jnp.bfloat16)
    spread = spread_rows(green_block(tables, ids_ref[0])[:bs // 2], lambda i: i // half, tall, bs).astype(jnp.bfloat16)
    spread = jnp.dot(spread, rep_t, preferred_element_type=jnp.float32)
    same = (
        lax.broadcasted_iota(jnp.int32, (tall, tall), 0) % half
        == lax.broadcasted_iota(jnp.int32, (tall, tall), 1) % half
    )
    occ_w = jnp.where(same, spread, 0.0).astype(jnp.bfloat16)
    low = lax.broadcasted_iota(jnp.int32, (bs // 2, half, lanes), 2) < lanes // 2

    def product(j, h):
        block = b_ref[:, :, columns(j)].astype(jnp.float32)[:, h * half:(h + 1) * half]
        side = block.reshape(tall, 2 * lanes).astype(jnp.bfloat16)
        results[h][...] = jnp.dot(occ_w, side, preferred_element_type=jnp.float32)

    def placed(j, h):
        for t in range(2):
            got = results[h][:, t * lanes:(t + 1) * lanes].reshape(bs // 2, 2, half, lanes)
            pair = halves_joined(got[:, 0], got[:, 1], low, lanes)
            o_ref[h * tiles + 2 * j + t] = jnp.concatenate(pair, axis=1).astype(jnp.bfloat16)

    copy(0).wait()
    product(0, 0)
    product(0, 1)
    placed(0, 0)

    @pl.loop(1, tiles // 2)
    def _(j):
        copy(j).wait()
        placed(j - 1, 1)
        product(j, 0)
        placed(j, 0)
        product(j, 1)

    placed(tiles // 2 - 1, 1)


def chi_kernel(bs, sends, tgt_ref, o_ref, v_ref, *refs):
    keep_ref, send_refs, refs = refs[0], refs[1:1 + sends], refs[1 + sends:]
    out0, out1, *accs = refs
    low_acc, high_acc = accs[0], accs[-1]
    tiles, aux, lanes = o_ref.shape[1:]
    half = aux // 2
    for ref in accs:
        ref[...] = jnp.zeros_like(ref)
    low = lax.broadcasted_iota(jnp.int32, (bs, lanes), 1) < bs
    shared = len(accs) == 1
    outs = (out0, out1)
    group = 4 * bs

    def scatter(n):
        for a in range(aux):
            for t in range(2):
                value = outs[n % 2][t, pl.ds(a // half * (half * bs) + a % half, bs, stride=half), :]
                first = tgt_ref[a * aux + n * 4 + 2 * t]
                second = tgt_ref[a * aux + n * 4 + 2 * t + 1]
                low_acc[first] += jnp.where(low, value, 0.0) if shared else value
                high_acc[second] += jnp.where(low, 0.0, value) if shared else value

    for n in range(aux // 4):
        if n:
            scatter(n - 1)
        got = lax.dot_general(
            flat(o_ref, slice(None), range(tiles)),
            flat(v_ref, slice(n * group // aux, (n + 1) * group // aux), range(tiles)),
            (((1,), (1,)), ((), ())),
            preferred_element_type=jnp.float32,
        )
        for t in range(2):
            outs[n % 2][t] = got[:, t * lanes:(t + 1) * lanes]
    scatter(aux // 4 - 1)

    pairs = keep_ref.shape[0]

    def joined(i):
        if shared:
            one, two = low_acc[2 * i], low_acc[2 * i + 1]
            return jnp.where(low, one, two) + pltpu.roll(jnp.where(low, two, one), bs, 1)
        left = jnp.where(low, low_acc[2 * i], high_acc[2 * i + 1])
        right = jnp.where(low, low_acc[2 * i + 1], high_acc[2 * i])
        return left + pltpu.roll(right, bs, 1)

    @pl.loop(0, pairs)
    def _(i):
        keep_ref[i] = joined(i)
        for k, send_ref in enumerate(send_refs):
            send_ref[i] = joined((k + 1) * pairs + i).astype(jnp.bfloat16)


def chi_blocks_of(ids, targets, tables, integrals, d_parts, blocks, sends):
    bs, aux, width = integrals.shape
    pairs = blocks // 2 // (sends + 1)
    side = jax.ShapeDtypeStruct((bs, bs // 2, aux, 2 * bs), jnp.bfloat16)
    params = pltpu.CompilerParams(vmem_limit_bytes=GRANT)
    cost = pl.CostEstimate(flops=2 * (aux * bs) ** 2 * width, bytes_accessed=4 * aux * bs * width, transcendentals=0)
    virt_side = pl.pallas_call(
        functools.partial(virt_kernel, bs, len(tables)),
        in_specs=in_smem(1) + in_vmem(len(tables) + PARTS),
        out_specs=in_vmem(1)[0],
        out_shape=side,
        compiler_params=params,
        cost_estimate=cost,
    )(ids, *tables, *d_parts)
    occ_side = pl.pallas_call(
        functools.partial(occ_kernel, len(tables)),
        in_specs=in_smem(1) + in_vmem(len(tables)) + [pl.BlockSpec(memory_space=pl.ANY)],
        out_specs=in_vmem(1)[0],
        out_shape=side,
        scratch_shapes=[
            pltpu.VMEM(integrals.shape, integrals.dtype),
            pltpu.SemaphoreType.DMA((bs // 4,)),
        ]
        + [pltpu.VMEM((bs * aux // 2, 4 * bs), jnp.float32)] * 2,
        compiler_params=pltpu.CompilerParams(vmem_limit_bytes=40 << 20),
        cost_estimate=cost,
    )(ids, *tables, integrals)
    accs = 2 if blocks <= 128 else 1
    acc = pltpu.VMEM((blocks, bs, 2 * bs), jnp.float32)
    out = pltpu.VMEM((2, aux * bs, 2 * bs), jnp.float32)
    return pl.pallas_call(
        functools.partial(chi_kernel, bs, sends),
        in_specs=in_smem(1) + in_vmem(2),
        out_specs=in_vmem(1 + sends),
        out_shape=[jax.ShapeDtypeStruct((pairs, bs, 2 * bs), jnp.float32)]
        + [jax.ShapeDtypeStruct((pairs, bs, 2 * bs), jnp.bfloat16)] * sends,
        scratch_shapes=[out, out] + [acc] * accs,
        compiler_params=pltpu.CompilerParams(vmem_limit_bytes=GRANT + 4 * (accs * blocks + 2 * aux * 2) * bs * 2 * bs),
        cost_estimate=cost,
    )(targets, occ_side, virt_side)


def gather_rounds(bits):
    return [(bit, 1) for bit in reversed(range(bits))]


def local(orb, three_centre, green_occ, green_virt, pair_atoms, basis_count, chi_target):
    bs = three_centre.shape[1]
    bits = orb.bit_length() - 1
    me = lax.axis_index("orb")

    def exchange(value, flip):
        return lax.ppermute(value, "orb", [(i, i ^ flip) for i in range(orb)])

    integrals = three_centre[0]
    table, ids, place = packed(
        me[None].astype(jnp.int32), basis_count, pair_atoms, chi_target, green_occ, green_virt, bs, bits
    )
    rounds = gather_rounds(bits)
    tables, d_parts = [table], []
    for k, (shift, step) in enumerate(rounds):
        after = tables[-1:] if k else []
        table = tables[0] if len(tables) == 1 else jnp.concatenate(tables, axis=0)
        if k and len(d_parts) == k:
            table, d_parts[-1] = lax.optimization_barrier((table, d_parts[-1]))
        tables = [table] + [exchange(table, v << shift) for v in range(1, 1 << step)]
        parts = [i for i in range(PARTS) if min(i, len(rounds) - 1) == k]
        d_parts += [relayout(integrals, i, after) for i in parts]
    total, send = chi_blocks_of(ids[0], place[0], tables, integrals, d_parts, orb * CB_DEV, 1)
    total = total + exchange(send, 1).astype(jnp.float32)
    groups = [list(range(parity, orb, 2)) for parity in range(2)]
    came = lax.all_to_all(
        total.reshape(orb // 2, -1, bs, 2 * bs).astype(jnp.bfloat16), "orb", 0, 0, axis_index_groups=groups, tiled=True
    )
    total = came.astype(jnp.float32).sum(axis=0)
    total = total.reshape(CB_DEV // 2, bs, 2, bs).transpose(0, 2, 1, 3)
    return total.reshape(CB_DEV, bs * bs)


def solution(mesh):
    in_specs = (
        P("orb", None, None, None),
        P(("grp", "orb"), None),
        P(("grp", "orb"), None),
        P("orb", None),
        P("orb"),
        P("orb", None),
    )
    out_specs = P(("grp", "orb"), None)
    return jax.shard_map(
        functools.partial(local, mesh.shape["orb"]), mesh=mesh, in_specs=in_specs, out_specs=out_specs, check_vma=False
    )
```

```python
import functools

import jax
import jax.numpy as jnp
from jax import lax
from jax.experimental import pallas as pl
from jax.experimental.pallas import tpu as pltpu
from jax.sharding import PartitionSpec as P

CB_DEV = 4
LAM = 4
PARTS = 4
GRANT = 8 << 20


def pack_kernel(quarter, table_rounds, me_ref, count_ref, *refs):
    sources, (out_ref, ids_ref, place_ref), (rows_ref, *held, sems) = refs[:4], refs[4:7], refs[7:]
    copies = [pltpu.make_async_copy(src, dst, sems.at[k]) for k, (src, dst) in enumerate(zip(sources, held))]
    for copy in copies:
        copy.start()
    for copy in copies:
        copy.wait()
    pair_ref, tgt_ref, occ_ref, virt_ref = held
    lanes = out_ref.shape[2]
    half = out_ref.shape[1] // 2
    for i in range(half):
        rows_ref[i:i + 1, :] = occ_ref[:, i * lanes:(i + 1) * lanes].astype(jnp.float32)
        rows_ref[half + i:half + i + 1, :] = virt_ref[:, i * lanes:(i + 1) * lanes].astype(jnp.float32)
    bs = lanes // 2
    row = lax.broadcasted_iota(jnp.int32, rows_ref.shape, 0)
    lane = lax.broadcasted_iota(jnp.int32, rows_ref.shape, 1)
    count = count_ref[0]
    valid = (2 * (row % half) + lane // bs < count) & (lane % bs < count)
    out_ref[0] = jnp.where(valid, rows_ref[...], 0.0).astype(jnp.bfloat16)

    me = me_ref[0]
    rel = pair_ref[...] ^ me
    ids, weight = jnp.zeros_like(rel), 1
    for shift, step in table_rounds:
        ids = ids + ((rel >> shift) & ((1 << step) - 1)) * weight
        weight <<= step
    ids_ref[...] = ids

    targets = tgt_ref[...]
    owner = targets // CB_DEV
    rel = owner ^ me
    place = ((rel & 1) * 2 + ((rel >> 1) & 1)) * quarter + (owner >> 2)
    place_ref[...] = place * CB_DEV + targets % CB_DEV


def packed(me, basis_count, pair_atoms, chi_target, green_occ, green_virt, bs, bits):
    return pl.pallas_call(
        functools.partial(pack_kernel, 1 << (bits - 2), gather_rounds(bits)),
        in_specs=in_smem(2) + [pl.BlockSpec(memory_space=pl.ANY)] * 4,
        out_specs=in_vmem(3),
        out_shape=[
            jax.ShapeDtypeStruct((1, bs, 2 * bs), jnp.bfloat16),
            jax.ShapeDtypeStruct(pair_atoms.shape, jnp.int32),
            jax.ShapeDtypeStruct(chi_target.shape, jnp.int32),
        ],
        scratch_shapes=[pltpu.VMEM((bs, 2 * bs), jnp.float32)]
        + [pltpu.VMEM(x.shape, x.dtype) for x in (pair_atoms, chi_target, green_occ, green_virt)]
        + [pltpu.SemaphoreType.DMA((4,))],
        compiler_params=pltpu.CompilerParams(vmem_limit_bytes=60 << 20),
    )(me, basis_count, pair_atoms, chi_target, green_occ, green_virt)


def halves_joined(one, two, low, lanes):
    turned = pltpu.roll(jnp.where(low, two, one), lanes // 2, one.ndim - 1)
    return jnp.where(low, one, turned), jnp.where(low, turned, two)


def relayout_kernel(part, b_hbm, *refs):
    d_ref, b_ref, sems, *turns = refs[-5:]
    lams, aux, width = b_ref.shape
    lanes = d_ref.shape[3]
    tiles, half, bs = width // lanes, aux // 2, lanes // 2

    def copy(i):
        held = pl.ds(2 * i, 2)
        return pltpu.make_async_copy(b_hbm.at[pl.ds(part * lams + 2 * i, 2)], b_ref.at[held], sems.at[i])

    for i in range(lams // 2):
        copy(i).start()
    low = lax.broadcasted_iota(jnp.int32, (aux, lanes), 1) < bs

    def turned(i, turn):
        for c in range(tiles):
            one, two = [b_ref[2 * i + k, :, c * lanes:(c + 1) * lanes].astype(jnp.float32) for k in range(2)]
            for k, joined in enumerate(halves_joined(one, two, low, lanes)):
                for h in range(2):
                    at = (h * bs + 2 * c + k) * half
                    turn[at:at + half, :] = joined[h * half:(h + 1) * half]
        for a in range(aux):
            rows = turn[pl.ds(a // half * (bs * half) + a % half, bs, stride=half), :].astype(jnp.bfloat16)
            d_ref[a * (bs // aux):(a + 1) * (bs // aux), i] = rows.reshape(bs // aux, aux, lanes)

    @pl.loop(0, lams // 4)
    def _(i):
        for k, turn in enumerate(turns):
            copy(2 * i + k).wait()
        for k, turn in enumerate(turns):
            turned(2 * i + k, turn)


def in_vmem(count):
    return [pl.BlockSpec(memory_space=pltpu.VMEM)] * count


def in_smem(count):
    return [pl.BlockSpec(memory_space=pltpu.SMEM)] * count


def relayout(integrals, part, after):
    bs, aux, width = integrals.shape
    lams = bs // PARTS
    hidden = pl.BlockSpec(memory_space=pl.ANY)
    return pl.pallas_call(
        functools.partial(relayout_kernel, part),
        in_specs=[hidden] * (1 + len(after)),
        out_specs=in_vmem(1)[0],
        out_shape=jax.ShapeDtypeStruct((bs, lams // 2, aux, 2 * bs), jnp.bfloat16),
        scratch_shapes=[
            pltpu.VMEM((lams, aux, width), integrals.dtype),
            pltpu.SemaphoreType.DMA((lams // 2,)),
        ]
        + [pltpu.VMEM((aux * bs, 2 * bs), jnp.float32)] * 2,
        compiler_params=pltpu.CompilerParams(vmem_limit_bytes=48 << 20),
        cost_estimate=pl.CostEstimate(
            flops=2 * bs * aux * width * 256 // PARTS,
            bytes_accessed=4 * bs * aux * width // PARTS,
            transcendentals=0,
        ),
    )(integrals, *after)


def spread_rows(block, of_row, count, bs):
    shape = (count, bs // 2)
    pick = of_row(lax.broadcasted_iota(jnp.int32, shape, 0)) // 2 == lax.broadcasted_iota(jnp.int32, shape, 1)
    got = jnp.dot(pick.astype(jnp.bfloat16), block, preferred_element_type=jnp.float32)
    odd = of_row(lax.broadcasted_iota(jnp.int32, (count, bs), 0)) % 2 == 1
    return jnp.where(odd, got[:, bs:], got[:, :bs])


def green_block(tables, slot):
    count = tables[0].shape[0]
    block = tables[0][slot % count].astype(jnp.float32)
    for k in range(1, len(tables)):
        block = jnp.where(slot // count == k, tables[k][slot % count].astype(jnp.float32), block)
    return block.astype(jnp.bfloat16)


def flat(ref, blocks, tiles):
    got = [ref[blocks, t] for t in tiles]
    return jnp.concatenate([x.reshape(x.shape[0] * x.shape[1], x.shape[2]) for x in got], axis=1)


def sides_kernel(pieces, ids_ref, *refs):
    tables, d_parts, refs = refs[:pieces], refs[pieces:pieces + PARTS], refs[pieces + PARTS:]
    b_hbm, v_ref, o_ref, b_ref, sems, *results = refs
    bs, aux, width = b_ref.shape
    half, lanes = aux // 2, 2 * bs
    tiles = width // lanes

    def columns(j):
        return pl.ds(pl.multiple_of(j * (2 * lanes), 2 * lanes), 2 * lanes)

    def copy(j):
        return pltpu.make_async_copy(b_hbm.at[:, :, columns(j)], b_ref.at[:, :, columns(j)], sems.at[j])

    for j in range(tiles // 2):
        copy(j).start()

    wide = LAM * bs
    spread = spread_rows(green_block(tables, ids_ref[1])[bs // 2:], lambda i: i % bs, wide, bs)
    spread = jnp.concatenate([spread] * LAM, axis=1)
    same = (
        lax.broadcasted_iota(jnp.int32, (wide, wide), 0) // bs == lax.broadcasted_iota(jnp.int32, (wide, wide), 1) // bs
    )
    virt_w = jnp.where(same, spread, 0.0).astype(jnp.bfloat16)
    each = d_parts[0].shape[1]
    for part in range(PARTS):
        for at in range(0, each, 2):
            got = jnp.dot(flat(d_parts[part], slice(None), [at, at + 1]), virt_w, preferred_element_type=jnp.float32)
            got = got.astype(jnp.bfloat16)
            for t in range(2):
                v_ref[:, part * each + at + t] = got[:, t * lanes:(t + 1) * lanes].reshape(v_ref.shape[:1] + (aux, lanes))

    tall = bs * half
    rep_t = (
        lax.broadcasted_iota(jnp.int32, (bs, tall), 1) // half == lax.broadcasted_iota(jnp.int32, (bs, tall), 0)
    ).astype(jnp.bfloat16)
    spread = spread_rows(green_block(tables, ids_ref[0])[:bs // 2], lambda i: i // half, tall, bs).astype(jnp.bfloat16)
    spread = jnp.dot(spread, rep_t, preferred_element_type=jnp.float32)
    same = (
        lax.broadcasted_iota(jnp.int32, (tall, tall), 0) % half
        == lax.broadcasted_iota(jnp.int32, (tall, tall), 1) % half
    )
    occ_w = jnp.where(same, spread, 0.0).astype(jnp.bfloat16)
    low = lax.broadcasted_iota(jnp.int32, (bs // 2, half, lanes), 2) < lanes // 2

    def product(j, h):
        block = b_ref[:, :, columns(j)].astype(jnp.float32)[:, h * half:(h + 1) * half]
        side = block.reshape(tall, 2 * lanes).astype(jnp.bfloat16)
        results[h][...] = jnp.dot(occ_w, side, preferred_element_type=jnp.float32)

    def placed(j, h):
        for t in range(2):
            got = results[h][:, t * lanes:(t + 1) * lanes].reshape(bs // 2, 2, half, lanes)
            pair = halves_joined(got[:, 0], got[:, 1], low, lanes)
            o_ref[h * tiles + 2 * j + t] = jnp.concatenate(pair, axis=1).astype(jnp.bfloat16)

    copy(0).wait()
    product(0, 0)
    product(0, 1)
    placed(0, 0)

    @pl.loop(1, tiles // 2)
    def _(j):
        copy(j).wait()
        placed(j - 1, 1)
        product(j, 0)
        placed(j, 0)
        product(j, 1)

    placed(tiles // 2 - 1, 1)


def chi_kernel(bs, sends, tgt_ref, o_ref, v_ref, *refs):
    keep_ref, send_refs, refs = refs[0], refs[1:1 + sends], refs[1 + sends:]
    out0, out1, *accs = refs
    low_acc, high_acc = accs[0], accs[-1]
    tiles, aux, lanes = o_ref.shape[1:]
    half = aux // 2
    for ref in accs:
        ref[...] = jnp.zeros_like(ref)
    low = lax.broadcasted_iota(jnp.int32, (bs, lanes), 1) < bs
    shared = len(accs) == 1
    outs = (out0, out1)
    group = 4 * bs

    def scatter(n):
        for a in range(aux):
            for t in range(2):
                value = outs[n % 2][t, pl.ds(a // half * (half * bs) + a % half, bs, stride=half), :]
                first = tgt_ref[a * aux + n * 4 + 2 * t]
                second = tgt_ref[a * aux + n * 4 + 2 * t + 1]
                low_acc[first] += jnp.where(low, value, 0.0) if shared else value
                high_acc[second] += jnp.where(low, 0.0, value) if shared else value

    for n in range(aux // 4):
        if n:
            scatter(n - 1)
        got = lax.dot_general(
            flat(o_ref, slice(None), range(tiles)),
            flat(v_ref, slice(n * group // aux, (n + 1) * group // aux), range(tiles)),
            (((1,), (1,)), ((), ())),
            preferred_element_type=jnp.float32,
        )
        for t in range(2):
            outs[n % 2][t] = got[:, t * lanes:(t + 1) * lanes]
    scatter(aux // 4 - 1)

    pairs = keep_ref.shape[0]

    def joined(i):
        if shared:
            one, two = low_acc[2 * i], low_acc[2 * i + 1]
            return jnp.where(low, one, two) + pltpu.roll(jnp.where(low, two, one), bs, 1)
        left = jnp.where(low, low_acc[2 * i], high_acc[2 * i + 1])
        right = jnp.where(low, low_acc[2 * i + 1], high_acc[2 * i])
        return left + pltpu.roll(right, bs, 1)

    @pl.loop(0, pairs)
    def _(i):
        keep_ref[i] = joined(i)
        for k, send_ref in enumerate(send_refs):
            send_ref[i] = joined((k + 1) * pairs + i).astype(jnp.bfloat16)


def chi_blocks_of(ids, targets, tables, integrals, d_parts, blocks, sends):
    bs, aux, width = integrals.shape
    pairs = blocks // 2 // (sends + 1)
    side = jax.ShapeDtypeStruct((bs, bs // 2, aux, 2 * bs), jnp.bfloat16)
    cost = pl.CostEstimate(flops=2 * (aux * bs) ** 2 * width, bytes_accessed=4 * aux * bs * width, transcendentals=0)
    virt_side, occ_side = pl.pallas_call(
        functools.partial(sides_kernel, len(tables)),
        in_specs=in_smem(1) + in_vmem(len(tables) + PARTS) + [pl.BlockSpec(memory_space=pl.ANY)],
        out_specs=in_vmem(2),
        out_shape=[side, side],
        scratch_shapes=[
            pltpu.VMEM(integrals.shape, integrals.dtype),
            pltpu.SemaphoreType.DMA((bs // 4,)),
        ]
        + [pltpu.VMEM((bs * aux // 2, 4 * bs), jnp.float32)] * 2,
        compiler_params=pltpu.CompilerParams(vmem_limit_bytes=24 << 20),
        cost_estimate=cost,
    )(ids, *tables, *d_parts, integrals)
    accs = 2 if blocks <= 128 else 1
    acc = pltpu.VMEM((blocks, bs, 2 * bs), jnp.float32)
    out = pltpu.VMEM((2, aux * bs, 2 * bs), jnp.float32)
    return pl.pallas_call(
        functools.partial(chi_kernel, bs, sends),
        in_specs=in_smem(1) + in_vmem(2),
        out_specs=in_vmem(1 + sends),
        out_shape=[jax.ShapeDtypeStruct((pairs, bs, 2 * bs), jnp.float32)]
        + [jax.ShapeDtypeStruct((pairs, bs, 2 * bs), jnp.bfloat16)] * sends,
        scratch_shapes=[out, out] + [acc] * accs,
        compiler_params=pltpu.CompilerParams(vmem_limit_bytes=GRANT + 4 * (accs * blocks + 2 * aux * 2) * bs * 2 * bs),
        cost_estimate=cost,
    )(targets, occ_side, virt_side)


def gather_rounds(bits):
    return [(bit, 1) for bit in reversed(range(bits))]


def local(orb, three_centre, green_occ, green_virt, pair_atoms, basis_count, chi_target):
    bs = three_centre.shape[1]
    bits = orb.bit_length() - 1
    me = lax.axis_index("orb")

    def exchange(value, flip):
        return lax.ppermute(value, "orb", [(i, i ^ flip) for i in range(orb)])

    integrals = three_centre[0]
    table, ids, place = packed(
        me[None].astype(jnp.int32), basis_count, pair_atoms, chi_target, green_occ, green_virt, bs, bits
    )
    rounds = gather_rounds(bits)
    tables, d_parts = [table], []
    for k, (shift, step) in enumerate(rounds):
        after = tables[-1:] if k else []
        table = tables[0] if len(tables) == 1 else jnp.concatenate(tables, axis=0)
        if k and len(d_parts) == k:
            table, d_parts[-1] = lax.optimization_barrier((table, d_parts[-1]))
        tables = [table] + [exchange(table, v << shift) for v in range(1, 1 << step)]
        parts = [i for i in range(PARTS) if min(i, len(rounds) - 1) == k]
        d_parts += [relayout(integrals, i, after) for i in parts]
    total, send = chi_blocks_of(ids[0], place[0], tables, integrals, d_parts, orb * CB_DEV, 1)
    total = total + exchange(send, 1).astype(jnp.float32)
    rest = total.shape[0] // 2
    total = total[:rest] + exchange(total[rest:].astype(jnp.bfloat16), 2).astype(jnp.float32)
    groups = [list(range(low, orb, 4)) for low in range(4)]
    came = lax.all_to_all(
        total.reshape(orb // 4, -1, bs, 2 * bs).astype(jnp.bfloat16), "orb", 0, 0, axis_index_groups=groups, tiled=True
    )
    total = came.astype(jnp.float32).sum(axis=0)
    total = total.reshape(CB_DEV // 2, bs, 2, bs).transpose(0, 2, 1, 3)
    return total.reshape(CB_DEV, bs * bs)


def solution(mesh):
    in_specs = (
        P("orb", None, None, None),
        P(("grp", "orb"), None),
        P(("grp", "orb"), None),
        P("orb", None),
        P("orb"),
        P("orb", None),
    )
    out_specs = P(("grp", "orb"), None)
    return jax.shard_map(
        functools.partial(local, mesh.shape["orb"]), mesh=mesh, in_specs=in_specs, out_specs=out_specs, check_vma=False
    )
```

```python
import functools

import jax
import jax.numpy as jnp
from jax import lax
from jax.experimental import pallas as pl
from jax.experimental.pallas import tpu as pltpu
from jax.sharding import PartitionSpec as P

CB_DEV = 4
LAM = 4
GRANT = 8 << 20


def pack_kernel(place_rounds, table_rounds, me_ref, count_ref, *refs):
    sources, (out_ref, ids_ref, place_ref), (rows_ref, *held, sems) = refs[:4], refs[4:7], refs[7:]
    copies = [pltpu.make_async_copy(src, dst, sems.at[k]) for k, (src, dst) in enumerate(zip(sources, held))]
    for copy in copies:
        copy.start()
    for copy in copies:
        copy.wait()
    pair_ref, tgt_ref, occ_ref, virt_ref = held
    lanes = out_ref.shape[2]
    half = out_ref.shape[1] // 2
    for i in range(half):
        rows_ref[i:i + 1, :] = occ_ref[:, i * lanes:(i + 1) * lanes].astype(jnp.float32)
        rows_ref[half + i:half + i + 1, :] = virt_ref[:, i * lanes:(i + 1) * lanes].astype(jnp.float32)
    bs = lanes // 2
    row = lax.broadcasted_iota(jnp.int32, rows_ref.shape, 0)
    lane = lax.broadcasted_iota(jnp.int32, rows_ref.shape, 1)
    count = count_ref[0]
    valid = (2 * (row % half) + lane // bs < count) & (lane % bs < count)
    out_ref[0] = jnp.where(valid, rows_ref[...], 0.0).astype(jnp.bfloat16)

    me = me_ref[0]
    rel = pair_ref[...] ^ me
    ids, weight = jnp.zeros_like(rel), 1
    for shift, step in table_rounds:
        ids = ids + ((rel >> shift) & ((1 << step) - 1)) * weight
        weight <<= step
    ids_ref[...] = ids

    targets = tgt_ref[...]
    rel = (targets // CB_DEV) ^ me
    place = jnp.zeros_like(targets)
    for shift, step in place_rounds:
        place = (place << step) | ((rel >> shift) & ((1 << step) - 1))
    place_ref[...] = place * CB_DEV + targets % CB_DEV


def packed(me, basis_count, pair_atoms, chi_target, green_occ, green_virt, bs, bits):
    return pl.pallas_call(
        functools.partial(pack_kernel, owner_rounds(bits), gather_rounds(bits)),
        in_specs=in_smem(2) + [pl.BlockSpec(memory_space=pl.ANY)] * 4,
        out_specs=in_vmem(3),
        out_shape=[
            jax.ShapeDtypeStruct((1, bs, 2 * bs), jnp.bfloat16),
            jax.ShapeDtypeStruct(pair_atoms.shape, jnp.int32),
            jax.ShapeDtypeStruct(chi_target.shape, jnp.int32),
        ],
        scratch_shapes=[pltpu.VMEM((bs, 2 * bs), jnp.float32)]
        + [pltpu.VMEM(x.shape, x.dtype) for x in (pair_atoms, chi_target, green_occ, green_virt)]
        + [pltpu.SemaphoreType.DMA((4,))],
        compiler_params=pltpu.CompilerParams(vmem_limit_bytes=60 << 20),
    )(me, basis_count, pair_atoms, chi_target, green_occ, green_virt)


def halves_joined(one, two, low, lanes):
    turned = pltpu.roll(jnp.where(low, two, one), lanes // 2, one.ndim - 1)
    return jnp.where(low, one, turned), jnp.where(low, turned, two)


def in_vmem(count):
    return [pl.BlockSpec(memory_space=pltpu.VMEM)] * count


def in_smem(count):
    return [pl.BlockSpec(memory_space=pltpu.SMEM)] * count


def spread_rows(block, of_row, count, bs):
    shape = (count, bs // 2)
    pick = of_row(lax.broadcasted_iota(jnp.int32, shape, 0)) // 2 == lax.broadcasted_iota(jnp.int32, shape, 1)
    got = jnp.dot(pick.astype(jnp.bfloat16), block, preferred_element_type=jnp.float32)
    odd = of_row(lax.broadcasted_iota(jnp.int32, (count, bs), 0)) % 2 == 1
    return jnp.where(odd, got[:, bs:], got[:, :bs])


def green_block(tables, slot):
    count = tables[0].shape[0]
    block = tables[0][slot % count].astype(jnp.float32)
    for k in range(1, len(tables)):
        block = jnp.where(slot // count == k, tables[k][slot % count].astype(jnp.float32), block)
    return block.astype(jnp.bfloat16)


def flat(ref, blocks, tiles):
    got = [ref[blocks, t] for t in tiles]
    return jnp.concatenate([x.reshape(x.shape[0] * x.shape[1], x.shape[2]) for x in got], axis=1)


def sides_kernel(pieces, ids_ref, *refs):
    tables, (b_hbm, v_ref, o_ref, b_ref, sems, virt_res, turn, *occ_res) = refs[:pieces], refs[pieces:]
    bs, aux, width = b_ref.shape
    half, lanes = aux // 2, 2 * bs
    tiles = width // lanes
    wide = LAM * bs
    steps = width // wide
    group = aux // LAM

    def columns(j):
        return pl.ds(pl.multiple_of(j * wide, wide), wide)

    def copy(j):
        return pltpu.make_async_copy(b_hbm.at[:, :, columns(j)], b_ref.at[:, :, columns(j)], sems.at[j])

    for j in range(steps):
        copy(j).start()

    spread = spread_rows(green_block(tables, ids_ref[1])[bs // 2:], lambda i: i % bs, wide, bs)
    spread = jnp.concatenate([spread] * LAM, axis=1)
    same = (
        lax.broadcasted_iota(jnp.int32, (wide, wide), 0) // bs == lax.broadcasted_iota(jnp.int32, (wide, wide), 1) // bs
    )
    virt_w = jnp.where(same, spread, 0.0).astype(jnp.bfloat16)

    tall = bs * half
    rep_t = (
        lax.broadcasted_iota(jnp.int32, (bs, tall), 1) // half == lax.broadcasted_iota(jnp.int32, (bs, tall), 0)
    ).astype(jnp.bfloat16)
    spread = spread_rows(green_block(tables, ids_ref[0])[:bs // 2], lambda i: i // half, tall, bs).astype(jnp.bfloat16)
    spread = jnp.dot(spread, rep_t, preferred_element_type=jnp.float32)
    same = (
        lax.broadcasted_iota(jnp.int32, (tall, tall), 0) % half
        == lax.broadcasted_iota(jnp.int32, (tall, tall), 1) % half
    )
    occ_w = jnp.where(same, spread, 0.0).astype(jnp.bfloat16)
    low = lax.broadcasted_iota(jnp.int32, (bs // 2, half, lanes), 2) < lanes // 2

    def occ_product(j, h):
        block = b_ref[:, :, columns(j)].astype(jnp.float32)[:, h * half:(h + 1) * half]
        side = block.reshape(tall, wide).astype(jnp.bfloat16)
        occ_res[h][...] = jnp.dot(occ_w, side, preferred_element_type=jnp.float32)

    def occ_placed(j, h):
        for t in range(wide // lanes):
            got = occ_res[h][:, t * lanes:(t + 1) * lanes].reshape(bs // 2, 2, half, lanes)
            pair = halves_joined(got[:, 0], got[:, 1], low, lanes)
            o_ref[h * tiles + 2 * j + t] = jnp.concatenate(pair, axis=1).astype(jnp.bfloat16)

    def virt_product(j):
        block = b_ref[:, :, columns(j)].reshape(bs * aux, wide)
        virt_res[...] = jnp.dot(block, virt_w, preferred_element_type=jnp.float32)

    def virt_turned(j):
        for t in range(wide // lanes):
            got = virt_res[:, t * lanes:(t + 1) * lanes].reshape(bs // 2, 2, 2, half, lanes)
            for h in range(2):
                for k, joined in enumerate(halves_joined(got[:, 0, h], got[:, 1, h], low, lanes)):
                    at = ((j % group) * LAM + 2 * t + k) * half
                    turn[j // group % 2, :, h, pl.ds(pl.multiple_of(at, half), half), :] = joined

    def virt_placed(block, tile):
        for a in range(aux):
            rows = turn[block % 2, tile, a // half, pl.ds(a % half, aux, stride=half), :]
            v_ref[a * (bs // aux) + block, tile] = rows.astype(jnp.bfloat16)

    @pl.loop(0, steps)
    def _(j):
        before = jnp.maximum(j - 1, 0)
        block = jnp.maximum(j // group - 1, 0)
        copy(j).wait()
        occ_placed(before, 1)
        occ_product(j, 0)
        virt_turned(before)
        virt_product(j)
        occ_placed(j, 0)
        occ_product(j, 1)
        for tile in range(tiles // group):
            virt_placed(block, (j % group) * (tiles // group) + tile)

    occ_placed(steps - 1, 1)
    virt_turned(steps - 1)
    for tile in range(tiles):
        virt_placed(steps // group - 1, tile)


def chi_kernel(bs, sends, tgt_ref, o_ref, v_ref, *refs):
    keep_ref, send_refs, refs = refs[0], refs[1:1 + sends], refs[1 + sends:]
    out0, out1, *accs = refs
    low_acc, high_acc = accs[0], accs[-1]
    tiles, aux, lanes = o_ref.shape[1:]
    half = aux // 2
    for ref in accs:
        ref[...] = jnp.zeros_like(ref)
    low = lax.broadcasted_iota(jnp.int32, (bs, lanes), 1) < bs
    shared = len(accs) == 1
    outs = (out0, out1)
    group = 4 * bs

    def scatter(n):
        for a in range(aux):
            for t in range(2):
                value = outs[n % 2][t, pl.ds(a // half * (half * bs) + a % half, bs, stride=half), :]
                first = tgt_ref[a * aux + n * 4 + 2 * t]
                second = tgt_ref[a * aux + n * 4 + 2 * t + 1]
                low_acc[first] += jnp.where(low, value, 0.0) if shared else value
                high_acc[second] += jnp.where(low, 0.0, value) if shared else value

    for n in range(aux // 4):
        if n:
            scatter(n - 1)
        got = lax.dot_general(
            flat(o_ref, slice(None), range(tiles)),
            flat(v_ref, slice(n * group // aux, (n + 1) * group // aux), range(tiles)),
            (((1,), (1,)), ((), ())),
            preferred_element_type=jnp.float32,
        )
        for t in range(2):
            outs[n % 2][t] = got[:, t * lanes:(t + 1) * lanes]
    scatter(aux // 4 - 1)

    pairs = keep_ref.shape[0]

    def joined(i):
        if shared:
            one, two = low_acc[2 * i], low_acc[2 * i + 1]
            return jnp.where(low, one, two) + pltpu.roll(jnp.where(low, two, one), bs, 1)
        left = jnp.where(low, low_acc[2 * i], high_acc[2 * i + 1])
        right = jnp.where(low, low_acc[2 * i + 1], high_acc[2 * i])
        return left + pltpu.roll(right, bs, 1)

    @pl.loop(0, pairs)
    def _(i):
        keep_ref[i] = joined(i)
        for k, send_ref in enumerate(send_refs):
            send_ref[i] = joined((k + 1) * pairs + i).astype(jnp.bfloat16)


def chi_blocks_of(ids, targets, tables, integrals, blocks, sends):
    bs, aux, width = integrals.shape
    pairs = blocks // 2 // (sends + 1)
    side = jax.ShapeDtypeStruct((bs, bs // 2, aux, 2 * bs), jnp.bfloat16)
    cost = pl.CostEstimate(flops=2 * (aux * bs) ** 2 * width, bytes_accessed=4 * aux * bs * width, transcendentals=0)
    virt_side, occ_side = pl.pallas_call(
        functools.partial(sides_kernel, len(tables)),
        in_specs=in_smem(1) + in_vmem(len(tables)) + [pl.BlockSpec(memory_space=pl.ANY)],
        out_specs=in_vmem(2),
        out_shape=[side, side],
        scratch_shapes=[
            pltpu.VMEM(integrals.shape, integrals.dtype),
            pltpu.SemaphoreType.DMA((bs // LAM,)),
            pltpu.VMEM((bs * aux, LAM * bs), jnp.float32),
            pltpu.VMEM((2, bs // 2, 2, aux * aux // 2, 2 * bs), jnp.float32),
        ]
        + [pltpu.VMEM((bs * aux // 2, LAM * bs), jnp.float32)] * 2,
        compiler_params=pltpu.CompilerParams(vmem_limit_bytes=32 << 20),
        cost_estimate=cost,
    )(ids, *tables, integrals)
    accs = 2 if blocks <= 128 else 1
    acc = pltpu.VMEM((blocks, bs, 2 * bs), jnp.float32)
    out = pltpu.VMEM((2, aux * bs, 2 * bs), jnp.float32)
    return pl.pallas_call(
        functools.partial(chi_kernel, bs, sends),
        in_specs=in_smem(1) + in_vmem(2),
        out_specs=in_vmem(1 + sends),
        out_shape=[jax.ShapeDtypeStruct((pairs, bs, 2 * bs), jnp.float32)]
        + [jax.ShapeDtypeStruct((pairs, bs, 2 * bs), jnp.bfloat16)] * sends,
        scratch_shapes=[out, out] + [acc] * accs,
        compiler_params=pltpu.CompilerParams(vmem_limit_bytes=GRANT + 4 * (accs * blocks + 2 * aux * 2) * bs * 2 * bs),
        cost_estimate=cost,
    )(targets, occ_side, virt_side)


def gather_rounds(bits):
    return [(bit, 1) for bit in reversed(range(bits))]


def owner_rounds(bits):
    rounds, at = [], 0
    while at < bits:
        step = 1 if at < 2 else min(2, bits - at)
        rounds.append((at, step))
        at += step
    return rounds


def local(orb, three_centre, green_occ, green_virt, pair_atoms, basis_count, chi_target):
    bs = three_centre.shape[1]
    bits = orb.bit_length() - 1
    me = lax.axis_index("orb")

    def exchange(value, flip):
        return lax.ppermute(value, "orb", [(i, i ^ flip) for i in range(orb)])

    integrals = three_centre[0]
    table, ids, place = packed(
        me[None].astype(jnp.int32), basis_count, pair_atoms, chi_target, green_occ, green_virt, bs, bits
    )
    tables = [table]
    for shift, step in gather_rounds(bits):
        table = tables[0] if len(tables) == 1 else jnp.concatenate(tables, axis=0)
        tables = [table] + [exchange(table, v << shift) for v in range(1, 1 << step)]
    total, *sends = chi_blocks_of(ids[0], place[0], tables, integrals, orb * CB_DEV, 1)
    for k, (shift, step) in enumerate(owner_rounds(bits)):
        if k:
            rest = total.shape[0] >> step
            sends = [total[v * rest:(v + 1) * rest].astype(jnp.bfloat16) for v in range(1, 1 << step)]
            total = total[:rest]
        for v, send in enumerate(sends):
            total = total + exchange(send, (v + 1) << shift).astype(jnp.float32)
    total = total.reshape(CB_DEV // 2, bs, 2, bs).transpose(0, 2, 1, 3)
    return total.reshape(CB_DEV, bs * bs)


def solution(mesh):
    in_specs = (
        P("orb", None, None, None),
        P(("grp", "orb"), None),
        P(("grp", "orb"), None),
        P("orb", None),
        P("orb"),
        P("orb", None),
    )
    out_specs = P(("grp", "orb"), None)
    return jax.shard_map(
        functools.partial(local, mesh.shape["orb"]), mesh=mesh, in_specs=in_specs, out_specs=out_specs, check_vma=False
    )
```

```python
import functools

import jax
import jax.numpy as jnp
from jax import lax
from jax.experimental import pallas as pl
from jax.experimental.pallas import tpu as pltpu
from jax.sharding import PartitionSpec as P

CB_DEV = 4
LAM = 4
WIDE = 512
PARTS = 4
GRANT = 3 << 20


def pack_kernel(place_rounds, table_rounds, me_ref, count_ref, *refs):
    sources, (out_ref, ids_ref, place_ref), (rows_ref, *held, sems) = refs[:4], refs[4:7], refs[7:]
    copies = [pltpu.make_async_copy(src, dst, sems.at[k]) for k, (src, dst) in enumerate(zip(sources, held))]
    for copy in copies:
        copy.start()
    for copy in copies:
        copy.wait()
    pair_ref, tgt_ref, occ_ref, virt_ref = held
    lanes = out_ref.shape[2]
    half = out_ref.shape[1] // 2
    for i in range(half):
        rows_ref[i:i + 1, :] = occ_ref[:, i * lanes:(i + 1) * lanes].astype(jnp.float32)
        rows_ref[half + i:half + i + 1, :] = virt_ref[:, i * lanes:(i + 1) * lanes].astype(jnp.float32)
    bs = lanes // 2
    row = lax.broadcasted_iota(jnp.int32, rows_ref.shape, 0)
    lane = lax.broadcasted_iota(jnp.int32, rows_ref.shape, 1)
    count = count_ref[0]
    valid = (2 * (row % half) + lane // bs < count) & (lane % bs < count)
    out_ref[0] = jnp.where(valid, rows_ref[...], 0.0).astype(jnp.bfloat16)

    me = me_ref[0]
    rel = pair_ref[...] ^ me
    ids, weight = jnp.zeros_like(rel), 1
    for shift, step in table_rounds:
        ids = ids + ((rel >> shift) & ((1 << step) - 1)) * weight
        weight <<= step
    ids_ref[...] = ids

    targets = tgt_ref[...]
    rel = (targets // CB_DEV) ^ me
    place = jnp.zeros_like(targets)
    for shift, step in place_rounds:
        place = (place << step) | ((rel >> shift) & ((1 << step) - 1))
    place_ref[...] = place * CB_DEV + targets % CB_DEV


def packed(me, basis_count, pair_atoms, chi_target, green_occ, green_virt, bs, bits):
    return pl.pallas_call(
        functools.partial(pack_kernel, owner_rounds(bits), gather_rounds(bits)),
        in_specs=in_smem(2) + [pl.BlockSpec(memory_space=pl.ANY)] * 4,
        out_specs=in_vmem(3),
        out_shape=[
            jax.ShapeDtypeStruct((1, bs, 2 * bs), jnp.bfloat16),
            jax.ShapeDtypeStruct(pair_atoms.shape, jnp.int32),
            jax.ShapeDtypeStruct(chi_target.shape, jnp.int32),
        ],
        scratch_shapes=[pltpu.VMEM((bs, 2 * bs), jnp.float32)]
        + [pltpu.VMEM(x.shape, x.dtype) for x in (pair_atoms, chi_target, green_occ, green_virt)]
        + [pltpu.SemaphoreType.DMA((4,))],
        compiler_params=pltpu.CompilerParams(vmem_limit_bytes=60 << 20),
    )(me, basis_count, pair_atoms, chi_target, green_occ, green_virt)


def halves_joined(one, two, low, lanes):
    turned = pltpu.roll(jnp.where(low, two, one), lanes // 2, one.ndim - 1)
    return jnp.where(low, one, turned), jnp.where(low, turned, two)


def relayout_kernel(part, b_hbm, *refs):
    d_ref, b_ref, sems, *turns = refs[-5:]
    lams, aux, width = b_ref.shape
    lanes = d_ref.shape[3]
    tiles, half, bs = width // lanes, aux // 2, lanes // 2

    def copy(i):
        held = pl.ds(2 * i, 2)
        return pltpu.make_async_copy(b_hbm.at[pl.ds(part * lams + 2 * i, 2)], b_ref.at[held], sems.at[i])

    for i in range(lams // 2):
        copy(i).start()
    low = lax.broadcasted_iota(jnp.int32, (aux, lanes), 1) < bs

    def turned(i, turn):
        for c in range(tiles):
            one, two = [b_ref[2 * i + k, :, c * lanes:(c + 1) * lanes].astype(jnp.float32) for k in range(2)]
            for k, joined in enumerate(halves_joined(one, two, low, lanes)):
                for h in range(2):
                    at = (h * bs + 2 * c + k) * half
                    turn[at:at + half, :] = joined[h * half:(h + 1) * half]
        for a in range(aux):
            rows = turn[pl.ds(a // half * (bs * half) + a % half, bs, stride=half), :].astype(jnp.bfloat16)
            d_ref[a * (bs // aux):(a + 1) * (bs // aux), i] = rows.reshape(bs // aux, aux, lanes)

    @pl.loop(0, lams // 4)
    def _(i):
        for k, turn in enumerate(turns):
            copy(2 * i + k).wait()
        for k, turn in enumerate(turns):
            turned(2 * i + k, turn)


def in_vmem(count):
    return [pl.BlockSpec(memory_space=pltpu.VMEM)] * count


def in_smem(count):
    return [pl.BlockSpec(memory_space=pltpu.SMEM)] * count


def relayout(integrals, part, after):
    bs, aux, width = integrals.shape
    lams = bs // PARTS
    hidden = pl.BlockSpec(memory_space=pl.ANY)
    return pl.pallas_call(
        functools.partial(relayout_kernel, part),
        in_specs=[hidden] * (1 + len(after)),
        out_specs=in_vmem(1)[0],
        out_shape=jax.ShapeDtypeStruct((bs, lams // 2, aux, 2 * bs), jnp.bfloat16),
        scratch_shapes=[
            pltpu.VMEM((lams, aux, width), integrals.dtype),
            pltpu.SemaphoreType.DMA((lams // 2,)),
        ]
        + [pltpu.VMEM((aux * bs, 2 * bs), jnp.float32)] * 2,
        compiler_params=pltpu.CompilerParams(vmem_limit_bytes=48 << 20),
        cost_estimate=pl.CostEstimate(
            flops=2 * bs * aux * width * 256 // PARTS,
            bytes_accessed=4 * bs * aux * width // PARTS,
            transcendentals=0,
        ),
    )(integrals, *after)


def spread_rows(block, of_row, count, bs):
    shape = (count, bs // 2)
    pick = of_row(lax.broadcasted_iota(jnp.int32, shape, 0)) // 2 == lax.broadcasted_iota(jnp.int32, shape, 1)
    got = jnp.dot(pick.astype(jnp.bfloat16), block, preferred_element_type=jnp.float32)
    odd = of_row(lax.broadcasted_iota(jnp.int32, (count, bs), 0)) % 2 == 1
    return jnp.where(odd, got[:, bs:], got[:, :bs])


def green_block(tables, slot):
    count = tables[0].shape[0]
    block = tables[0][slot % count].astype(jnp.float32)
    for k in range(1, len(tables)):
        block = jnp.where(slot // count == k, tables[k][slot % count].astype(jnp.float32), block)
    return block.astype(jnp.bfloat16)


def flat(ref, blocks, tiles):
    got = [ref[blocks, t] for t in tiles]
    return jnp.concatenate([x.reshape(x.shape[0] * x.shape[1], x.shape[2]) for x in got], axis=1)


def sides_kernel(pieces, ids_ref, *refs):
    tables, d_parts, refs = refs[:pieces], refs[pieces:pieces + PARTS], refs[pieces + PARTS:]
    b_hbm, v_ref, o_ref, b_ref, sems, *results = refs
    bs, aux, width = b_ref.shape
    half, lanes = aux // 2, 2 * bs
    tiles = width // lanes

    per = WIDE // lanes

    def columns(j):
        return pl.ds(pl.multiple_of(j * WIDE, WIDE), WIDE)

    def copy(j):
        return pltpu.make_async_copy(b_hbm.at[:, :, columns(j)], b_ref.at[:, :, columns(j)], sems.at[j])

    for j in range(tiles // per):
        copy(j).start()

    wide = LAM * bs
    spread = spread_rows(green_block(tables, ids_ref[1])[bs // 2:], lambda i: i % bs, wide, bs)
    spread = jnp.concatenate([spread] * LAM, axis=1)
    same = (
        lax.broadcasted_iota(jnp.int32, (wide, wide), 0) // bs == lax.broadcasted_iota(jnp.int32, (wide, wide), 1) // bs
    )
    virt_w = jnp.where(same, spread, 0.0).astype(jnp.bfloat16)
    each = d_parts[0].shape[1]
    for part in range(PARTS):
        for at in range(0, each, 2):
            got = jnp.dot(flat(d_parts[part], slice(None), [at, at + 1]), virt_w, preferred_element_type=jnp.float32)
            got = got.astype(jnp.bfloat16)
            for t in range(2):
                v_ref[:, part * each + at + t] = got[:, t * lanes:(t + 1) * lanes].reshape(v_ref.shape[:1] + (aux, lanes))

    tall = bs * half
    rep_t = (
        lax.broadcasted_iota(jnp.int32, (bs, tall), 1) // half == lax.broadcasted_iota(jnp.int32, (bs, tall), 0)
    ).astype(jnp.bfloat16)
    spread = spread_rows(green_block(tables, ids_ref[0])[:bs // 2], lambda i: i // half, tall, bs).astype(jnp.bfloat16)
    spread = jnp.dot(spread, rep_t, preferred_element_type=jnp.float32)
    same = (
        lax.broadcasted_iota(jnp.int32, (tall, tall), 0) % half
        == lax.broadcasted_iota(jnp.int32, (tall, tall), 1) % half
    )
    occ_w = jnp.where(same, spread, 0.0).astype(jnp.bfloat16)
    low = lax.broadcasted_iota(jnp.int32, (bs // 2, half, lanes), 2) < lanes // 2

    def product(j, h):
        block = b_ref[:, :, columns(j)].astype(jnp.float32)[:, h * half:(h + 1) * half]
        side = block.reshape(tall, WIDE).astype(jnp.bfloat16)
        results[h][...] = jnp.dot(occ_w, side, preferred_element_type=jnp.float32)

    def placed(j, h):
        for t in range(per):
            got = results[h][:, t * lanes:(t + 1) * lanes].reshape(bs // 2, 2, half, lanes)
            pair = halves_joined(got[:, 0], got[:, 1], low, lanes)
            o_ref[h * tiles + per * j + t] = jnp.concatenate(pair, axis=1).astype(jnp.bfloat16)

    copy(0).wait()
    product(0, 0)
    product(0, 1)
    placed(0, 0)

    @pl.loop(1, tiles // per)
    def _(j):
        copy(j).wait()
        placed(j - 1, 1)
        product(j, 0)
        placed(j, 0)
        product(j, 1)

    placed(tiles // per - 1, 1)


def chi_kernel(bs, sends, tgt_ref, o_ref, v_ref, *refs):
    keep_ref, send_refs, refs = refs[0], refs[1:1 + sends], refs[1 + sends:]
    out0, out1, *accs = refs
    low_acc, high_acc = accs[0], accs[-1]
    tiles, aux, lanes = o_ref.shape[1:]
    half = aux // 2
    for ref in accs:
        ref[...] = jnp.zeros_like(ref)
    low = lax.broadcasted_iota(jnp.int32, (bs, lanes), 1) < bs
    shared = len(accs) == 1
    outs = (out0, out1)
    wide = WIDE // lanes

    def scatter(n):
        for a in range(aux):
            for t in range(wide):
                value = outs[n % 2][t, pl.ds(a // half * (half * bs) + a % half, bs, stride=half), :]
                at = a * aux + 2 * (n * wide + t)
                first, second = tgt_ref[at], tgt_ref[at + 1]
                low_acc[first] += jnp.where(low, value, 0.0) if shared else value
                high_acc[second] += jnp.where(low, 0.0, value) if shared else value

    last = aux * bs // WIDE - 1
    for n in range(last + 1):
        if n:
            scatter(n - 1)
        got = lax.dot_general(
            flat(o_ref, slice(None), range(tiles)),
            flat(v_ref, slice(n * WIDE // aux, (n + 1) * WIDE // aux), range(tiles)),
            (((1,), (1,)), ((), ())),
            preferred_element_type=jnp.float32,
        )
        for t in range(wide):
            outs[n % 2][t] = got[:, t * lanes:(t + 1) * lanes]
    scatter(last)

    pairs = keep_ref.shape[0]

    def joined(i):
        if shared:
            one, two = low_acc[2 * i], low_acc[2 * i + 1]
            return jnp.where(low, one, two) + pltpu.roll(jnp.where(low, two, one), bs, 1)
        left = jnp.where(low, low_acc[2 * i], high_acc[2 * i + 1])
        right = jnp.where(low, low_acc[2 * i + 1], high_acc[2 * i])
        return left + pltpu.roll(right, bs, 1)

    @pl.loop(0, pairs)
    def _(i):
        keep_ref[i] = joined(i)
        for k, send_ref in enumerate(send_refs):
            send_ref[i] = joined((k + 1) * pairs + i).astype(jnp.bfloat16)


def chi_blocks_of(ids, targets, tables, integrals, d_parts, blocks, sends):
    bs, aux, width = integrals.shape
    pairs = blocks // 2 // (sends + 1)
    side = jax.ShapeDtypeStruct((bs, bs // 2, aux, 2 * bs), jnp.bfloat16)
    cost = pl.CostEstimate(flops=2 * (aux * bs) ** 2 * width, bytes_accessed=4 * aux * bs * width, transcendentals=0)
    virt_side, occ_side = pl.pallas_call(
        functools.partial(sides_kernel, len(tables)),
        in_specs=in_smem(1) + in_vmem(len(tables) + PARTS) + [pl.BlockSpec(memory_space=pl.ANY)],
        out_specs=in_vmem(2),
        out_shape=[side, side],
        scratch_shapes=[
            pltpu.VMEM(integrals.shape, integrals.dtype),
            pltpu.SemaphoreType.DMA((width // WIDE,)),
        ]
        + [pltpu.VMEM((bs * aux // 2, WIDE), jnp.float32)] * 2,
        compiler_params=pltpu.CompilerParams(vmem_limit_bytes=24 << 20),
        cost_estimate=cost,
    )(ids, *tables, *d_parts, integrals)
    accs = 2 if blocks <= 128 else 1
    acc = pltpu.VMEM((blocks, bs, 2 * bs), jnp.float32)
    out = pltpu.VMEM((WIDE // (2 * bs), aux * bs, 2 * bs), jnp.float32)
    return pl.pallas_call(
        functools.partial(chi_kernel, bs, sends),
        in_specs=in_smem(1) + in_vmem(2),
        out_specs=in_vmem(1 + sends),
        out_shape=[jax.ShapeDtypeStruct((pairs, bs, 2 * bs), jnp.float32)]
        + [jax.ShapeDtypeStruct((pairs, bs, 2 * bs), jnp.bfloat16)] * sends,
        scratch_shapes=[out, out] + [acc] * accs,
        compiler_params=pltpu.CompilerParams(vmem_limit_bytes=GRANT + 4 * (accs * blocks * bs * 2 * bs + 2 * aux * bs * WIDE)),
        cost_estimate=cost,
    )(targets, occ_side, virt_side)


def gather_rounds(bits):
    return [(bit, 1) for bit in reversed(range(bits))]


def owner_rounds(bits):
    rounds, at = [], 0
    while at < bits:
        step = 1 if at < 2 else min(2, bits - at)
        rounds.append((at, step))
        at += step
    return rounds


def local(orb, three_centre, green_occ, green_virt, pair_atoms, basis_count, chi_target):
    bs = three_centre.shape[1]
    bits = orb.bit_length() - 1
    me = lax.axis_index("orb")

    def exchange(value, flip):
        return lax.ppermute(value, "orb", [(i, i ^ flip) for i in range(orb)])

    integrals = three_centre[0]
    table, ids, place = packed(
        me[None].astype(jnp.int32), basis_count, pair_atoms, chi_target, green_occ, green_virt, bs, bits
    )
    rounds = gather_rounds(bits)
    tables, d_parts = [table], []
    for k, (shift, step) in enumerate(rounds):
        after = tables[-1:] if k else []
        table = tables[0] if len(tables) == 1 else jnp.concatenate(tables, axis=0)
        if k and len(d_parts) == k:
            table, d_parts[-1] = lax.optimization_barrier((table, d_parts[-1]))
        tables = [table] + [exchange(table, v << shift) for v in range(1, 1 << step)]
        parts = [i for i in range(PARTS) if min(i, len(rounds) - 1) == k]
        d_parts += [relayout(integrals, i, after) for i in parts]
    total, *sends = chi_blocks_of(ids[0], place[0], tables, integrals, d_parts, orb * CB_DEV, 1)
    for k, (shift, step) in enumerate(owner_rounds(bits)):
        if k:
            rest = total.shape[0] >> step
            sends = [total[v * rest:(v + 1) * rest].astype(jnp.bfloat16) for v in range(1, 1 << step)]
            total = total[:rest]
        for v, send in enumerate(sends):
            total = total + exchange(send, (v + 1) << shift).astype(jnp.float32)
    total = total.reshape(CB_DEV // 2, bs, 2, bs).transpose(0, 2, 1, 3)
    return total.reshape(CB_DEV, bs * bs)


def solution(mesh):
    in_specs = (
        P("orb", None, None, None),
        P(("grp", "orb"), None),
        P(("grp", "orb"), None),
        P("orb", None),
        P("orb"),
        P("orb", None),
    )
    out_specs = P(("grp", "orb"), None)
    return jax.shard_map(
        functools.partial(local, mesh.shape["orb"]), mesh=mesh, in_specs=in_specs, out_specs=out_specs, check_vma=False
    )
```

```python
import functools

import jax
import jax.numpy as jnp
from jax import lax
from jax.experimental import pallas as pl
from jax.experimental.pallas import tpu as pltpu
from jax.sharding import PartitionSpec as P

CB_DEV = 4
LAM = 4
WIDE = 512
PARTS = (32, 16, 16)
GRANT = 3 << 20


def pack_kernel(place_rounds, table_rounds, me_ref, count_ref, *refs):
    sources, (out_ref, ids_ref, place_ref), (rows_ref, *held, sems) = refs[:4], refs[4:7], refs[7:]
    copies = [pltpu.make_async_copy(src, dst, sems.at[k]) for k, (src, dst) in enumerate(zip(sources, held))]
    for copy in copies:
        copy.start()
    for copy in copies:
        copy.wait()
    pair_ref, tgt_ref, occ_ref, virt_ref = held
    lanes = out_ref.shape[2]
    half = out_ref.shape[1] // 2
    for i in range(half):
        rows_ref[i:i + 1, :] = occ_ref[:, i * lanes:(i + 1) * lanes].astype(jnp.float32)
        rows_ref[half + i:half + i + 1, :] = virt_ref[:, i * lanes:(i + 1) * lanes].astype(jnp.float32)
    bs = lanes // 2
    row = lax.broadcasted_iota(jnp.int32, rows_ref.shape, 0)
    lane = lax.broadcasted_iota(jnp.int32, rows_ref.shape, 1)
    count = count_ref[0]
    valid = (2 * (row % half) + lane // bs < count) & (lane % bs < count)
    out_ref[0] = jnp.where(valid, rows_ref[...], 0.0).astype(jnp.bfloat16)

    me = me_ref[0]
    rel = pair_ref[...] ^ me
    ids, weight = jnp.zeros_like(rel), 1
    for shift, step in table_rounds:
        ids = ids + ((rel >> shift) & ((1 << step) - 1)) * weight
        weight <<= step
    ids_ref[...] = ids

    targets = tgt_ref[...]
    rel = (targets // CB_DEV) ^ me
    place = jnp.zeros_like(targets)
    for shift, step in place_rounds:
        place = (place << step) | ((rel >> shift) & ((1 << step) - 1))
    place_ref[...] = place * CB_DEV + targets % CB_DEV


def packed(me, basis_count, pair_atoms, chi_target, green_occ, green_virt, bs, bits):
    return pl.pallas_call(
        functools.partial(pack_kernel, owner_rounds(bits), owner_rounds(bits)[::-1]),
        in_specs=in_smem(2) + [pl.BlockSpec(memory_space=pl.ANY)] * 4,
        out_specs=in_vmem(3),
        out_shape=[
            jax.ShapeDtypeStruct((1, bs, 2 * bs), jnp.bfloat16),
            jax.ShapeDtypeStruct(pair_atoms.shape, jnp.int32),
            jax.ShapeDtypeStruct(chi_target.shape, jnp.int32),
        ],
        scratch_shapes=[pltpu.VMEM((bs, 2 * bs), jnp.float32)]
        + [pltpu.VMEM(x.shape, x.dtype) for x in (pair_atoms, chi_target, green_occ, green_virt)]
        + [pltpu.SemaphoreType.DMA((4,))],
        compiler_params=pltpu.CompilerParams(vmem_limit_bytes=60 << 20),
    )(me, basis_count, pair_atoms, chi_target, green_occ, green_virt)


def halves_joined(one, two, low, lanes):
    turned = pltpu.roll(jnp.where(low, two, one), lanes // 2, one.ndim - 1)
    return jnp.where(low, one, turned), jnp.where(low, turned, two)


def relayout_kernel(first, b_hbm, *refs):
    d_ref, b_ref, sems, *turns = refs[-5:]
    lams, aux, width = b_ref.shape
    lanes = d_ref.shape[3]
    tiles, half, bs = width // lanes, aux // 2, lanes // 2

    def copy(i):
        held = pl.ds(2 * i, 2)
        return pltpu.make_async_copy(b_hbm.at[pl.ds(first + 2 * i, 2)], b_ref.at[held], sems.at[i])

    for i in range(lams // 2):
        copy(i).start()
    low = lax.broadcasted_iota(jnp.int32, (aux, lanes), 1) < bs

    def turned(i, turn):
        for c in range(tiles):
            one, two = [b_ref[2 * i + k, :, c * lanes:(c + 1) * lanes].astype(jnp.float32) for k in range(2)]
            for k, joined in enumerate(halves_joined(one, two, low, lanes)):
                for h in range(2):
                    at = (h * bs + 2 * c + k) * half
                    turn[at:at + half, :] = joined[h * half:(h + 1) * half]
        for a in range(aux):
            rows = turn[pl.ds(a // half * (bs * half) + a % half, bs, stride=half), :].astype(jnp.bfloat16)
            d_ref[a * (bs // aux):(a + 1) * (bs // aux), i] = rows.reshape(bs // aux, aux, lanes)

    @pl.loop(0, lams // 4)
    def _(i):
        for k, turn in enumerate(turns):
            copy(2 * i + k).wait()
        for k, turn in enumerate(turns):
            turned(2 * i + k, turn)


def in_vmem(count):
    return [pl.BlockSpec(memory_space=pltpu.VMEM)] * count


def in_smem(count):
    return [pl.BlockSpec(memory_space=pltpu.SMEM)] * count


def relayout(integrals, part, after):
    bs, aux, width = integrals.shape
    lams = PARTS[part]
    hidden = pl.BlockSpec(memory_space=pl.ANY)
    return pl.pallas_call(
        functools.partial(relayout_kernel, sum(PARTS[:part])),
        in_specs=[hidden] * (1 + len(after)),
        out_specs=in_vmem(1)[0],
        out_shape=jax.ShapeDtypeStruct((bs, lams // 2, aux, 2 * bs), jnp.bfloat16),
        scratch_shapes=[
            pltpu.VMEM((lams, aux, width), integrals.dtype),
            pltpu.SemaphoreType.DMA((lams // 2,)),
        ]
        + [pltpu.VMEM((aux * bs, 2 * bs), jnp.float32)] * 2,
        compiler_params=pltpu.CompilerParams(vmem_limit_bytes=48 << 20),
        cost_estimate=pl.CostEstimate(
            flops=2 * lams * aux * width * 256,
            bytes_accessed=4 * lams * aux * width,
            transcendentals=0,
        ),
    )(integrals, *after)


def spread_rows(block, of_row, count, bs):
    shape = (count, bs // 2)
    pick = of_row(lax.broadcasted_iota(jnp.int32, shape, 0)) // 2 == lax.broadcasted_iota(jnp.int32, shape, 1)
    got = jnp.dot(pick.astype(jnp.bfloat16), block, preferred_element_type=jnp.float32)
    odd = of_row(lax.broadcasted_iota(jnp.int32, (count, bs), 0)) % 2 == 1
    return jnp.where(odd, got[:, bs:], got[:, :bs])


def green_block(tables, slot):
    count = tables[0].shape[0]
    block = tables[0][slot % count].astype(jnp.float32)
    for k in range(1, len(tables)):
        block = jnp.where(slot // count == k, tables[k][slot % count].astype(jnp.float32), block)
    return block.astype(jnp.bfloat16)


def flat(ref, blocks, tiles):
    got = [ref[blocks, t] for t in tiles]
    return jnp.concatenate([x.reshape(x.shape[0] * x.shape[1], x.shape[2]) for x in got], axis=1)


def sides_kernel(pieces, ids_ref, *refs):
    tables, refs = refs[:pieces], refs[pieces:]
    d_parts, refs = refs[:len(PARTS)], refs[len(PARTS):]
    b_hbm, v_ref, o_ref, b_ref, sems, *results = refs
    bs, aux, width = b_ref.shape
    half, lanes = aux // 2, 2 * bs
    tiles = width // lanes

    per = WIDE // lanes

    def columns(j):
        return pl.ds(pl.multiple_of(j * WIDE, WIDE), WIDE)

    def copy(j):
        return pltpu.make_async_copy(b_hbm.at[:, :, columns(j)], b_ref.at[:, :, columns(j)], sems.at[j])

    for j in range(tiles // per):
        copy(j).start()

    wide = LAM * bs
    spread = spread_rows(green_block(tables, ids_ref[1])[bs // 2:], lambda i: i % bs, wide, bs)
    spread = jnp.concatenate([spread] * LAM, axis=1)
    same = (
        lax.broadcasted_iota(jnp.int32, (wide, wide), 0) // bs == lax.broadcasted_iota(jnp.int32, (wide, wide), 1) // bs
    )
    virt_w = jnp.where(same, spread, 0.0).astype(jnp.bfloat16)

    def virt_product(part, before, step):
        got = jnp.dot(flat(d_parts[part], slice(None), [2 * step, 2 * step + 1]), virt_w, preferred_element_type=jnp.float32)
        got = got.astype(jnp.bfloat16)
        for t in range(2):
            v_ref[:, before + 2 * step + t] = got[:, t * lanes:(t + 1) * lanes].reshape(v_ref.shape[:1] + (aux, lanes))

    tall = bs * half
    rep_t = (
        lax.broadcasted_iota(jnp.int32, (bs, tall), 1) // half == lax.broadcasted_iota(jnp.int32, (bs, tall), 0)
    ).astype(jnp.bfloat16)
    spread = spread_rows(green_block(tables, ids_ref[0])[:bs // 2], lambda i: i // half, tall, bs).astype(jnp.bfloat16)
    spread = jnp.dot(spread, rep_t, preferred_element_type=jnp.float32)
    same = (
        lax.broadcasted_iota(jnp.int32, (tall, tall), 0) % half
        == lax.broadcasted_iota(jnp.int32, (tall, tall), 1) % half
    )
    occ_w = jnp.where(same, spread, 0.0).astype(jnp.bfloat16)
    low = lax.broadcasted_iota(jnp.int32, (bs // 2, half, lanes), 2) < lanes // 2

    def product(j, h):
        block = b_ref[:, :, columns(j)].astype(jnp.float32)[:, h * half:(h + 1) * half]
        side = block.reshape(tall, WIDE).astype(jnp.bfloat16)
        results[h][...] = jnp.dot(occ_w, side, preferred_element_type=jnp.float32)

    def placed(j, h):
        for t in range(per):
            got = results[h][:, t * lanes:(t + 1) * lanes].reshape(bs // 2, 2, half, lanes)
            pair = halves_joined(got[:, 0], got[:, 1], low, lanes)
            o_ref[h * tiles + per * j + t] = jnp.concatenate(pair, axis=1).astype(jnp.bfloat16)

    done = 0
    for part, d_ref in enumerate(d_parts):
        steps = d_ref.shape[1] // per

        @pl.loop(0, steps)
        def _(i):
            j = done + i
            copy(j).wait()
            placed(jnp.maximum(j - 1, 0), 1)
            product(j, 0)
            for k in range(per // 2):
                virt_product(part, done * per, i * (per // 2) + k)
            placed(j, 0)
            product(j, 1)

        done += steps

    placed(done - 1, 1)


def chi_kernel(bs, sends, tgt_ref, o_ref, v_ref, *refs):
    keep_ref, send_refs, refs = refs[0], refs[1:1 + sends], refs[1 + sends:]
    out0, out1, *accs = refs
    low_acc, high_acc = accs[0], accs[-1]
    tiles, aux, lanes = o_ref.shape[1:]
    half = aux // 2
    for ref in accs:
        ref[...] = jnp.zeros_like(ref)
    low = lax.broadcasted_iota(jnp.int32, (bs, lanes), 1) < bs
    shared = len(accs) == 1
    outs = (out0, out1)
    columns = [(0, WIDE)] + [(at, WIDE // 2) for at in range(WIDE, aux * bs, WIDE // 2)]

    def scatter(n):
        for a in range(aux):
            for t in range(columns[n][1] // lanes):
                value = outs[n % 2][t, pl.ds(a // half * (half * bs) + a % half, bs, stride=half), :]
                at = a * aux + 2 * (columns[n][0] // lanes + t)
                first, second = tgt_ref[at], tgt_ref[at + 1]
                low_acc[first] += jnp.where(low, value, 0.0) if shared else value
                high_acc[second] += jnp.where(low, 0.0, value) if shared else value

    for n, (at, wide) in enumerate(columns):
        if n:
            scatter(n - 1)
        got = lax.dot_general(
            flat(o_ref, slice(None), range(tiles)),
            flat(v_ref, slice(at // aux, (at + wide) // aux), range(tiles)),
            (((1,), (1,)), ((), ())),
            preferred_element_type=jnp.float32,
        )
        for t in range(wide // lanes):
            outs[n % 2][t] = got[:, t * lanes:(t + 1) * lanes]
    scatter(len(columns) - 1)

    pairs = keep_ref.shape[0]

    def joined(i):
        if shared:
            one, two = low_acc[2 * i], low_acc[2 * i + 1]
            return jnp.where(low, one, two) + pltpu.roll(jnp.where(low, two, one), bs, 1)
        left = jnp.where(low, low_acc[2 * i], high_acc[2 * i + 1])
        right = jnp.where(low, low_acc[2 * i + 1], high_acc[2 * i])
        return left + pltpu.roll(right, bs, 1)

    @pl.loop(0, pairs, unroll=4)
    def _(i):
        keep_ref[i] = joined(i)
        for k, send_ref in enumerate(send_refs):
            send_ref[i] = joined((k + 1) * pairs + i).astype(jnp.bfloat16)


def chi_blocks_of(ids, targets, tables, integrals, d_parts, blocks, sends):
    bs, aux, width = integrals.shape
    pairs = blocks // 2 // (sends + 1)
    side = jax.ShapeDtypeStruct((bs, bs // 2, aux, 2 * bs), jnp.bfloat16)
    cost = pl.CostEstimate(flops=2 * (aux * bs) ** 2 * width, bytes_accessed=4 * aux * bs * width, transcendentals=0)
    virt_side, occ_side = pl.pallas_call(
        functools.partial(sides_kernel, len(tables)),
        in_specs=in_smem(1) + in_vmem(len(tables) + len(PARTS)) + [pl.BlockSpec(memory_space=pl.ANY)],
        out_specs=in_vmem(2),
        out_shape=[side, side],
        scratch_shapes=[
            pltpu.VMEM(integrals.shape, integrals.dtype),
            pltpu.SemaphoreType.DMA((width // WIDE,)),
        ]
        + [pltpu.VMEM((bs * aux // 2, WIDE), jnp.float32)] * 2,
        compiler_params=pltpu.CompilerParams(vmem_limit_bytes=24 << 20),
        cost_estimate=cost,
    )(ids, *tables, *d_parts, integrals)
    accs = 2 if blocks <= 128 else 1
    acc = pltpu.VMEM((blocks, bs, 2 * bs), jnp.float32)
    out = pltpu.VMEM((WIDE // (2 * bs), aux * bs, 2 * bs), jnp.float32)
    return pl.pallas_call(
        functools.partial(chi_kernel, bs, sends),
        in_specs=in_smem(1) + in_vmem(2),
        out_specs=in_vmem(1 + sends),
        out_shape=[jax.ShapeDtypeStruct((pairs, bs, 2 * bs), jnp.float32)]
        + [jax.ShapeDtypeStruct((pairs, bs, 2 * bs), jnp.bfloat16)] * sends,
        scratch_shapes=[out, out] + [acc] * accs,
        compiler_params=pltpu.CompilerParams(vmem_limit_bytes=GRANT + 4 * (accs * blocks * bs * 2 * bs + 2 * aux * bs * WIDE)),
        cost_estimate=cost,
    )(targets, occ_side, virt_side)


def owner_rounds(bits):
    rounds, at = [], 0
    while at < bits:
        step = 1 if at < 2 else min(2, bits - at)
        rounds.append((at, step))
        at += step
    return rounds


def local(orb, three_centre, green_occ, green_virt, pair_atoms, basis_count, chi_target):
    bs = three_centre.shape[1]
    bits = orb.bit_length() - 1
    me = lax.axis_index("orb")

    def exchange(value, flip):
        return lax.ppermute(value, "orb", [(i, i ^ flip) for i in range(orb)])

    integrals = three_centre[0]
    table, ids, place = packed(
        me[None].astype(jnp.int32), basis_count, pair_atoms, chi_target, green_occ, green_virt, bs, bits
    )
    rounds = owner_rounds(bits)[::-1]
    tables, d_parts = [table], []
    for k, (shift, step) in enumerate(rounds):
        after = tables[-1:] if k else []
        table = tables[0] if len(tables) == 1 else jnp.concatenate(tables, axis=0)
        if k and len(d_parts) == k:
            table, d_parts[-1] = lax.optimization_barrier((table, d_parts[-1]))
        tables = [table] + [exchange(table, v << shift) for v in range(1, 1 << step)]
        parts = [i for i in range(len(PARTS)) if min(i, len(rounds) - 1) == k]
        d_parts += [relayout(integrals, i, after) for i in parts]
    total, *sends = chi_blocks_of(ids[0], place[0], tables, integrals, d_parts, orb * CB_DEV, 1)
    for k, (shift, step) in enumerate(owner_rounds(bits)):
        if k:
            rest = total.shape[0] >> step
            sends = [total[v * rest:(v + 1) * rest].astype(jnp.bfloat16) for v in range(1, 1 << step)]
            total = total[:rest]
        for v, send in enumerate(sends):
            total = total + exchange(send, (v + 1) << shift).astype(jnp.float32)
    total = total.reshape(CB_DEV // 2, bs, 2, bs).transpose(0, 2, 1, 3)
    return total.reshape(CB_DEV, bs * bs)


def solution(mesh):
    in_specs = (
        P("orb", None, None, None),
        P(("grp", "orb"), None),
        P(("grp", "orb"), None),
        P("orb", None),
        P("orb"),
        P("orb", None),
    )
    out_specs = P(("grp", "orb"), None)
    return jax.shard_map(
        functools.partial(local, mesh.shape["orb"]), mesh=mesh, in_specs=in_specs, out_specs=out_specs, check_vma=False
    )
```

```python
import functools

import jax
import jax.numpy as jnp
from jax import lax
from jax.experimental import pallas as pl
from jax.experimental.pallas import tpu as pltpu
from jax.sharding import PartitionSpec as P

CB_DEV = 4
LAM = 4
WIDE = 512
PARTS = (40, 16, 8)
GRANT = 3 << 20


def pack_kernel(place_rounds, slot_rounds, me_ref, count_ref, *refs):
    sources, (out_ref, ids_ref, place_ref), (rows_ref, *held, sems) = refs[:4], refs[4:7], refs[7:]
    copies = [pltpu.make_async_copy(src, dst, sems.at[k]) for k, (src, dst) in enumerate(zip(sources, held))]
    for copy in copies:
        copy.start()
    for copy in copies:
        copy.wait()
    pair_ref, tgt_ref, occ_ref, virt_ref = held
    lanes = out_ref.shape[2]
    half = out_ref.shape[1] // 2
    for i in range(half):
        rows_ref[i:i + 1, :] = occ_ref[:, i * lanes:(i + 1) * lanes].astype(jnp.float32)
        rows_ref[half + i:half + i + 1, :] = virt_ref[:, i * lanes:(i + 1) * lanes].astype(jnp.float32)
    bs = lanes // 2
    row = lax.broadcasted_iota(jnp.int32, rows_ref.shape, 0)
    lane = lax.broadcasted_iota(jnp.int32, rows_ref.shape, 1)
    count = count_ref[0]
    valid = (2 * (row % half) + lane // bs < count) & (lane % bs < count)
    out_ref[0] = jnp.where(valid, rows_ref[...], 0.0).astype(jnp.bfloat16)

    me = me_ref[0]
    rel = pair_ref[...] ^ me
    ids, weight = jnp.zeros_like(rel), 1
    for shift, step in slot_rounds:
        ids = ids + ((rel >> shift) & ((1 << step) - 1)) * weight
        weight <<= step
    ids_ref[...] = ids

    targets = tgt_ref[...]
    rel = (targets // CB_DEV) ^ me
    place = jnp.zeros_like(targets)
    for shift, step in place_rounds:
        place = (place << step) | ((rel >> shift) & ((1 << step) - 1))
    place_ref[...] = place * CB_DEV + targets % CB_DEV


def packed(me, basis_count, pair_atoms, chi_target, green_occ, green_virt, bs, bits):
    return pl.pallas_call(
        functools.partial(pack_kernel, owner_rounds(bits), table_rounds(bits)),
        in_specs=in_smem(2) + [pl.BlockSpec(memory_space=pl.ANY)] * 4,
        out_specs=in_vmem(3),
        out_shape=[
            jax.ShapeDtypeStruct((1, bs, 2 * bs), jnp.bfloat16),
            jax.ShapeDtypeStruct(pair_atoms.shape, jnp.int32),
            jax.ShapeDtypeStruct(chi_target.shape, jnp.int32),
        ],
        scratch_shapes=[pltpu.VMEM((bs, 2 * bs), jnp.float32)]
        + [pltpu.VMEM(x.shape, x.dtype) for x in (pair_atoms, chi_target, green_occ, green_virt)]
        + [pltpu.SemaphoreType.DMA((4,))],
        compiler_params=pltpu.CompilerParams(vmem_limit_bytes=60 << 20),
    )(me, basis_count, pair_atoms, chi_target, green_occ, green_virt)


def halves_joined(one, two, low, lanes):
    turned = pltpu.roll(jnp.where(low, two, one), lanes // 2, one.ndim - 1)
    return jnp.where(low, one, turned), jnp.where(low, turned, two)


def relayout_kernel(first, b_hbm, *refs):
    d_ref, b_ref, sems, *turns = refs[-5:]
    lams, aux, width = b_ref.shape
    lanes = d_ref.shape[3]
    tiles, half, bs = width // lanes, aux // 2, lanes // 2

    def copy(i):
        held = pl.ds(2 * i, 2)
        return pltpu.make_async_copy(b_hbm.at[pl.ds(first + 2 * i, 2)], b_ref.at[held], sems.at[i])

    for i in range(lams // 2):
        copy(i).start()
    low = lax.broadcasted_iota(jnp.int32, (aux, lanes), 1) < bs

    def turned(i, turn):
        for c in range(tiles):
            one, two = [b_ref[2 * i + k, :, c * lanes:(c + 1) * lanes].astype(jnp.float32) for k in range(2)]
            for k, joined in enumerate(halves_joined(one, two, low, lanes)):
                for h in range(2):
                    at = (h * bs + 2 * c + k) * half
                    turn[at:at + half, :] = joined[h * half:(h + 1) * half]
        for a in range(aux):
            rows = turn[pl.ds(a // half * (bs * half) + a % half, bs, stride=half), :].astype(jnp.bfloat16)
            d_ref[a * (bs // aux):(a + 1) * (bs // aux), i] = rows.reshape(bs // aux, aux, lanes)

    @pl.loop(0, lams // 4)
    def _(i):
        for k, turn in enumerate(turns):
            copy(2 * i + k).wait()
        for k, turn in enumerate(turns):
            turned(2 * i + k, turn)


def in_vmem(count):
    return [pl.BlockSpec(memory_space=pltpu.VMEM)] * count


def in_smem(count):
    return [pl.BlockSpec(memory_space=pltpu.SMEM)] * count


def relayout(integrals, part, after):
    bs, aux, width = integrals.shape
    lams = PARTS[part]
    hidden = pl.BlockSpec(memory_space=pl.ANY)
    return pl.pallas_call(
        functools.partial(relayout_kernel, sum(PARTS[:part])),
        in_specs=[hidden] * (1 + len(after)),
        out_specs=in_vmem(1)[0],
        out_shape=jax.ShapeDtypeStruct((bs, lams // 2, aux, 2 * bs), jnp.bfloat16),
        scratch_shapes=[
            pltpu.VMEM((lams, aux, width), integrals.dtype),
            pltpu.SemaphoreType.DMA((lams // 2,)),
        ]
        + [pltpu.VMEM((aux * bs, 2 * bs), jnp.float32)] * 2,
        compiler_params=pltpu.CompilerParams(vmem_limit_bytes=48 << 20),
        cost_estimate=pl.CostEstimate(
            flops=2 * lams * aux * width * 256,
            bytes_accessed=4 * lams * aux * width,
            transcendentals=0,
        ),
    )(integrals, *after)


def spread_rows(block, of_row, count, bs):
    shape = (count, bs // 2)
    pick = of_row(lax.broadcasted_iota(jnp.int32, shape, 0)) // 2 == lax.broadcasted_iota(jnp.int32, shape, 1)
    got = jnp.dot(pick.astype(jnp.bfloat16), block, preferred_element_type=jnp.float32)
    odd = of_row(lax.broadcasted_iota(jnp.int32, (count, bs), 0)) % 2 == 1
    return jnp.where(odd, got[:, bs:], got[:, :bs])


def green_block(tables, slot):
    count = tables[0].shape[0]
    block = tables[0][slot % count].astype(jnp.float32)
    for k in range(1, len(tables)):
        block = jnp.where(slot // count == k, tables[k][slot % count].astype(jnp.float32), block)
    return block.astype(jnp.bfloat16)


def flat(ref, blocks, tiles):
    got = [ref[blocks, t] for t in tiles]
    return jnp.concatenate([x.reshape(x.shape[0] * x.shape[1], x.shape[2]) for x in got], axis=1)


def sides_kernel(pieces, ids_ref, *refs):
    tables, refs = refs[:pieces], refs[pieces:]
    d_parts, refs = refs[:len(PARTS)], refs[len(PARTS):]
    b_hbm, v_ref, o_ref, b_ref, sems, *results = refs
    bs, aux, width = b_ref.shape
    half, lanes = aux // 2, 2 * bs
    tiles = width // lanes

    per = WIDE // lanes

    def columns(j):
        return pl.ds(pl.multiple_of(j * WIDE, WIDE), WIDE)

    def copy(j):
        return pltpu.make_async_copy(b_hbm.at[:, :, columns(j)], b_ref.at[:, :, columns(j)], sems.at[j])

    for j in range(tiles // per):
        copy(j).start()

    wide = LAM * bs
    spread = spread_rows(green_block(tables, ids_ref[1])[bs // 2:], lambda i: i % bs, wide, bs)
    spread = jnp.concatenate([spread] * LAM, axis=1)
    same = (
        lax.broadcasted_iota(jnp.int32, (wide, wide), 0) // bs == lax.broadcasted_iota(jnp.int32, (wide, wide), 1) // bs
    )
    virt_w = jnp.where(same, spread, 0.0).astype(jnp.bfloat16)

    def virt_product(part, before, step):
        held = [flat(d_parts[part], slice(None), [per * step + t, per * step + t + 1]) for t in range(0, per, 2)]
        got = jnp.dot(jnp.concatenate(held, axis=0), virt_w, preferred_element_type=jnp.float32).astype(jnp.bfloat16)
        count = held[0].shape[0]
        for t in range(per):
            side = got[t // 2 * count:(t // 2 + 1) * count, t % 2 * lanes:(t % 2 + 1) * lanes]
            v_ref[:, before + per * step + t] = side.reshape(v_ref.shape[:1] + (aux, lanes))

    tall = bs * half
    rep_t = (
        lax.broadcasted_iota(jnp.int32, (bs, tall), 1) // half == lax.broadcasted_iota(jnp.int32, (bs, tall), 0)
    ).astype(jnp.bfloat16)
    spread = spread_rows(green_block(tables, ids_ref[0])[:bs // 2], lambda i: i // half, tall, bs).astype(jnp.bfloat16)
    spread = jnp.dot(spread, rep_t, preferred_element_type=jnp.float32)
    same = (
        lax.broadcasted_iota(jnp.int32, (tall, tall), 0) % half
        == lax.broadcasted_iota(jnp.int32, (tall, tall), 1) % half
    )
    occ_w = jnp.where(same, spread, 0.0).astype(jnp.bfloat16)
    low = lax.broadcasted_iota(jnp.int32, (bs // 2, half, lanes), 2) < lanes // 2

    def product(j, h):
        block = b_ref[:, :, columns(j)].astype(jnp.float32)[:, h * half:(h + 1) * half]
        side = block.reshape(tall, WIDE).astype(jnp.bfloat16)
        results[h][...] = jnp.dot(occ_w, side, preferred_element_type=jnp.float32)

    def placed(j, h):
        for t in range(per):
            got = results[h][:, t * lanes:(t + 1) * lanes].reshape(bs // 2, 2, half, lanes)
            pair = halves_joined(got[:, 0], got[:, 1], low, lanes)
            o_ref[h * tiles + per * j + t] = jnp.concatenate(pair, axis=1).astype(jnp.bfloat16)

    done = 0
    for part, d_ref in enumerate(d_parts):
        steps = d_ref.shape[1] // per

        @pl.loop(0, steps)
        def _(i):
            j = done + i
            copy(j).wait()
            placed(jnp.maximum(j - 1, 0), 1)
            product(j, 0)
            virt_product(part, done * per, i)
            placed(j, 0)
            product(j, 1)

        done += steps

    placed(done - 1, 1)


def chi_kernel(bs, sends, tgt_ref, o_ref, v_ref, *refs):
    keep_ref, send_refs, refs = refs[0], refs[1:1 + sends], refs[1 + sends:]
    out0, out1, *accs = refs
    low_acc, high_acc = accs[0], accs[-1]
    tiles, aux, lanes = o_ref.shape[1:]
    half = aux // 2
    for ref in accs:
        ref[...] = jnp.zeros_like(ref)
    low = lax.broadcasted_iota(jnp.int32, (bs, lanes), 1) < bs
    shared = len(accs) == 1
    outs = (out0, out1)
    columns = [(0, WIDE)] + [(at, WIDE // 2) for at in range(WIDE, aux * bs, WIDE // 2)]

    def scatter(n):
        for a in range(aux):
            for t in range(columns[n][1] // lanes):
                value = outs[n % 2][t, pl.ds(a // half * (half * bs) + a % half, bs, stride=half), :]
                at = a * aux + 2 * (columns[n][0] // lanes + t)
                first, second = tgt_ref[at], tgt_ref[at + 1]
                low_acc[first] += jnp.where(low, value, 0.0) if shared else value
                high_acc[second] += jnp.where(low, 0.0, value) if shared else value

    for n, (at, wide) in enumerate(columns):
        if n:
            scatter(n - 1)
        got = lax.dot_general(
            flat(o_ref, slice(None), range(tiles)),
            flat(v_ref, slice(at // aux, (at + wide) // aux), range(tiles)),
            (((1,), (1,)), ((), ())),
            preferred_element_type=jnp.float32,
        )
        for t in range(wide // lanes):
            outs[n % 2][t] = got[:, t * lanes:(t + 1) * lanes]
    scatter(len(columns) - 1)

    pairs = keep_ref.shape[0]

    def joined(i):
        if shared:
            one, two = low_acc[2 * i], low_acc[2 * i + 1]
            return jnp.where(low, one, two) + pltpu.roll(jnp.where(low, two, one), bs, 1)
        left = jnp.where(low, low_acc[2 * i], high_acc[2 * i + 1])
        right = jnp.where(low, low_acc[2 * i + 1], high_acc[2 * i])
        return left + pltpu.roll(right, bs, 1)

    @pl.loop(0, pairs, unroll=4)
    def _(i):
        keep_ref[i] = joined(i)
        for k, send_ref in enumerate(send_refs):
            send_ref[i] = joined((k + 1) * pairs + i).astype(jnp.bfloat16)


def chi_blocks_of(ids, targets, tables, integrals, d_parts, blocks, sends):
    bs, aux, width = integrals.shape
    pairs = blocks // 2 // (sends + 1)
    side = jax.ShapeDtypeStruct((bs, bs // 2, aux, 2 * bs), jnp.bfloat16)
    cost = pl.CostEstimate(flops=2 * (aux * bs) ** 2 * width, bytes_accessed=4 * aux * bs * width, transcendentals=0)
    virt_side, occ_side = pl.pallas_call(
        functools.partial(sides_kernel, len(tables)),
        in_specs=in_smem(1) + in_vmem(len(tables) + len(PARTS)) + [pl.BlockSpec(memory_space=pl.ANY)],
        out_specs=in_vmem(2),
        out_shape=[side, side],
        scratch_shapes=[
            pltpu.VMEM(integrals.shape, integrals.dtype),
            pltpu.SemaphoreType.DMA((width // WIDE,)),
        ]
        + [pltpu.VMEM((bs * aux // 2, WIDE), jnp.float32)] * 2,
        compiler_params=pltpu.CompilerParams(vmem_limit_bytes=24 << 20),
        cost_estimate=cost,
    )(ids, *tables, *d_parts, integrals)
    accs = 2 if blocks <= 128 else 1
    acc = pltpu.VMEM((blocks, bs, 2 * bs), jnp.float32)
    out = pltpu.VMEM((WIDE // (2 * bs), aux * bs, 2 * bs), jnp.float32)
    return pl.pallas_call(
        functools.partial(chi_kernel, bs, sends),
        in_specs=in_smem(1) + in_vmem(2),
        out_specs=in_vmem(1 + sends),
        out_shape=[jax.ShapeDtypeStruct((pairs, bs, 2 * bs), jnp.float32)]
        + [jax.ShapeDtypeStruct((pairs, bs, 2 * bs), jnp.bfloat16)] * sends,
        scratch_shapes=[out, out] + [acc] * accs,
        compiler_params=pltpu.CompilerParams(vmem_limit_bytes=GRANT + 4 * (accs * blocks * bs * 2 * bs + 2 * aux * bs * WIDE)),
        cost_estimate=cost,
    )(targets, occ_side, virt_side)


def table_rounds(bits):
    rounds, at = [], 0
    while at < bits:
        step = 1 if at < 2 else min(2, bits - at)
        rounds.append((at, step))
        at += step
    return rounds[::-1]


def owner_rounds(bits):
    return [(0, 1)] + [(at, min(3, bits - at)) for at in range(1, bits, 3)]


def local(orb, three_centre, green_occ, green_virt, pair_atoms, basis_count, chi_target):
    bs = three_centre.shape[1]
    bits = orb.bit_length() - 1
    me = lax.axis_index("orb")

    def exchange(value, flip):
        return lax.ppermute(value, "orb", [(i, i ^ flip) for i in range(orb)])

    integrals = three_centre[0]
    table, ids, place = packed(
        me[None].astype(jnp.int32), basis_count, pair_atoms, chi_target, green_occ, green_virt, bs, bits
    )
    rounds = table_rounds(bits)
    tables, d_parts = [table], []
    for k, (shift, step) in enumerate(rounds):
        after = tables[-1:] if k else []
        table = tables[0] if len(tables) == 1 else jnp.concatenate(tables, axis=0)
        if k and len(d_parts) == k:
            table, d_parts[-1] = lax.optimization_barrier((table, d_parts[-1]))
        tables = [table] + [exchange(table, v << shift) for v in range(1, 1 << step)]
        parts = [i for i in range(len(PARTS)) if min(i, len(rounds) - 1) == k]
        d_parts += [relayout(integrals, i, after) for i in parts]
    total, *sends = chi_blocks_of(ids[0], place[0], tables, integrals, d_parts, orb * CB_DEV, 1)
    for k, (shift, step) in enumerate(owner_rounds(bits)):
        if k:
            rest = total.shape[0] >> step
            sends = [total[v * rest:(v + 1) * rest].astype(jnp.bfloat16) for v in range(1, 1 << step)]
            total = total[:rest]
        for v, send in enumerate(sends):
            total = total + exchange(send, (v + 1) << shift).astype(jnp.float32)
    total = total.reshape(CB_DEV // 2, bs, 2, bs).transpose(0, 2, 1, 3)
    return total.reshape(CB_DEV, bs * bs)


def solution(mesh):
    in_specs = (
        P("orb", None, None, None),
        P(("grp", "orb"), None),
        P(("grp", "orb"), None),
        P("orb", None),
        P("orb"),
        P("orb", None),
    )
    out_specs = P(("grp", "orb"), None)
    return jax.shard_map(
        functools.partial(local, mesh.shape["orb"]), mesh=mesh, in_specs=in_specs, out_specs=out_specs, check_vma=False
    )
```

```python
import functools

import jax
import jax.numpy as jnp
from jax import lax
from jax.experimental import pallas as pl
from jax.experimental.pallas import tpu as pltpu
from jax.sharding import PartitionSpec as P

CB_DEV = 4
LAM = 4
WIDE = 512
PARTS = (40, 16, 8)
GRANT = 3 << 20


def pack_kernel(place_rounds, slot_rounds, me_ref, count_ref, *refs):
    sources, (out_ref, ids_ref, place_ref), (rows_ref, *held, sems) = refs[:4], refs[4:7], refs[7:]
    copies = [pltpu.make_async_copy(src, dst, sems.at[k]) for k, (src, dst) in enumerate(zip(sources, held))]
    for copy in copies:
        copy.start()
    for copy in copies:
        copy.wait()
    pair_ref, tgt_ref, occ_ref, virt_ref = held
    lanes = out_ref.shape[2]
    half = out_ref.shape[1] // 2
    for i in range(half):
        rows_ref[i:i + 1, :] = occ_ref[:, i * lanes:(i + 1) * lanes].astype(jnp.float32)
        rows_ref[half + i:half + i + 1, :] = virt_ref[:, i * lanes:(i + 1) * lanes].astype(jnp.float32)
    bs = lanes // 2
    row = lax.broadcasted_iota(jnp.int32, rows_ref.shape, 0)
    lane = lax.broadcasted_iota(jnp.int32, rows_ref.shape, 1)
    count = count_ref[0]
    valid = (2 * (row % half) + lane // bs < count) & (lane % bs < count)
    out_ref[0] = jnp.where(valid, rows_ref[...], 0.0).astype(jnp.bfloat16)

    me = me_ref[0]
    rel = pair_ref[...] ^ me
    ids, weight = jnp.zeros_like(rel), 1
    for shift, step in slot_rounds:
        ids = ids + ((rel >> shift) & ((1 << step) - 1)) * weight
        weight <<= step
    ids_ref[...] = ids

    targets = tgt_ref[...]
    rel = (targets // CB_DEV) ^ me
    place = jnp.zeros_like(targets)
    for shift, step in place_rounds:
        place = (place << step) | ((rel >> shift) & ((1 << step) - 1))
    place_ref[...] = place * CB_DEV + targets % CB_DEV


def packed(me, basis_count, pair_atoms, chi_target, green_occ, green_virt, bs, bits):
    return pl.pallas_call(
        functools.partial(pack_kernel, owner_rounds(bits), table_rounds(bits)),
        in_specs=in_smem(2) + [pl.BlockSpec(memory_space=pl.ANY)] * 4,
        out_specs=in_vmem(3),
        out_shape=[
            jax.ShapeDtypeStruct((1, bs, 2 * bs), jnp.bfloat16),
            jax.ShapeDtypeStruct(pair_atoms.shape, jnp.int32),
            jax.ShapeDtypeStruct(chi_target.shape, jnp.int32),
        ],
        scratch_shapes=[pltpu.VMEM((bs, 2 * bs), jnp.float32)]
        + [pltpu.VMEM(x.shape, x.dtype) for x in (pair_atoms, chi_target, green_occ, green_virt)]
        + [pltpu.SemaphoreType.DMA((4,))],
        compiler_params=pltpu.CompilerParams(vmem_limit_bytes=60 << 20),
    )(me, basis_count, pair_atoms, chi_target, green_occ, green_virt)


def halves_joined(one, two, low, lanes):
    turned = pltpu.roll(jnp.where(low, two, one), lanes // 2, one.ndim - 1)
    return jnp.where(low, one, turned), jnp.where(low, turned, two)


def relayout_kernel(first, b_hbm, *refs):
    d_ref, b_ref, sems, *turns = refs[-5:]
    lams, aux, width = b_ref.shape
    lanes = d_ref.shape[3]
    tiles, half, bs = width // lanes, aux // 2, lanes // 2

    def copy(i):
        held = pl.ds(2 * i, 2)
        return pltpu.make_async_copy(b_hbm.at[pl.ds(first + 2 * i, 2)], b_ref.at[held], sems.at[i])

    for i in range(lams // 2):
        copy(i).start()
    low = lax.broadcasted_iota(jnp.int32, (aux, lanes), 1) < bs

    def turned(i, turn):
        for c in range(tiles):
            one, two = [b_ref[2 * i + k, :, c * lanes:(c + 1) * lanes].astype(jnp.float32) for k in range(2)]
            for k, joined in enumerate(halves_joined(one, two, low, lanes)):
                for h in range(2):
                    at = (h * bs + 2 * c + k) * half
                    turn[at:at + half, :] = joined[h * half:(h + 1) * half]
        for a in range(aux):
            rows = turn[pl.ds(a // half * (bs * half) + a % half, bs, stride=half), :].astype(jnp.bfloat16)
            d_ref[a * (bs // aux):(a + 1) * (bs // aux), i] = rows.reshape(bs // aux, aux, lanes)

    @pl.loop(0, lams // 4)
    def _(i):
        for k, turn in enumerate(turns):
            copy(2 * i + k).wait()
        for k, turn in enumerate(turns):
            turned(2 * i + k, turn)


def in_vmem(count):
    return [pl.BlockSpec(memory_space=pltpu.VMEM)] * count


def in_smem(count):
    return [pl.BlockSpec(memory_space=pltpu.SMEM)] * count


def relayout(integrals, part, after):
    bs, aux, width = integrals.shape
    lams = PARTS[part]
    hidden = pl.BlockSpec(memory_space=pl.ANY)
    return pl.pallas_call(
        functools.partial(relayout_kernel, sum(PARTS[:part])),
        in_specs=[hidden] * (1 + len(after)),
        out_specs=in_vmem(1)[0],
        out_shape=jax.ShapeDtypeStruct((bs, lams // 2, aux, 2 * bs), jnp.bfloat16),
        scratch_shapes=[
            pltpu.VMEM((lams, aux, width), integrals.dtype),
            pltpu.SemaphoreType.DMA((lams // 2,)),
        ]
        + [pltpu.VMEM((aux * bs, 2 * bs), jnp.float32)] * 2,
        compiler_params=pltpu.CompilerParams(vmem_limit_bytes=48 << 20),
        cost_estimate=pl.CostEstimate(
            flops=2 * lams * aux * width * 256,
            bytes_accessed=4 * lams * aux * width,
            transcendentals=0,
        ),
    )(integrals, *after)


def spread_rows(block, of_row, count, bs):
    shape = (count, bs // 2)
    pick = of_row(lax.broadcasted_iota(jnp.int32, shape, 0)) // 2 == lax.broadcasted_iota(jnp.int32, shape, 1)
    got = jnp.dot(pick.astype(jnp.bfloat16), block, preferred_element_type=jnp.float32)
    odd = of_row(lax.broadcasted_iota(jnp.int32, (count, bs), 0)) % 2 == 1
    return jnp.where(odd, got[:, bs:], got[:, :bs])


def green_block(tables, slot):
    count = tables[0].shape[0]
    block = tables[0][slot % count].astype(jnp.float32)
    for k in range(1, len(tables)):
        block = jnp.where(slot // count == k, tables[k][slot % count].astype(jnp.float32), block)
    return block.astype(jnp.bfloat16)


def flat(ref, blocks, tiles):
    got = [ref[blocks, t] for t in tiles]
    return jnp.concatenate([x.reshape(x.shape[0] * x.shape[1], x.shape[2]) for x in got], axis=1)


def sides_kernel(pieces, ids_ref, *refs):
    tables, refs = refs[:pieces], refs[pieces:]
    d_parts, refs = refs[:len(PARTS)], refs[len(PARTS):]
    b_hbm, v_ref, o_ref, b_ref, sems, *results = refs
    bs, aux, width = b_ref.shape
    half, lanes = aux // 2, 2 * bs
    tiles = width // lanes

    per = WIDE // lanes

    def columns(j):
        return slice(j * WIDE, (j + 1) * WIDE)

    def copy(j):
        return pltpu.make_async_copy(b_hbm.at[:, :, columns(j)], b_ref.at[:, :, columns(j)], sems.at[j])

    for j in range(tiles // per):
        copy(j).start()

    wide = LAM * bs
    spread = spread_rows(green_block(tables, ids_ref[1])[bs // 2:], lambda i: i % bs, wide, bs)
    spread = jnp.concatenate([spread] * LAM, axis=1)
    same = (
        lax.broadcasted_iota(jnp.int32, (wide, wide), 0) // bs == lax.broadcasted_iota(jnp.int32, (wide, wide), 1) // bs
    )
    virt_w = jnp.where(same, spread, 0.0).astype(jnp.bfloat16)

    def virt_product(part, before, step):
        held = [flat(d_parts[part], slice(None), [per * step + t, per * step + t + 1]) for t in range(0, per, 2)]
        got = jnp.dot(jnp.concatenate(held, axis=0), virt_w, preferred_element_type=jnp.float32).astype(jnp.bfloat16)
        count = held[0].shape[0]
        for t in range(per):
            side = got[t // 2 * count:(t // 2 + 1) * count, t % 2 * lanes:(t % 2 + 1) * lanes]
            v_ref[:, before + per * step + t] = side.reshape(v_ref.shape[:1] + (aux, lanes))

    tall = bs * half
    rep_t = (
        lax.broadcasted_iota(jnp.int32, (bs, tall), 1) // half == lax.broadcasted_iota(jnp.int32, (bs, tall), 0)
    ).astype(jnp.bfloat16)
    spread = spread_rows(green_block(tables, ids_ref[0])[:bs // 2], lambda i: i // half, tall, bs).astype(jnp.bfloat16)
    spread = jnp.dot(spread, rep_t, preferred_element_type=jnp.float32)
    same = (
        lax.broadcasted_iota(jnp.int32, (tall, tall), 0) % half
        == lax.broadcasted_iota(jnp.int32, (tall, tall), 1) % half
    )
    occ_w = jnp.where(same, spread, 0.0).astype(jnp.bfloat16)
    low = lax.broadcasted_iota(jnp.int32, (bs // 2, half, lanes), 2) < lanes // 2

    def product(j, h):
        block = b_ref[:, :, columns(j)].astype(jnp.float32)[:, h * half:(h + 1) * half]
        side = block.reshape(tall, WIDE).astype(jnp.bfloat16)
        results[h][...] = jnp.dot(occ_w, side, preferred_element_type=jnp.float32)

    def placed(j, h):
        for t in range(per):
            got = results[h][:, t * lanes:(t + 1) * lanes].reshape(bs // 2, 2, half, lanes)
            pair = halves_joined(got[:, 0], got[:, 1], low, lanes)
            o_ref[h * tiles + per * j + t] = jnp.concatenate(pair, axis=1).astype(jnp.bfloat16)

    j = 0
    for part, d_ref in enumerate(d_parts):
        before = j * per
        for i in range(d_ref.shape[1] // per):
            copy(j).wait()
            if j:
                placed(j - 1, 1)
            product(j, 0)
            virt_product(part, before, i)
            placed(j, 0)
            product(j, 1)
            j += 1
    placed(j - 1, 1)


def chi_kernel(bs, sends, tgt_ref, o_ref, v_ref, *refs):
    keep_ref, send_refs, refs = refs[0], refs[1:1 + sends], refs[1 + sends:]
    out0, out1, *accs = refs
    low_acc, high_acc = accs[0], accs[-1]
    tiles, aux, lanes = o_ref.shape[1:]
    half = aux // 2
    for ref in accs:
        ref[...] = jnp.zeros_like(ref)
    low = lax.broadcasted_iota(jnp.int32, (bs, lanes), 1) < bs
    shared = len(accs) == 1
    outs = (out0, out1)
    columns = [(0, WIDE)] + [(at, WIDE // 2) for at in range(WIDE, aux * bs, WIDE // 2)]

    def scatter(n):
        for a in range(aux):
            for t in range(columns[n][1] // lanes):
                value = outs[n % 2][t, pl.ds(a // half * (half * bs) + a % half, bs, stride=half), :]
                at = a * aux + 2 * (columns[n][0] // lanes + t)
                first, second = tgt_ref[at], tgt_ref[at + 1]
                low_acc[first] += jnp.where(low, value, 0.0) if shared else value
                high_acc[second] += jnp.where(low, 0.0, value) if shared else value

    for n, (at, wide) in enumerate(columns):
        if n:
            scatter(n - 1)
        got = lax.dot_general(
            flat(o_ref, slice(None), range(tiles)),
            flat(v_ref, slice(at // aux, (at + wide) // aux), range(tiles)),
            (((1,), (1,)), ((), ())),
            preferred_element_type=jnp.float32,
        )
        for t in range(wide // lanes):
            outs[n % 2][t] = got[:, t * lanes:(t + 1) * lanes]
    scatter(len(columns) - 1)

    pairs = keep_ref.shape[0]

    def joined(i):
        if shared:
            one, two = low_acc[2 * i], low_acc[2 * i + 1]
            return jnp.where(low, one, two) + pltpu.roll(jnp.where(low, two, one), bs, 1)
        left = jnp.where(low, low_acc[2 * i], high_acc[2 * i + 1])
        right = jnp.where(low, low_acc[2 * i + 1], high_acc[2 * i])
        return left + pltpu.roll(right, bs, 1)

    @pl.loop(0, pairs, unroll=4)
    def _(i):
        keep_ref[i] = joined(i)
        for k, send_ref in enumerate(send_refs):
            send_ref[i] = joined((k + 1) * pairs + i).astype(jnp.bfloat16)


def chi_blocks_of(ids, targets, tables, integrals, d_parts, blocks, sends):
    bs, aux, width = integrals.shape
    pairs = blocks // 2 // (sends + 1)
    side = jax.ShapeDtypeStruct((bs, bs // 2, aux, 2 * bs), jnp.bfloat16)
    cost = pl.CostEstimate(flops=2 * (aux * bs) ** 2 * width, bytes_accessed=4 * aux * bs * width, transcendentals=0)
    virt_side, occ_side = pl.pallas_call(
        functools.partial(sides_kernel, len(tables)),
        in_specs=in_smem(1) + in_vmem(len(tables) + len(PARTS)) + [pl.BlockSpec(memory_space=pl.ANY)],
        out_specs=in_vmem(2),
        out_shape=[side, side],
        scratch_shapes=[
            pltpu.VMEM(integrals.shape, integrals.dtype),
            pltpu.SemaphoreType.DMA((width // WIDE,)),
        ]
        + [pltpu.VMEM((bs * aux // 2, WIDE), jnp.float32)] * 2,
        compiler_params=pltpu.CompilerParams(vmem_limit_bytes=24 << 20),
        cost_estimate=cost,
    )(ids, *tables, *d_parts, integrals)
    accs = 2 if blocks <= 128 else 1
    acc = pltpu.VMEM((blocks, bs, 2 * bs), jnp.float32)
    out = pltpu.VMEM((WIDE // (2 * bs), aux * bs, 2 * bs), jnp.float32)
    return pl.pallas_call(
        functools.partial(chi_kernel, bs, sends),
        in_specs=in_smem(1) + in_vmem(2),
        out_specs=in_vmem(1 + sends),
        out_shape=[jax.ShapeDtypeStruct((pairs, bs, 2 * bs), jnp.float32)]
        + [jax.ShapeDtypeStruct((pairs, bs, 2 * bs), jnp.bfloat16)] * sends,
        scratch_shapes=[out, out] + [acc] * accs,
        compiler_params=pltpu.CompilerParams(vmem_limit_bytes=GRANT + 4 * (accs * blocks * bs * 2 * bs + 2 * aux * bs * WIDE)),
        cost_estimate=cost,
    )(targets, occ_side, virt_side)


def table_rounds(bits):
    rounds, at = [], 0
    while at < bits:
        step = 1 if at < 2 else min(2, bits - at)
        rounds.append((at, step))
        at += step
    return rounds[::-1]


def owner_rounds(bits):
    return table_rounds(bits)[::-1]


def local(orb, three_centre, green_occ, green_virt, pair_atoms, basis_count, chi_target):
    bs = three_centre.shape[1]
    bits = orb.bit_length() - 1
    me = lax.axis_index("orb")

    def exchange(value, flip):
        return lax.ppermute(value, "orb", [(i, i ^ flip) for i in range(orb)])

    integrals = three_centre[0]
    table, ids, place = packed(
        me[None].astype(jnp.int32), basis_count, pair_atoms, chi_target, green_occ, green_virt, bs, bits
    )
    rounds = table_rounds(bits)
    tables, d_parts = [table], []
    for k, (shift, step) in enumerate(rounds):
        after = tables[-1:] if k else []
        table = tables[0] if len(tables) == 1 else jnp.concatenate(tables, axis=0)
        if k and len(d_parts) == k:
            table, d_parts[-1] = lax.optimization_barrier((table, d_parts[-1]))
        tables = [table] + [exchange(table, v << shift) for v in range(1, 1 << step)]
        parts = [i for i in range(len(PARTS)) if min(i, len(rounds) - 1) == k]
        d_parts += [relayout(integrals, i, after) for i in parts]
    total, *sends = chi_blocks_of(ids[0], place[0], tables, integrals, d_parts, orb * CB_DEV, 1)
    for k, (shift, step) in enumerate(owner_rounds(bits)):
        if k:
            rest = total.shape[0] >> step
            sends = [total[v * rest:(v + 1) * rest].astype(jnp.bfloat16) for v in range(1, 1 << step)]
            total = total[:rest]
        for v, send in enumerate(sends):
            total = total + exchange(send, (v + 1) << shift).astype(jnp.float32)
    total = total.reshape(CB_DEV // 2, bs, 2, bs).transpose(0, 2, 1, 3)
    return total.reshape(CB_DEV, bs * bs)


def solution(mesh):
    in_specs = (
        P("orb", None, None, None),
        P(("grp", "orb"), None),
        P(("grp", "orb"), None),
        P("orb", None),
        P("orb"),
        P("orb", None),
    )
    out_specs = P(("grp", "orb"), None)
    return jax.shard_map(
        functools.partial(local, mesh.shape["orb"]), mesh=mesh, in_specs=in_specs, out_specs=out_specs, check_vma=False
    )
```

```python
import functools

import jax
import jax.numpy as jnp
from jax import lax
from jax.experimental import pallas as pl
from jax.experimental.pallas import tpu as pltpu
from jax.sharding import PartitionSpec as P

CB_DEV = 4
LAM = 4
WIDE = 512
PARTS = (40, 16, 8)
GRANT = 3 << 20


def pack_kernel(place_rounds, slot_rounds, me_ref, count_ref, *refs):
    sources, (out_ref, ids_ref, place_ref), (rows_ref, *held, sems) = refs[:4], refs[4:7], refs[7:]
    copies = [pltpu.make_async_copy(src, dst, sems.at[k]) for k, (src, dst) in enumerate(zip(sources, held))]
    for copy in copies:
        copy.start()
    for copy in copies:
        copy.wait()
    pair_ref, tgt_ref, occ_ref, virt_ref = held
    lanes = out_ref.shape[2]
    half = out_ref.shape[1] // 2
    for i in range(half):
        rows_ref[i:i + 1, :] = occ_ref[:, i * lanes:(i + 1) * lanes].astype(jnp.float32)
        rows_ref[half + i:half + i + 1, :] = virt_ref[:, i * lanes:(i + 1) * lanes].astype(jnp.float32)
    bs = lanes // 2
    row = lax.broadcasted_iota(jnp.int32, rows_ref.shape, 0)
    lane = lax.broadcasted_iota(jnp.int32, rows_ref.shape, 1)
    count = count_ref[0]
    valid = (2 * (row % half) + lane // bs < count) & (lane % bs < count)
    out_ref[0] = jnp.where(valid, rows_ref[...], 0.0).astype(jnp.bfloat16)

    me = me_ref[0]
    rel = pair_ref[...] ^ me
    ids, weight = jnp.zeros_like(rel), 1
    for shift, step in slot_rounds:
        ids = ids + ((rel >> shift) & ((1 << step) - 1)) * weight
        weight <<= step
    ids_ref[...] = ids

    targets = tgt_ref[...]
    rel = (targets // CB_DEV) ^ me
    place = jnp.zeros_like(targets)
    for shift, step in place_rounds:
        place = (place << step) | ((rel >> shift) & ((1 << step) - 1))
    place_ref[...] = place * CB_DEV + targets % CB_DEV


def packed(me, basis_count, pair_atoms, chi_target, green_occ, green_virt, bs, bits):
    return pl.pallas_call(
        functools.partial(pack_kernel, owner_rounds(bits), table_rounds(bits)),
        in_specs=in_smem(2) + [pl.BlockSpec(memory_space=pl.ANY)] * 4,
        out_specs=in_vmem(3),
        out_shape=[
            jax.ShapeDtypeStruct((1, bs, 2 * bs), jnp.bfloat16),
            jax.ShapeDtypeStruct(pair_atoms.shape, jnp.int32),
            jax.ShapeDtypeStruct(chi_target.shape, jnp.int32),
        ],
        scratch_shapes=[pltpu.VMEM((bs, 2 * bs), jnp.float32)]
        + [pltpu.VMEM(x.shape, x.dtype) for x in (pair_atoms, chi_target, green_occ, green_virt)]
        + [pltpu.SemaphoreType.DMA((4,))],
        compiler_params=pltpu.CompilerParams(vmem_limit_bytes=60 << 20),
    )(me, basis_count, pair_atoms, chi_target, green_occ, green_virt)


def halves_joined(one, two, low, lanes):
    turned = pltpu.roll(jnp.where(low, two, one), lanes // 2, one.ndim - 1)
    return jnp.where(low, one, turned), jnp.where(low, turned, two)


def relayout_kernel(first, b_hbm, *refs):
    d_ref, b_ref, sems, *turns = refs[-5:]
    lams, aux, width = b_ref.shape
    lanes = d_ref.shape[3]
    tiles, half, bs = width // lanes, aux // 2, lanes // 2

    def copy(i):
        held = pl.ds(2 * i, 2)
        return pltpu.make_async_copy(b_hbm.at[pl.ds(first + 2 * i, 2)], b_ref.at[held], sems.at[i])

    for i in range(lams // 2):
        copy(i).start()
    low = lax.broadcasted_iota(jnp.int32, (aux, lanes), 1) < bs

    def turned(i, turn):
        for c in range(tiles):
            one, two = [b_ref[2 * i + k, :, c * lanes:(c + 1) * lanes].astype(jnp.float32) for k in range(2)]
            for k, joined in enumerate(halves_joined(one, two, low, lanes)):
                for h in range(2):
                    at = (h * bs + 2 * c + k) * half
                    turn[at:at + half, :] = joined[h * half:(h + 1) * half]
        for a in range(aux):
            rows = turn[pl.ds(a // half * (bs * half) + a % half, bs, stride=half), :].astype(jnp.bfloat16)
            d_ref[a * (bs // aux):(a + 1) * (bs // aux), i] = rows.reshape(bs // aux, aux, lanes)

    @pl.loop(0, lams // 4)
    def _(i):
        for k, turn in enumerate(turns):
            copy(2 * i + k).wait()
        for k, turn in enumerate(turns):
            turned(2 * i + k, turn)


def in_vmem(count):
    return [pl.BlockSpec(memory_space=pltpu.VMEM)] * count


def in_smem(count):
    return [pl.BlockSpec(memory_space=pltpu.SMEM)] * count


def relayout(integrals, part, after):
    bs, aux, width = integrals.shape
    lams = PARTS[part]
    hidden = pl.BlockSpec(memory_space=pl.ANY)
    return pl.pallas_call(
        functools.partial(relayout_kernel, sum(PARTS[:part])),
        in_specs=[hidden] * (1 + len(after)),
        out_specs=in_vmem(1)[0],
        out_shape=jax.ShapeDtypeStruct((bs, lams // 2, aux, 2 * bs), jnp.bfloat16),
        scratch_shapes=[
            pltpu.VMEM((lams, aux, width), integrals.dtype),
            pltpu.SemaphoreType.DMA((lams // 2,)),
        ]
        + [pltpu.VMEM((aux * bs, 2 * bs), jnp.float32)] * 2,
        compiler_params=pltpu.CompilerParams(vmem_limit_bytes=48 << 20),
        cost_estimate=pl.CostEstimate(
            flops=2 * lams * aux * width * 256,
            bytes_accessed=4 * lams * aux * width,
            transcendentals=0,
        ),
    )(integrals, *after)


def spread_rows(block, of_row, count, bs):
    shape = (count, bs // 2)
    pick = of_row(lax.broadcasted_iota(jnp.int32, shape, 0)) // 2 == lax.broadcasted_iota(jnp.int32, shape, 1)
    got = jnp.dot(pick.astype(jnp.bfloat16), block, preferred_element_type=jnp.float32)
    odd = of_row(lax.broadcasted_iota(jnp.int32, (count, bs), 0)) % 2 == 1
    return jnp.where(odd, got[:, bs:], got[:, :bs])


def green_block(tables, slot):
    count = tables[0].shape[0]
    block = tables[0][slot % count].astype(jnp.float32)
    for k in range(1, len(tables)):
        block = jnp.where(slot // count == k, tables[k][slot % count].astype(jnp.float32), block)
    return block.astype(jnp.bfloat16)


def flat(ref, blocks, tiles):
    got = [ref[blocks, t] for t in tiles]
    return jnp.concatenate([x.reshape(x.shape[0] * x.shape[1], x.shape[2]) for x in got], axis=1)


def sides_kernel(pieces, ids_ref, *refs):
    tables, refs = refs[:pieces], refs[pieces:]
    d_parts, refs = refs[:len(PARTS)], refs[len(PARTS):]
    b_hbm, v_ref, o_ref, b_ref, sems, *results = refs
    bs, aux, width = b_ref.shape
    half, lanes = aux // 2, 2 * bs
    tiles = width // lanes

    per = WIDE // lanes

    def columns(j):
        return slice(j * WIDE, (j + 1) * WIDE)

    def copy(j):
        return pltpu.make_async_copy(b_hbm.at[:, :, columns(j)], b_ref.at[:, :, columns(j)], sems.at[j])

    for j in range(tiles // per):
        copy(j).start()

    wide = LAM * bs
    spread = spread_rows(green_block(tables, ids_ref[1])[bs // 2:], lambda i: i % bs, wide, bs)
    spread = jnp.concatenate([spread] * LAM, axis=1)
    same = (
        lax.broadcasted_iota(jnp.int32, (wide, wide), 0) // bs == lax.broadcasted_iota(jnp.int32, (wide, wide), 1) // bs
    )
    virt_w = jnp.where(same, spread, 0.0).astype(jnp.bfloat16)

    def virt_product(part, before, step):
        held = [flat(d_parts[part], slice(None), [per * step + t, per * step + t + 1]) for t in range(0, per, 2)]
        got = jnp.dot(jnp.concatenate(held, axis=0), virt_w, preferred_element_type=jnp.float32).astype(jnp.bfloat16)
        count = held[0].shape[0]
        for t in range(per):
            side = got[t // 2 * count:(t // 2 + 1) * count, t % 2 * lanes:(t % 2 + 1) * lanes]
            v_ref[:, before + per * step + t] = side.reshape(v_ref.shape[:1] + (aux, lanes))

    tall = bs * half
    rep_t = (
        lax.broadcasted_iota(jnp.int32, (bs, tall), 1) // half == lax.broadcasted_iota(jnp.int32, (bs, tall), 0)
    ).astype(jnp.bfloat16)
    spread = spread_rows(green_block(tables, ids_ref[0])[:bs // 2], lambda i: i // half, tall, bs).astype(jnp.bfloat16)
    spread = jnp.dot(spread, rep_t, preferred_element_type=jnp.float32)
    same = (
        lax.broadcasted_iota(jnp.int32, (tall, tall), 0) % half
        == lax.broadcasted_iota(jnp.int32, (tall, tall), 1) % half
    )
    occ_w = jnp.where(same, spread, 0.0).astype(jnp.bfloat16)
    low = lax.broadcasted_iota(jnp.int32, (bs // 2, half, lanes), 2) < lanes // 2

    def product(j, h):
        block = b_ref[:, :, columns(j)].astype(jnp.float32)[:, h * half:(h + 1) * half]
        side = block.reshape(tall, WIDE).astype(jnp.bfloat16)
        results[h][...] = jnp.dot(occ_w, side, preferred_element_type=jnp.float32)

    def placed(j, h):
        for t in range(per):
            got = results[h][:, t * lanes:(t + 1) * lanes].reshape(bs // 2, 2, half, lanes)
            pair = halves_joined(got[:, 0], got[:, 1], low, lanes)
            o_ref[h * tiles + per * j + t] = jnp.concatenate(pair, axis=1).astype(jnp.bfloat16)

    j = 0
    for part, d_ref in enumerate(d_parts):
        before = j * per
        for i in range(d_ref.shape[1] // per):
            copy(j).wait()
            if j:
                placed(j - 1, 1)
            product(j, 0)
            virt_product(part, before, i)
            placed(j, 0)
            product(j, 1)
            j += 1
    placed(j - 1, 1)


def chi_kernel(bs, sends, tgt_ref, o_ref, v_ref, *refs):
    keep_ref, send_refs, refs = refs[0], refs[1:1 + sends], refs[1 + sends:]
    out0, out1, *accs = refs
    low_acc, high_acc = accs[0], accs[-1]
    tiles, aux, lanes = o_ref.shape[1:]
    half = aux // 2
    for ref in accs:
        ref[...] = jnp.zeros_like(ref)
    low = lax.broadcasted_iota(jnp.int32, (bs, lanes), 1) < bs
    shared = len(accs) == 1
    outs = (out0, out1)
    columns = [(at, WIDE // 2) for at in range(0, aux * bs, WIDE // 2)]

    def scatter(n):
        for a in range(aux):
            for t in range(columns[n][1] // lanes):
                value = outs[n % 2][t, pl.ds(a // half * (half * bs) + a % half, bs, stride=half), :]
                at = a * aux + 2 * (columns[n][0] // lanes + t)
                first, second = tgt_ref[at], tgt_ref[at + 1]
                low_acc[first] += jnp.where(low, value, 0.0) if shared else value
                high_acc[second] += jnp.where(low, 0.0, value) if shared else value

    for n, (at, wide) in enumerate(columns):
        if n:
            scatter(n - 1)
        got = lax.dot_general(
            flat(o_ref, slice(None), range(tiles)),
            flat(v_ref, slice(at // aux, (at + wide) // aux), range(tiles)),
            (((1,), (1,)), ((), ())),
            preferred_element_type=jnp.float32,
        )
        for t in range(wide // lanes):
            outs[n % 2][t] = got[:, t * lanes:(t + 1) * lanes]
    scatter(len(columns) - 1)

    pairs = keep_ref.shape[0]

    def joined(i):
        if shared:
            one, two = low_acc[2 * i], low_acc[2 * i + 1]
            return jnp.where(low, one, two) + pltpu.roll(jnp.where(low, two, one), bs, 1)
        left = jnp.where(low, low_acc[2 * i], high_acc[2 * i + 1])
        right = jnp.where(low, low_acc[2 * i + 1], high_acc[2 * i])
        return left + pltpu.roll(right, bs, 1)

    @pl.loop(0, pairs, unroll=8)
    def _(i):
        keep_ref[i] = joined(i)
        for k, send_ref in enumerate(send_refs):
            send_ref[i] = joined((k + 1) * pairs + i).astype(jnp.bfloat16)


def chi_blocks_of(ids, targets, tables, integrals, d_parts, blocks, sends):
    bs, aux, width = integrals.shape
    pairs = blocks // 2 // (sends + 1)
    side = jax.ShapeDtypeStruct((bs, bs // 2, aux, 2 * bs), jnp.bfloat16)
    cost = pl.CostEstimate(flops=2 * (aux * bs) ** 2 * width, bytes_accessed=4 * aux * bs * width, transcendentals=0)
    virt_side, occ_side = pl.pallas_call(
        functools.partial(sides_kernel, len(tables)),
        in_specs=in_smem(1) + in_vmem(len(tables) + len(PARTS)) + [pl.BlockSpec(memory_space=pl.ANY)],
        out_specs=in_vmem(2),
        out_shape=[side, side],
        scratch_shapes=[
            pltpu.VMEM(integrals.shape, integrals.dtype),
            pltpu.SemaphoreType.DMA((width // WIDE,)),
        ]
        + [pltpu.VMEM((bs * aux // 2, WIDE), jnp.float32)] * 2,
        compiler_params=pltpu.CompilerParams(vmem_limit_bytes=24 << 20),
        cost_estimate=cost,
    )(ids, *tables, *d_parts, integrals)
    accs = 2 if blocks <= 128 else 1
    acc = pltpu.VMEM((blocks, bs, 2 * bs), jnp.float32)
    out = pltpu.VMEM((WIDE // (2 * bs), aux * bs, 2 * bs), jnp.float32)
    return pl.pallas_call(
        functools.partial(chi_kernel, bs, sends),
        in_specs=in_smem(1) + in_vmem(2),
        out_specs=in_vmem(1 + sends),
        out_shape=[jax.ShapeDtypeStruct((pairs, bs, 2 * bs), jnp.float32)]
        + [jax.ShapeDtypeStruct((pairs, bs, 2 * bs), jnp.bfloat16)] * sends,
        scratch_shapes=[out, out] + [acc] * accs,
        compiler_params=pltpu.CompilerParams(vmem_limit_bytes=GRANT + 4 * (accs * blocks * bs * 2 * bs + 2 * aux * bs * WIDE)),
        cost_estimate=cost,
    )(targets, occ_side, virt_side)


def table_rounds(bits):
    rounds, at = [], 0
    while at < bits:
        step = 1 if at < 2 else min(2, bits - at)
        rounds.append((at, step))
        at += step
    return rounds[::-1]


def owner_rounds(bits):
    return table_rounds(bits)[::-1]


def local(orb, three_centre, green_occ, green_virt, pair_atoms, basis_count, chi_target):
    bs = three_centre.shape[1]
    bits = orb.bit_length() - 1
    me = lax.axis_index("orb")

    def exchange(value, flip):
        return lax.ppermute(value, "orb", [(i, i ^ flip) for i in range(orb)])

    integrals = three_centre[0]
    table, ids, place = packed(
        me[None].astype(jnp.int32), basis_count, pair_atoms, chi_target, green_occ, green_virt, bs, bits
    )
    rounds = table_rounds(bits)
    tables, d_parts = [table], []
    for k, (shift, step) in enumerate(rounds):
        after = tables[-1:] if k else []
        table = tables[0] if len(tables) == 1 else jnp.concatenate(tables, axis=0)
        if k and len(d_parts) == k:
            table, d_parts[-1] = lax.optimization_barrier((table, d_parts[-1]))
        tables = [table] + [exchange(table, v << shift) for v in range(1, 1 << step)]
        parts = [i for i in range(len(PARTS)) if min(i, len(rounds) - 1) == k]
        d_parts += [relayout(integrals, i, after) for i in parts]
    total, *sends = chi_blocks_of(ids[0], place[0], tables, integrals, d_parts, orb * CB_DEV, 1)
    for k, (shift, step) in enumerate(owner_rounds(bits)):
        if k:
            rest = total.shape[0] >> step
            sends = [total[v * rest:(v + 1) * rest].astype(jnp.bfloat16) for v in range(1, 1 << step)]
            total = total[:rest]
        for v, send in enumerate(sends):
            total = total + exchange(send, (v + 1) << shift).astype(jnp.float32)
    total = total.reshape(CB_DEV // 2, bs, 2, bs).transpose(0, 2, 1, 3)
    return total.reshape(CB_DEV, bs * bs)


def solution(mesh):
    in_specs = (
        P("orb", None, None, None),
        P(("grp", "orb"), None),
        P(("grp", "orb"), None),
        P("orb", None),
        P("orb"),
        P("orb", None),
    )
    out_specs = P(("grp", "orb"), None)
    return jax.shard_map(
        functools.partial(local, mesh.shape["orb"]), mesh=mesh, in_specs=in_specs, out_specs=out_specs, check_vma=False
    )
```
